32 devices in a mesh: dp: 16 (over z, x, core), head: 2 (over y).
Axes of the slice: x: 2, y: 2, z: 4, core: 2. Of those that a mesh axis runs over, the one named last changes fastest.
Arguments:
- inputs: float32 [32, 1024, 1152], P('dp', 'head'), may hold values from -6 to 6
- cond: float32 [32, 1152], P(('dp', 'head')), may hold values from -6 to 6
- order: int32 [32], P('dp'), may hold values from 0 to 31, each once
- grid_kind: int32 [32], P('dp'), may hold values from 0 to 1
- weight_ada: float32 [1152, 6912], P('dp', 'head'), may hold values from -0.1875 to 0.1875
- bias_ada: float32 [6912], replicated, may hold values from -3 to 3
- weight_qkv: float32 [1152, 3456], P('dp', 'head'), may hold values from -0.1875 to 0.1875
- bias_query: float32 [1152], replicated, may hold values from -3 to 3
- bias_value: float32 [1152], replicated, may hold values from -2 to 2
- weight_out: float32 [1152, 1152], P('dp', 'head'), may hold values from -0.75 to 0.75
- bias_out: float32 [1152], replicated, may hold values from -2 to 2
- weight_up: float32 [1152, 4608], P('dp', 'head'), may hold values from -0.1875 to 0.1875
- bias_up: float32 [4608], replicated, may hold values from -3 to 3
- weight_down: float32 [4608, 1152], P('dp', 'head'), may hold values from -0.09375 to 0.09375
- bias_down: float32 [1152], replicated, may hold values from -2 to 2
- cotangent: float32 [32, 1024, 1152], P('dp', 'head'), may hold values from -6 to 6
Outputs:
- out_act: float32 [32, 1024, 1152], P('dp', 'head')
- input_grad: float32 [32, 1024, 1152], P('dp', 'head')
- cond_grad: float32 [32, 1152], P(('dp', 'head'))
- weight_ada_grad: float32 [1152, 6912], P('dp', 'head')
- weight_qkv_grad: float32 [1152, 3456], P('dp', 'head')
- weight_out_grad: float32 [1152, 1152], P('dp', 'head')
- weight_up_grad: float32 [1152, 4608], P('dp', 'head')
- weight_down_grad: float32 [4608, 1152], P('dp', 'head')
- bias_ada_grad: float32 [6912], replicated
- bias_query_grad: float32 [1152], replicated
- bias_value_grad: float32 [1152], replicated
- bias_out_grad: float32 [1152], replicated
- bias_up_grad: float32 [4608], replicated
- bias_down_grad: float32 [1152], replicated
The draws below stay inside these ranges and needn't reach their ends.
Inputs may be any that keep to these rules, and one draw needn't show every extreme that they name: order lists every initial image exactly once.
All inputs are finite; a program needn't handle non-finite values.
Results may differ from the reference program's by a relative error of at most 0.02.
The reference program's roundings to bfloat16 on the way count: a program that leaves them out, or rounds other values in their place, can miss the bound.
Values may be sent and summed in bfloat16 or wider, within the bound.
A program may use at most 320 MiB of HBM per device.

```python
import jax
import jax.numpy as jnp
from jax import lax

H = 16
HD = 72
D = 1152
FF = 4608
SLOTS = 1024
IMAGES = 32


def touch_ends(drawn, key, low, top_value):
    spot = [jax.random.randint(jax.random.fold_in(key, axis), (), 0, length) for axis, length in enumerate(drawn.shape)]
    main_axis = drawn.shape.index(max(drawn.shape))
    neighbour = spot[:main_axis] + [(spot[main_axis] + 1) % drawn.shape[main_axis]] + spot[main_axis + 1:]
    return drawn.at[tuple(spot)].set(low).at[tuple(neighbour)].set(top_value)


def block_levels(stream_key, shape, pieces, smallest, largest):
    def one(axis_at, shards_of):
        draws = jax.random.uniform(jax.random.fold_in(jax.random.fold_in(stream_key, 6), axis_at), (shards_of,), jnp.float32, smallest / len(pieces), largest / len(pieces))
        return jnp.repeat(jnp.exp(draws), shape[axis_at] // shards_of).reshape((-1,) + (1,) * (len(shape) - axis_at - 1))

    gain = one(*pieces[0])
    for cut in pieces[1:]:
        gain = gain * one(*cut)
    return gain


def bell_draw(stream_key, dims, width, most, shards=(), held_as=jnp.bfloat16):
    values = width * jax.random.normal(stream_key, dims, jnp.float32)
    if shards:
        values = values * block_levels(stream_key, dims, shards, -0.22, 0.18)
    return jnp.clip(values, -most, most).astype(held_as)


def setup_inputs(seed: int = 0) -> dict:
    keys = jax.random.split(jax.random.key(seed), 17)
    return {
        "inputs": bell_draw(keys[0], (IMAGES, SLOTS, D), 1.0, 6.0, ((0, 16), (1, 2)), jnp.float32),
        "cond": bell_draw(keys[1], (IMAGES, D), 1.0, 6.0, ((0, 32),), jnp.float32),
        "order": jax.random.permutation(keys[2], IMAGES).astype(jnp.int32),
        "grid_kind": touch_ends(jax.random.randint(keys[3], (IMAGES,), 0, 2), jax.random.fold_in(keys[3], 1), 0, 1).astype(jnp.int32),
        "weight_ada": bell_draw(keys[4], (D, 6 * D), D ** -0.5, 0.1875, ((0, 16), (1, 2)), jnp.float32),
        "bias_ada": bell_draw(keys[5], (6 * D,), 0.5, 3.0, (), jnp.float32),
        "weight_qkv": bell_draw(keys[6], (D, 3 * D), D ** -0.5, 0.1875, ((0, 16), (1, 2)), jnp.float32),
        "bias_query": bell_draw(keys[7], (D,), 0.5, 3.0, (), jnp.float32),
        "bias_value": bell_draw(keys[8], (D,), 0.3, 2.0, (), jnp.float32),
        "weight_out": bell_draw(keys[9], (D, D), HD ** -0.5, 0.75, ((0, 16), (1, 2)), jnp.float32),
        "bias_out": bell_draw(keys[10], (D,), 0.3, 2.0, (), jnp.float32),
        "weight_up": bell_draw(keys[11], (D, FF), D ** -0.5, 0.1875, ((0, 16), (1, 2)), jnp.float32),
        "bias_up": bell_draw(keys[12], (FF,), 0.5, 3.0, (), jnp.float32),
        "weight_down": bell_draw(keys[13], (FF, D), FF ** -0.5, 0.09375, ((0, 16), (1, 2)), jnp.float32),
        "bias_down": bell_draw(keys[14], (D,), 0.3, 2.0, (), jnp.float32),
        "cotangent": bell_draw(keys[15], (IMAGES, SLOTS, D), 1.0, 6.0, ((0, 16), (1, 2)), jnp.float32),
    }


@jax.custom_vjp
def low(v):
    return lax.optimization_barrier(v.astype(jnp.bfloat16)).astype(jnp.float32)

@jax.custom_vjp
def low_back(v):
    return v

def low_keep(v):
    return (low(v), None)

def low_pass(kept, grad):
    return (grad,)

def back_keep(v):
    return (v, None)

def back_low(kept, grad):
    return (low(grad),)
low.defvjp(low_keep, low_pass)
low_back.defvjp(back_keep, back_low)
norm_eps = 1e-06
mask_fill = -1000000000.0

def layer_norm(values):
    center = values - lax.optimization_barrier(jnp.mean(values, axis=-1, keepdims=True))
    spread = lax.optimization_barrier(jnp.mean(center * center, axis=-1, keepdims=True))
    return center * lax.rsqrt(spread + norm_eps)

def modulate(values, offset, factor):
    return layer_norm(values) * (1.0 + factor[:, None, :]) + offset[:, None, :]

def gelu_tanh(values):
    inner_arg = 0.7978845608028654 * (values + 0.044715 * values * values * values)
    return 0.5 * values * (1.0 + jnp.tanh(inner_arg))

def silu_act(values):
    return values * jax.nn.sigmoid(values)

def matmul_high(left, right):
    return jnp.matmul(left, right, precision=lax.Precision.HIGHEST)

def block_forward(block_values, cond_rows, counts, weight_ada, bias_ada, weight_qkv, bias_query, bias_value, weight_out, bias_out, weight_up, bias_up, weight_down, bias_down):
    images, slot_count, model_width = block_values.shape
    hidden_cond = low(silu_act(cond_rows))
    modulation = low_back(matmul_high(hidden_cond, low(weight_ada))) + bias_ada
    mod_parts = modulation.reshape(images, 6, model_width)
    normed = low(modulate(block_values, mod_parts[:, 0], mod_parts[:, 1]))
    bias_qkv = jnp.concatenate([bias_query, jnp.zeros_like(bias_query), bias_value])
    projected = low(low_back(matmul_high(normed, low(weight_qkv)) + bias_qkv))
    projected = projected.reshape(images, slot_count, 3, H, HD)
    queries = projected[:, :, 0]
    keys_all = projected[:, :, 1]
    values_all = projected[:, :, 2]
    scores = jnp.einsum('bshd,bthd->bhst', queries, keys_all, precision=lax.Precision.HIGHEST)
    scores = low_back(scores * HD ** (-0.5))
    valid_keys = jnp.arange(slot_count, dtype=jnp.int32)[None, :] < counts[:, None]
    scores = jnp.where(valid_keys[:, None, None, :], scores, mask_fill)
    row_peak = lax.optimization_barrier(jnp.max(scores, axis=-1, keepdims=True))
    exponent = jnp.exp(scores - row_peak)
    soft_weights = exponent / lax.optimization_barrier(jnp.sum(exponent, axis=-1, keepdims=True))
    attn_mix = jnp.einsum('bhst,bthd->bshd', low(soft_weights), values_all, precision=lax.Precision.HIGHEST)
    attended = low(low_back(attn_mix)).reshape(images, slot_count, model_width)
    branch = low_back(matmul_high(attended, low(weight_out))) + bias_out
    middle = block_values + mod_parts[:, 2][:, None, :] * branch
    second = low(modulate(middle, mod_parts[:, 3], mod_parts[:, 4]))
    hidden_pre = low_back(matmul_high(second, low(weight_up))) + bias_up
    activ = low(gelu_tanh(hidden_pre))
    mlp_out = low_back(matmul_high(activ, low(weight_down))) + bias_down
    return middle + mod_parts[:, 5][:, None, :] * mlp_out

def reference(inputs, cond, order, grid_kind, weight_ada, bias_ada, weight_qkv, bias_query, bias_value, weight_out, bias_out, weight_up, bias_up, weight_down, bias_down, cotangent):
    per_block = 4
    counts_all = jnp.where(grid_kind == 0, SLOTS, SLOTS - SLOTS // 16).astype(jnp.int32)
    params = (weight_ada, bias_ada, weight_qkv, bias_query, bias_value, weight_out, bias_out, weight_up, bias_up, weight_down, bias_down)

    def one_block(carry, block_index):
        grad_params, grad_cond = carry
        first_image = (block_index * per_block).astype(jnp.int32)
        block_values = lax.dynamic_slice_in_dim(inputs, first_image, per_block, 0)
        block_cot = lax.dynamic_slice_in_dim(cotangent, first_image, per_block, 0)
        image_rows = lax.dynamic_slice_in_dim(order, first_image, per_block, 0).astype(jnp.int32)
        block_counts = lax.dynamic_slice_in_dim(counts_all, first_image, per_block, 0)
        cond_rows = jnp.take(cond, image_rows, axis=0)

        def forward(values_in, cond_in, *weights):
            return block_forward(values_in, cond_in, block_counts, *weights)
        result, pullback = jax.vjp(forward, block_values, cond_rows, *params)
        gradients = pullback(block_cot)
        grad_params = tuple((summed + addend for summed, addend in zip(grad_params, gradients[2:])))
        grad_cond = grad_cond.at[image_rows].add(gradients[1])
        return ((grad_params, grad_cond), (result, gradients[0]))
    start_carry = (tuple((jnp.zeros_like(param) for param in params)), jnp.zeros_like(cond))
    (grad_params, grad_cond), (results, grad_inputs) = lax.scan(one_block, start_carry, jnp.arange(IMAGES // per_block, dtype=jnp.int32))
    out_act = results.reshape(IMAGES, SLOTS, D)
    input_grad = grad_inputs.reshape(IMAGES, SLOTS, D)
    return (out_act, input_grad, grad_cond, grad_params[0], grad_params[2], grad_params[5], grad_params[7], grad_params[9], grad_params[1], grad_params[3], grad_params[4], grad_params[6], grad_params[8], grad_params[10])
```

```python
import functools
import math

import jax
import jax.numpy as jnp
from jax import lax
from jax.experimental import pallas as pl
from jax.experimental.pallas import tpu as pltpu
from jax.sharding import PartitionSpec as P

H = 16
norm_eps = 1e-06
log2_e = 1.4426950408889634
gelu_in = 0.7978845608028654
gelu_cube = 0.044715
f32 = jnp.float32
bf16 = jnp.bfloat16
VMEM_MOST = 60 * 1024 * 1024


def mm(left, right):
    return jnp.dot(left, right, preferred_element_type=f32)


def mm_nt(left, right):
    return lax.dot_general(left, right, (((1,), (1,)), ((), ())), preferred_element_type=f32)


def center_spread(values):
    center = values - jnp.mean(values, axis=-1, keepdims=True)
    spread = jnp.mean(center * center, axis=-1, keepdims=True)
    return center, lax.rsqrt(spread + norm_eps)


def norm_back(grad, unit, inv):
    return inv * (
        grad
        - jnp.mean(grad, axis=-1, keepdims=True)
        - unit * jnp.mean(grad * unit, axis=-1, keepdims=True)
    )


def whole_spec(shape):
    zeros = (0,) * len(shape)
    return pl.BlockSpec(shape, lambda *_: zeros)


def once_spec(shape):
    zeros = (0,) * len(shape)
    return pl.BlockSpec(shape, lambda *_: zeros, pipeline_mode=pl.Buffered(1))


def params(most=VMEM_MOST):
    return pltpu.CompilerParams(vmem_limit_bytes=most)


def place(quarter):
    return (quarter % 2) * 2 + quarter // 2


def qkv_kernel(tm, x_ref, mod_ref, w_ref, b_ref, qkv_ref, norm_ref):
    part = pl.program_id(0)
    rows = pl.ds(pl.multiple_of(pl.program_id(1) * tm, tm), tm)

    @pl.when(part == 0)
    def _():
        center, inv = center_spread(x_ref[...].astype(f32))
        norm_ref[rows, :] = (center * inv * (1.0 + mod_ref[1:2, :]) + mod_ref[0:1, :]).astype(bf16)

    groups, _, rows_each, width = w_ref.shape
    weight = w_ref[...].reshape(groups * rows_each, width)
    out = (mm(norm_ref[rows, :], weight) + b_ref[0]).astype(bf16)
    size = qkv_ref.shape[2]
    for j in range(qkv_ref.shape[0]):
        qkv_ref[j] = out[:, j * size : (j + 1) * size]


def qkv_call(x, mod, weight, bias):
    slots, width = x.shape
    tm = min(256, slots)
    groups, parts, rows_each, part_width = weight.shape
    size = width // H
    heads = part_width // size
    return pl.pallas_call(
        functools.partial(qkv_kernel, tm),
        grid=(parts, slots // tm),
        in_specs=[
            pl.BlockSpec((tm, width), lambda p, i: (i, 0)),
            whole_spec(mod.shape),
            pl.BlockSpec((groups, 1, rows_each, part_width), lambda p, i: (0, place(p), 0, 0)),
            pl.BlockSpec((1, 1, part_width), lambda p, i: (p, 0, 0)),
        ],
        out_specs=[
            pl.BlockSpec((heads, tm, size), lambda p, i: (p, i, 0)),
            whole_spec((slots, width)),
        ],
        out_shape=[
            jax.ShapeDtypeStruct((3 * H, slots, size), bf16),
            jax.ShapeDtypeStruct((slots, width), bf16),
        ],
        compiler_params=params(),
        name="qkv_forward",
    )(x, mod, weight, bias)


def masked(scores, full, kept):
    return jnp.concatenate(
        [scores[:kept], jnp.where(full, scores[kept:], -1e30)], axis=0
    )


def attn_kernel(ts, kind_ref, q_ref, k_ref, v_ref, o_ref, lse_ref):
    slots, size = q_ref.shape[1:]
    kept = slots - slots // 16
    factor = log2_e * size ** (-0.5)
    full = kind_ref[0] == 0
    keys = k_ref[0]
    values_t = v_ref[0].T
    for start in range(0, slots, ts):
        here = slice(start, start + ts)
        scores = masked(mm_nt(keys, q_ref[0, here, :]), full, kept)
        peak = jnp.max(scores, axis=0, keepdims=True) * factor
        exponent = jnp.exp2(scores * factor - peak)
        total = jnp.sum(exponent, axis=0, keepdims=True)
        mix = mm(values_t, exponent.astype(bf16)) * (1.0 / total)
        o_ref[0, here, :] = mix.T.astype(bf16)
        lse_ref[0, :, here] = peak + jnp.log2(total)


def attn_call(kind, qkv):
    _, slots, size = qkv.shape
    ts = min(256, slots)
    block = (1, slots, size)
    return pl.pallas_call(
        functools.partial(attn_kernel, ts),
        grid=(H,),
        in_specs=[
            pl.BlockSpec(memory_space=pltpu.SMEM),
            pl.BlockSpec(block, lambda h: (h, 0, 0)),
            pl.BlockSpec(block, lambda h: (h + H, 0, 0)),
            pl.BlockSpec(block, lambda h: (h + 2 * H, 0, 0)),
        ],
        out_specs=[
            pl.BlockSpec(block, lambda h: (h, 0, 0)),
            pl.BlockSpec((1, 1, slots), lambda h: (h, 0, 0)),
        ],
        out_shape=[
            jax.ShapeDtypeStruct((H, slots, size), bf16),
            jax.ShapeDtypeStruct((H, 1, slots), f32),
        ],
        compiler_params=params(),
        name="attention_forward",
    )(kind, qkv, qkv, qkv)


def attn_back_kernel(ts, kind_ref, q_ref, k_ref, v_ref, g_ref, lse_ref, out_ref, dk_s, dv_s):
    slots, size = q_ref.shape[1:]
    kept = slots - slots // 16
    scale = size ** (-0.5)
    factor = log2_e * scale
    full = kind_ref[0] == 0
    keys = k_ref[0]
    keys_t = keys.T
    values = v_ref[0]
    for start in range(0, slots, ts):
        here = slice(start, start + ts)
        queries = q_ref[0, here, :]
        grad = g_ref[0, here, :]
        scores = masked(mm_nt(keys, queries), full, kept)
        probs = jnp.exp2(scores * factor - lse_ref[0, :, here])
        grad_probs = mm_nt(values, grad)
        weighted = probs * grad_probs
        inner = jnp.sum(weighted, axis=0, keepdims=True)
        grad_scores = (weighted - probs * inner).astype(bf16)
        add_v = mm(probs.astype(bf16), grad)
        add_k = mm(grad_scores, queries)
        if start == 0:
            dv_s[...] = add_v
            dk_s[...] = add_k
        else:
            dv_s[...] += add_v
            dk_s[...] += add_k
        out_ref[0, 0, here, :] = (mm(keys_t, grad_scores) * scale).T.astype(bf16)
    out_ref[1, 0] = (dk_s[...] * scale).astype(bf16)
    out_ref[2, 0] = dv_s[...].astype(bf16)


def attn_back_call(kind, qkv, grad, lse):
    _, slots, size = qkv.shape
    ts = min(256, slots)
    block = (1, slots, size)
    return pl.pallas_call(
        functools.partial(attn_back_kernel, ts),
        grid=(H,),
        in_specs=[
            pl.BlockSpec(memory_space=pltpu.SMEM),
            pl.BlockSpec(block, lambda h: (h, 0, 0)),
            pl.BlockSpec(block, lambda h: (h + H, 0, 0)),
            pl.BlockSpec(block, lambda h: (h + 2 * H, 0, 0)),
            pl.BlockSpec(block, lambda h: (h, 0, 0)),
            pl.BlockSpec((1, 1, slots), lambda h: (h, 0, 0)),
        ],
        out_specs=pl.BlockSpec((3, 1, slots, size), lambda h: (0, h, 0, 0)),
        out_shape=jax.ShapeDtypeStruct((3, H, slots, size), bf16),
        scratch_shapes=[pltpu.VMEM((slots, size), f32), pltpu.VMEM((slots, size), f32)],
        compiler_params=params(),
        name="attention_backward",
    )(kind, qkv, qkv, qkv, grad, lse)


def columns_of(w_ref):
    groups, parts, rows_each, width = w_ref.shape
    return jnp.concatenate(
        [w_ref[:, place(n)].reshape(groups * rows_each, width) for n in range(parts)], axis=1
    )


def out_kernel(o_ref, x_ref, mod_ref, w_ref, b_ref, att_ref, branch_ref, second_ref, w_s):
    @pl.when(pl.program_id(0) == 0)
    def _():
        w_s[...] = columns_of(w_ref)

    attended = jnp.concatenate([o_ref[j] for j in range(o_ref.shape[0])], axis=1)
    att_ref[...] = attended
    branch = mm(attended, w_s[...]) + b_ref[...]
    branch_ref[...] = branch.astype(bf16)
    middle = x_ref[...].astype(f32) + mod_ref[2:3, :] * branch
    center, inv = center_spread(middle)
    second_ref[...] = (center * inv * (1.0 + mod_ref[4:5, :]) + mod_ref[3:4, :]).astype(bf16)


def out_call(mix, x, mod, weight, bias):
    slots, width = x.shape
    tm = min(256, slots)
    size = width // H
    tile = pl.BlockSpec((tm, width), lambda i: (i, 0))
    return pl.pallas_call(
        out_kernel,
        grid=(slots // tm,),
        in_specs=[
            pl.BlockSpec((H, tm, size), lambda i: (0, i, 0)),
            tile,
            whole_spec(mod.shape),
            whole_spec(weight.shape),
            whole_spec((1, width)),
        ],
        out_specs=[tile, tile, tile],
        out_shape=[jax.ShapeDtypeStruct((slots, width), bf16)] * 3,
        scratch_shapes=[pltpu.VMEM((width, width), bf16)],
        compiler_params=params(),
        name="out_projection",
    )(mix, x, mod, weight, bias.reshape(1, width))


def mlp_kernel(
    tm, second_ref, cot_ref, mod_ref, up_ref, down_ref, b_ref,
    mlp_ref, gsec_ref, dup_ref, ddown_ref, bias_ref,
    gm_s, sec_t, act_t, gh_s, down_s,
):
    part = pl.program_id(0)
    slots, width = second_ref.shape
    tiles = slots // tm

    @pl.when(part == 0)
    def _():
        sec_t[...] = second_ref[...].T
        gm_s[...] = (cot_ref[...].astype(f32) * mod_ref[5:6, :]).astype(bf16)
        mlp_ref[...] = jnp.zeros_like(mlp_ref)
        gsec_ref[...] = jnp.zeros_like(gsec_ref)

    groups, _, rows_each, hidden = up_ref.shape
    chunks, halves, chunk, half = down_ref.shape
    for j in range(chunks):
        down_s[j * chunk : (j + 1) * chunk, :] = jnp.concatenate(
            [down_ref[j, s] for s in range(halves)], axis=1
        )
    bias_ref[...] = jnp.zeros_like(bias_ref)

    def tile(i, carry):
        rows = pl.ds(pl.multiple_of(i * tm, tm), tm)
        up = up_ref[...].reshape(width, hidden)
        pre = mm(second_ref[rows, :], up) + b_ref[0]
        square = pre * pre
        tanh = jnp.tanh(gelu_in * (pre + gelu_cube * pre * square))
        act = (0.5 * pre * (1.0 + tanh)).astype(bf16)
        slope = 0.5 * (1.0 + tanh) + 0.5 * pre * (1.0 - tanh * tanh) * (
            gelu_in * (1.0 + 3.0 * gelu_cube * square)
        )
        grad = mm_nt(gm_s[rows, :], down_s[...]) * slope
        bias_ref[0] += jnp.sum(grad, axis=0, keepdims=True)
        grad_low = grad.astype(bf16)
        gh_s[rows, :] = grad_low
        act_t[:, rows] = act.T
        mlp_ref[rows, :] += mm(act, down_s[...])
        gsec_ref[rows, :] += mm_nt(grad_low, up)
        return carry

    lax.fori_loop(0, tiles, tile, 0)
    per = groups // 2
    for j in range(2):
        dup_ref[per * j : per * (j + 1), 0] = (
            mm(sec_t[per * j * rows_each : per * (j + 1) * rows_each, :], gh_s[...])
            .astype(bf16)
            .reshape(per, rows_each, hidden)
        )
    per = chunks // 2
    for j in range(2):
        grad = mm(act_t[per * j * chunk : per * (j + 1) * chunk, :], gm_s[...]).astype(bf16)
        for r in range(per):
            for s in range(halves):
                ddown_ref[per * j + r, s] = grad[
                    r * chunk : (r + 1) * chunk, s * half : (s + 1) * half
                ]


def mlp_call(second, cot, mod, up, down, bias):
    slots, width = second.shape
    tm = min(256, slots)
    groups, parts, rows_each, hidden = up.shape
    chunks, halves, chunk, half = down.shape
    per = chunks // parts
    up_spec = pl.BlockSpec((groups, 1, rows_each, hidden), lambda p: (0, place(p), 0, 0))
    down_spec = pl.BlockSpec((per, halves, chunk, half), lambda p: (p, 0, 0, 0))
    return pl.pallas_call(
        functools.partial(mlp_kernel, tm),
        grid=(parts,),
        in_specs=[
            once_spec((slots, width)),
            once_spec((slots, width)),
            whole_spec(mod.shape),
            up_spec,
            down_spec,
            pl.BlockSpec((1, 1, hidden), lambda p: (p, 0, 0)),
        ],
        out_specs=[
            once_spec((slots, width)),
            once_spec((slots, width)),
            up_spec,
            down_spec,
            pl.BlockSpec((1, 1, hidden), lambda p: (p, 0, 0)),
        ],
        out_shape=[
            jax.ShapeDtypeStruct((slots, width), f32),
            jax.ShapeDtypeStruct((slots, width), f32),
            jax.ShapeDtypeStruct(up.shape, bf16),
            jax.ShapeDtypeStruct(down.shape, bf16),
            jax.ShapeDtypeStruct((parts, 1, hidden), f32),
        ],
        scratch_shapes=[
            pltpu.VMEM((slots, width), bf16),
            pltpu.VMEM((width, slots), bf16),
            pltpu.VMEM((hidden, slots), bf16),
            pltpu.VMEM((slots, hidden), bf16),
            pltpu.VMEM((hidden, width), bf16),
        ],
        compiler_params=params(),
        name="feed_forward_both_ways",
    )(second, cot, mod, up, down, bias)


def mid_back_kernel(
    x_ref, branch_ref, mlp_ref, gsec_ref, cot_ref, att_ref, mod_ref, w_ref, b_ref,
    act_ref, gmid_ref, gatt_ref, dw_ref, sums_ref, w_s, dw_s,
):
    step = pl.program_id(0)

    @pl.when(step == 0)
    def _():
        w_s[...] = columns_of(w_ref)
        sums_ref[...] = jnp.zeros_like(sums_ref)
        dw_s[...] = jnp.zeros_like(dw_s)

    gate_a = mod_ref[2:3, :]
    gate_m = mod_ref[5:6, :]
    branch = branch_ref[...].astype(f32)
    middle = x_ref[...].astype(f32) + gate_a * branch
    mlp = mlp_ref[...] + b_ref[...]
    cot = cot_ref[...].astype(f32)
    act_ref[...] = (middle + gate_m * mlp).astype(act_ref.dtype)
    center, inv = center_spread(middle)
    unit = center * inv
    grad = gsec_ref[...]
    grad_mid = cot + norm_back(grad * (1.0 + mod_ref[4:5, :]), unit, inv)
    gmid_ref[...] = grad_mid
    grad_branch = gate_a * grad_mid

    def add(row, value):
        sums_ref[row : row + 1, :] += jnp.sum(value, axis=0, keepdims=True)

    add(0, grad_mid * branch)
    add(1, grad)
    add(2, grad * unit)
    add(3, cot * mlp)
    add(4, grad_branch)
    add(5, gate_m * cot)
    grad_low = grad_branch.astype(bf16)
    grad_att = mm_nt(grad_low, w_s[...]).astype(bf16)
    size = gatt_ref.shape[2]
    for j in range(gatt_ref.shape[0]):
        gatt_ref[j] = grad_att[:, j * size : (j + 1) * size]
    dw_s[...] += mm(att_ref[...].T, grad_low)

    @pl.when(step == pl.num_programs(0) - 1)
    def _():
        groups, parts, rows_each, width = dw_ref.shape
        low = dw_s[...].astype(bf16)
        for n in range(parts):
            dw_ref[:, place(n)] = low[:, n * width : (n + 1) * width].reshape(
                groups, rows_each, width
            )


def mid_back_call(x, branch, mlp, gsec, cot, attended, mod, weight, bias_down):
    slots, width = x.shape
    tm = min(256, slots)
    size = width // H
    tile = pl.BlockSpec((tm, width), lambda i: (i, 0))
    return pl.pallas_call(
        mid_back_kernel,
        grid=(slots // tm,),
        in_specs=[tile] * 6 + [whole_spec(mod.shape), whole_spec(weight.shape), whole_spec((1, width))],
        out_specs=[
            tile,
            tile,
            pl.BlockSpec((H, tm, size), lambda i: (0, i, 0)),
            whole_spec(weight.shape),
            whole_spec((8, width)),
        ],
        out_shape=[
            jax.ShapeDtypeStruct((slots, width), bf16),
            jax.ShapeDtypeStruct((slots, width), f32),
            jax.ShapeDtypeStruct((H, slots, size), bf16),
            jax.ShapeDtypeStruct(weight.shape, bf16),
            jax.ShapeDtypeStruct((8, width), f32),
        ],
        scratch_shapes=[pltpu.VMEM((width, width), bf16), pltpu.VMEM((width, width), f32)],
        compiler_params=params(),
        name="middle_backward",
    )(x, branch, mlp, gsec, cot, attended, mod, weight, bias_down.reshape(1, width))


def qkv_back_kernel(tm, g_ref, norm_ref, w_ref, x_ref, gmid_ref, mod_ref, gin_ref, dw_ref, bias_ref, sums_ref, norm_t, gp_s, gn_s):
    part = pl.program_id(0)
    slots, width = x_ref.shape
    tiles = slots // tm
    groups, _, rows_each, part_width = w_ref.shape
    heads = g_ref.shape[0]

    @pl.when(part == 0)
    def _():
        norm_t[...] = norm_ref[...].T
        gn_s[...] = jnp.zeros_like(gn_s)

    def tile(i, total):
        rows = pl.ds(pl.multiple_of(i * tm, tm), tm)
        grad = jnp.concatenate([g_ref[j, rows, :] for j in range(heads)], axis=1)
        gp_s[rows, :] = grad
        gn_s[rows, :] += mm_nt(grad, w_ref[...].reshape(width, part_width))
        return total + jnp.sum(grad.astype(f32), axis=0, keepdims=True)

    bias_ref[0] = lax.fori_loop(0, tiles, tile, jnp.zeros((1, part_width), f32))
    per = groups // 2
    for j in range(2):
        dw_ref[per * j : per * (j + 1), 0] = (
            mm(norm_t[per * j * rows_each : per * (j + 1) * rows_each, :], gp_s[...])
            .astype(bf16)
            .reshape(per, rows_each, part_width)
        )

    @pl.when(part == pl.num_programs(0) - 1)
    def _():
        def finish(i, sums):
            rows = pl.ds(pl.multiple_of(i * tm, tm), tm)
            center, inv = center_spread(x_ref[rows, :].astype(f32))
            unit = center * inv
            grad = gn_s[rows, :]
            gin_ref[rows, :] = (
                gmid_ref[rows, :] + norm_back(grad * (1.0 + mod_ref[1:2, :]), unit, inv)
            ).astype(gin_ref.dtype)
            return (
                sums[0] + jnp.sum(grad, axis=0, keepdims=True),
                sums[1] + jnp.sum(grad * unit, axis=0, keepdims=True),
            )

        zero = jnp.zeros((1, width), f32)
        shift, scale = lax.fori_loop(0, tiles, finish, (zero, zero))
        sums_ref[...] = jnp.zeros_like(sums_ref)
        sums_ref[0:1, :] = shift
        sums_ref[1:2, :] = scale


def qkv_back_call(grad, norm, weight, x, gmid, mod):
    slots, width = x.shape
    tm = min(256, slots)
    size = width // H
    groups, parts, rows_each, part_width = weight.shape
    heads = part_width // size
    w_spec = pl.BlockSpec((groups, 1, rows_each, part_width), lambda p: (0, place(p), 0, 0))
    return pl.pallas_call(
        functools.partial(qkv_back_kernel, tm),
        grid=(parts,),
        in_specs=[
            pl.BlockSpec((heads, slots, size), lambda p: (p, 0, 0)),
            once_spec((slots, width)),
            w_spec,
            once_spec((slots, width)),
            once_spec((slots, width)),
            whole_spec(mod.shape),
        ],
        out_specs=[
            once_spec((slots, width)),
            w_spec,
            pl.BlockSpec((1, 1, part_width), lambda p: (p, 0, 0)),
            whole_spec((8, width)),
        ],
        out_shape=[
            jax.ShapeDtypeStruct((slots, width), bf16),
            jax.ShapeDtypeStruct(weight.shape, bf16),
            jax.ShapeDtypeStruct((parts, 1, part_width), f32),
            jax.ShapeDtypeStruct((8, width), f32),
        ],
        scratch_shapes=[
            pltpu.VMEM((width, slots), bf16),
            pltpu.VMEM((slots, part_width), bf16),
            pltpu.VMEM((slots, width), f32),
        ],
        compiler_params=params(),
        name="qkv_backward",
    )(grad, norm, weight, x, gmid, mod)


MESH = pl.DeviceIdType.MESH


class Place:
    def __init__(self):
        self.dp = lax.axis_size("dp")
        head = lax.axis_size("head")
        near = self.dp // 8
        at = lax.axis_index("dp")
        self.size = {"z": 4, "x": 2, "c": near, "y": head}
        self.at = {
            "z": lax.div(at, 2 * near),
            "x": lax.rem(lax.div(at, near), 2),
            "c": lax.rem(at, near),
            "y": lax.axis_index("head"),
        }
        self.count = self.dp * head
        self.me = at * head + self.at["y"]

    def device(self, axis, index):
        spot = dict(self.at)
        spot[axis] = index
        return ((spot["z"] * 2 + spot["x"]) * self.size["c"] + spot["c"], spot["y"])

    def numbered(self, index):
        head = self.size["y"]
        return (lax.div(index, head), lax.rem(index, head))

    def after(self, axis, step):
        return lax.rem(self.at[axis] + step, self.size[axis])

    def before(self, axis, step):
        return lax.rem(self.at[axis] + self.size[axis] - step, self.size[axis])


class Sems:
    def __init__(self, send, recv):
        self.send, self.recv, self.used = send, recv, 0
        self.sent = []

    def copy(self, src, dst, device):
        at = self.used
        self.used += 1
        made = pltpu.make_async_remote_copy(
            src_ref=src, dst_ref=dst, send_sem=self.send.at[at], recv_sem=self.recv.at[at],
            device_id=device, device_id_type=MESH,
        )
        made.start()
        self.sent.append(made)
        return at

    def arrived(self, at, dst, device):
        pltpu.make_async_remote_copy(
            src_ref=dst, dst_ref=dst, send_sem=self.send.at[at], recv_sem=self.recv.at[at],
            device_id=device, device_id_type=MESH,
        ).wait_recv()

    def local(self, src, dst):
        at = self.used
        self.used += 1
        made = pltpu.make_async_copy(src, dst, self.send.at[at])
        made.start()
        return made

    def drain(self):
        for made in self.sent:
            made.wait_send()


AXES = "zxcy"


class Gather:
    def __init__(self, place, sems, piece, full, axes, rows=None):
        self.place, self.sems, self.piece, self.full, self.axes = place, sems, piece, full, axes
        self.rows = rows
        self.slots = {}

    def part(self, got, axis=None, index=None):
        spot = dict(self.place.at)
        if axis is not None:
            spot[axis] = index
        spots = tuple(slice(None) if name in got else spot[name] for name in AXES)
        if self.rows is not None:
            spots = spots + (pl.ds(*self.rows), slice(None))
        return self.full.at[spots]

    def first(self):
        return self.piece if self.rows is None else self.piece.at[pl.ds(*self.rows)]

    def own(self):
        self.kept = self.sems.local(self.first(), self.part(""))

    def start(self, stage):
        axis = self.axes[stage]
        got = self.axes[:stage]
        if stage == 1:
            self.kept.wait()
        src = self.first() if stage == 0 else self.part(got)
        for step in range(1, self.place.size[axis]):
            self.slots[stage, step] = self.sems.copy(
                src, self.part(got), self.place.device(axis, self.place.after(axis, step))
            )

    def wait(self, stage):
        axis = self.axes[stage]
        got = self.axes[:stage]
        for step in range(1, self.place.size[axis]):
            index = self.place.before(axis, step)
            self.sems.arrived(
                self.slots[stage, step], self.part(got, axis, index), self.place.device(axis, index)
            )


def greet(place):
    barrier = pltpu.get_barrier_semaphore()

    def one(step, carry):
        pl.semaphore_signal(
            barrier, inc=1, device_id=place.numbered(lax.rem(place.me + step, place.count)),
            device_id_type=MESH,
        )
        return carry

    lax.fori_loop(1, place.count, one, 0)
    pl.semaphore_wait(barrier, place.count - 1)


def sems_needed(sizes, units, pairs):
    return units * (1 + sum(size - 1 for size in sizes.values())) + pairs


def exchange(place, sems, mine, whole):
    sent = []
    for step in range(1, place.size["y"]):
        other = place.after("y", step)
        sent.append(
            (step, sems.copy(mine.at[other], whole.at[place.at["y"]], place.device("y", other)))
        )
    kept = sems.local(mine.at[place.at["y"]], whole.at[place.at["y"]])

    def finish():
        kept.wait()
        for step, at in sent:
            index = place.before("y", step)
            sems.arrived(at, whole.at[index], place.device("y", index))

    return finish


def start_kernel(
    silu_ref, ada_ref, x_ref, cot_ref, qkv_ref, out_ref, up_ref, down_ref,
    mod_ref, rows_ref, hot_ref, x_full, cot_full, qkv_full, out_full, up_full, down_full,
    silu_s, share_s, terms_s, send, recv, share_send, share_recv,
):
    place = Place()
    sems = Sems(send, recv)
    count, me = place.count, place.me
    width = silu_ref.shape[1] - hot_ref.shape[1]
    rows_each = ada_ref.shape[0]
    greet(place)

    half = 16 * (qkv_ref.shape[0] // 32)
    silu = Gather(place, sems, silu_ref, silu_s, "zxyc")
    units = [
        Gather(place, sems, qkv_ref, qkv_full, "zxyc", (0, half)),
        Gather(place, sems, qkv_ref, qkv_full, "zyxc", (half, qkv_ref.shape[0] - half)),
        Gather(place, sems, out_ref, out_full, "zyxc"),
        Gather(place, sems, up_ref, up_full, "zyxc"),
        Gather(place, sems, down_ref, down_full, "zxyc"),
    ]
    silu.own()
    silu.start(0)
    for unit in units[:2]:
        unit.own()
        unit.start(0)
    x_done = exchange(place, sems, x_ref, x_full)
    for unit in units[2:]:
        unit.own()
        unit.start(0)
    silu.wait(0)
    silu.start(1)
    silu.wait(1)
    silu.start(2)
    silu.wait(2)
    silu.start(3)
    silu.wait(3)

    rows = silu_s[...].reshape(count, silu_ref.shape[1])
    hot = (
        rows[:, width:] == lax.broadcasted_iota(jnp.int32, (count, hot_ref.shape[1]), 1).astype(f32)
    ).astype(bf16)
    hot_ref[...] = hot.astype(f32)
    first = lax.axis_index("dp") * rows_each
    pick = (
        lax.broadcasted_iota(jnp.int32, (width, rows_each), 0)
        == first + lax.broadcasted_iota(jnp.int32, (width, rows_each), 1)
    ).astype(bf16)
    local = mm(rows[:, :width].astype(bf16), pick).astype(bf16)
    grouped = mm(hot[:, :count], local)
    rows_ref[...] = grouped
    share = mm(grouped.astype(bf16), ada_ref[...])
    share_s[...] = share.reshape(share_s.shape)

    def push(step):
        to = lax.rem(me + step, count)
        return pltpu.make_async_remote_copy(
            src_ref=share_s.at[to], dst_ref=terms_s.at[me],
            send_sem=share_send.at[step], recv_sem=share_recv.at[step],
            device_id=place.numbered(to), device_id_type=MESH,
        )

    def came(step):
        source = lax.rem(me + count - step, count)
        return pltpu.make_async_remote_copy(
            src_ref=terms_s.at[source], dst_ref=terms_s.at[source],
            send_sem=share_send.at[step], recv_sem=share_recv.at[step],
            device_id=place.numbered(source), device_id_type=MESH,
        )

    def do_push(step, carry):
        push(step).start()
        return carry

    lax.fori_loop(1, count, do_push, 0)
    terms_s[me] = share_s[me]

    def do_wait(step, carry):
        came(step).wait_recv()
        return carry

    def do_sent(step, carry):
        push(step).wait_send()
        return carry

    for unit in units[:2]:
        unit.wait(0)
        unit.start(1)
    lax.fori_loop(1, count, do_wait, 0)
    heads = place.size["y"]
    for y in range(heads):
        mod_ref[y] = lax.fori_loop(
            0, count // heads, lambda i, total: total + terms_s[i * heads + y],
            jnp.zeros(terms_s.shape[1:], f32),
        )
    for unit in units[2:]:
        unit.wait(0)
        unit.start(1)
    cot_done = exchange(place, sems, cot_ref, cot_full)
    for stage in (1, 2):
        for unit in units:
            unit.wait(stage)
            unit.start(stage + 1)
    x_done()
    cot_done()
    for unit in units:
        unit.wait(3)
    sems.drain()
    lax.fori_loop(1, count, do_sent, 0)


def start_call(silu, order_mine, ada, x, cot, qkv, out, up, down):
    dp, head = lax.axis_size("dp"), lax.axis_size("head")
    count = dp * head
    lead = (4, 2, dp // 8, head)
    lanes = max(128, count)
    width = silu.shape[1]
    row = jnp.concatenate(
        [silu.astype(bf16).astype(f32), jnp.broadcast_to(order_mine.astype(f32), (1, lanes))], axis=1
    )
    sizes = {"z": 4, "x": 2, "c": dp // 8, "y": head}
    needed = sems_needed(sizes, 6, 2 * head)
    anywhere = pl.BlockSpec(memory_space=pl.ANY)
    vmem = pl.BlockSpec(memory_space=pltpu.VMEM)
    slot_shape = x.shape
    return pl.pallas_call(
        start_kernel,
        in_specs=[anywhere, vmem] + [anywhere] * 6,
        out_specs=[vmem] * 3 + [anywhere] * 6,
        out_shape=[
            jax.ShapeDtypeStruct((head, 1, ada.shape[1]), f32),
            jax.ShapeDtypeStruct((count, ada.shape[0]), f32),
            jax.ShapeDtypeStruct((count, lanes), f32),
            jax.ShapeDtypeStruct(slot_shape, bf16),
            jax.ShapeDtypeStruct(slot_shape, bf16),
        ]
        + [jax.ShapeDtypeStruct(lead + piece.shape, bf16) for piece in (qkv, out, up, down)],
        scratch_shapes=[
            pltpu.VMEM(lead + (1, width + lanes), f32),
            pltpu.VMEM((count, 1, ada.shape[1]), f32),
            pltpu.VMEM((count, 1, ada.shape[1]), f32),
            pltpu.SemaphoreType.DMA((needed,)),
            pltpu.SemaphoreType.DMA((needed,)),
            pltpu.SemaphoreType.DMA((count,)),
            pltpu.SemaphoreType.DMA((count,)),
        ],
        compiler_params=pltpu.CompilerParams(
            collective_id=0, has_side_effects=True, vmem_limit_bytes=VMEM_MOST
        ),
        name="gather_start",
    )(row, ada, x, cot, qkv, out, up, down)


class Scatter:
    def __init__(self, place, sems, grad, held, recvs, axes, rows=None):
        self.place, self.sems, self.grad, self.held, self.recvs, self.axes = (
            place, sems, grad, held, recvs, axes
        )
        self.rows = rows
        self.slots = {}

    @staticmethod
    def scratch(sizes, axes, rows, width):
        held = pltpu.VMEM(tuple(sizes[a] for a in "zxy") + (rows, width), bf16)
        recvs = []
        for at, axis in enumerate(axes):
            left = tuple(sizes[a] for a in "zxy" if a not in axes[: at + 1])
            recvs.append(pltpu.VMEM((sizes[axis] - 1,) + left + (rows, width), bf16))
        return [held] + recvs

    def wanted(self, of):
        spots = tuple(of if name == "c" else slice(None) for name in AXES)
        if self.rows is not None:
            spots = spots + (pl.ds(*self.rows), slice(None))
        return self.grad.at[spots]

    def share(self, stage, index):
        done = self.axes[1:stage]
        spots = []
        for name in "zxy":
            if name in done:
                spots.append(self.place.at[name])
            elif name == self.axes[stage]:
                spots.append(index)
            else:
                spots.append(slice(None))
        return self.held.at[tuple(spots)]

    def start(self, stage):
        axis = self.axes[stage]
        place = self.place
        if stage == 0:
            self.kept = self.sems.local(self.wanted(place.at["c"]), self.held)
        for step in range(1, place.size[axis]):
            index = place.after(axis, step)
            src = self.wanted(index) if stage == 0 else self.share(stage, index)
            self.slots[stage, step] = self.sems.copy(
                src, self.recvs[stage].at[step - 1], place.device(axis, index)
            )

    def arrive(self, stage):
        axis = self.axes[stage]
        place = self.place
        if stage == 0:
            self.kept.wait()
        for step in range(1, place.size[axis]):
            self.sems.arrived(
                self.slots[stage, step], self.recvs[stage].at[step - 1],
                place.device(axis, place.before(axis, step)),
            )

    def finish(self, stage):
        self.arrive(stage)
        place = self.place
        left = [a for a in "zxy" if a not in self.axes[: stage + 1]]
        recv = self.recvs[stage]

        def one(at, carry):
            spots = {}
            for a in reversed(left):
                spots[a] = lax.rem(at, place.size[a])
                at = lax.div(at, place.size[a])
            where = tuple(spots.get(a, place.at[a]) for a in "zxy")
            inner = tuple(spots[a] for a in left)
            total = self.held[where].astype(f32)
            for step in range(recv.shape[0]):
                total = total + recv[(step,) + inner].astype(f32)
            self.held[where] = total.astype(bf16)
            return carry

        lax.fori_loop(0, math.prod(place.size[a] for a in left), one, 0)

    def result(self, stage):
        self.arrive(stage)
        place = self.place
        recv = self.recvs[stage]
        total = self.held[tuple(place.at[a] for a in "zxy")].astype(f32)
        for step in range(recv.shape[0]):
            total = total + recv[step].astype(f32)
        return total


def halves(rows):
    first = 16 * (rows // 32)
    return ((0, first), (first, rows - first))


SUM_AXES = ("cyxz", "cxyz")


def sum_scratch(sizes, grads):
    scratch = []
    for rows, width, whole in grads:
        near = sizes["c"]
        scratch.append(
            pltpu.VMEM((rows, width) if whole else (near, rows // near, width), f32)
        )
        for span, axes in zip(halves(rows), SUM_AXES):
            scratch += Scatter.scratch(sizes, axes, span[1], width)
    return scratch


class Sums:
    def __init__(self, place, sems, grads, finals, scratch):
        self.place, self.sems, self.finals = place, sems, finals
        scratch = list(scratch)
        self.totals, self.pairs = [], []
        for grad in grads:
            self.totals.append(scratch.pop(0))
            pair = []
            for span, axes in zip(halves(grad.shape[4]), SUM_AXES):
                held, recvs, scratch = scratch[0], scratch[1:5], scratch[5:]
                pair.append((Scatter(place, sems, grad, held, recvs, axes, span), span))
            self.pairs.append(pair)
        self.ticks = len(self.pairs) + 3

    def start(self, tick):
        for back in range(3, -1, -1):
            if 0 <= tick - back < len(self.pairs):
                for unit, _ in self.pairs[tick - back]:
                    unit.start(back)

    def finish(self, tick):
        if 0 <= tick - 3 < len(self.pairs):
            for unit, span in self.pairs[tick - 3]:
                self.settle(tick - 3, unit, span)
        for back in range(2, -1, -1):
            if 0 <= tick - back < len(self.pairs):
                for unit, _ in self.pairs[tick - back]:
                    unit.finish(back)

    def settle(self, at, unit, span):
        value = unit.result(3)
        first, size = span
        total = self.totals[at]
        if len(total.shape) == 2:
            total[first : first + size, :] = value
            return
        each = total.shape[1]
        for to in range(total.shape[0]):
            low, high = max(first, to * each), min(first + size, (to + 1) * each)
            if low < high:
                total[to, low - to * each : high - to * each, :] = value[
                    low - first : high - first, :
                ]

    def deliver(self):
        place = self.place
        mine = place.at["c"]
        self.kept, self.flights = [], []
        for total, final in zip(self.totals, self.finals):
            if len(total.shape) == 2:
                self.kept.append(self.sems.local(total, final))
                continue
            self.kept.append(self.sems.local(total.at[mine], final.at[mine]))
            for step in range(1, place.size["c"]):
                to = place.after("c", step)
                slot = self.sems.copy(total.at[to], final.at[mine], place.device("c", to))
                self.flights.append((final, step, slot))

    def delivered(self):
        for made in self.kept:
            made.wait()
        for final, step, slot in self.flights:
            source = self.place.before("c", step)
            self.sems.arrived(slot, final.at[source], self.place.device("c", source))


def sums_kernel(act_ref, up_ref, down_ref, act_full, dup_ref, ddown_ref, send, recv, *scratch):
    place = Place()
    sems = Sems(send, recv)
    sums = Sums(place, sems, (up_ref, down_ref), (dup_ref, ddown_ref), scratch)
    greet(place)
    act_done = exchange(place, sems, act_ref, act_full)
    for tick in range(sums.ticks):
        sums.start(tick)
        sums.finish(tick)
    sums.deliver()
    sums.delivered()
    act_done()
    sems.drain()


def sizes_of():
    dp, head = lax.axis_size("dp"), lax.axis_size("head")
    return {"z": 4, "x": 2, "c": dp // 8, "y": head}


def final_shape(grad, near):
    return jax.ShapeDtypeStruct((near, grad.shape[4] // near, grad.shape[5]), f32)


def sums_call(act, up, down):
    sizes = sizes_of()
    anywhere = pl.BlockSpec(memory_space=pl.ANY)
    needed = sems_needed(sizes, 4, 2 * sizes["y"] + 4 * sizes["c"])
    return pl.pallas_call(
        sums_kernel,
        in_specs=[anywhere] * 3,
        out_specs=[anywhere] * 3,
        out_shape=[
            jax.ShapeDtypeStruct(act.shape, bf16),
            final_shape(up, sizes["c"]),
            jax.ShapeDtypeStruct(down.shape[4:], f32),
        ],
        scratch_shapes=[
            pltpu.SemaphoreType.DMA((needed,)),
            pltpu.SemaphoreType.DMA((needed,)),
        ]
        + sum_scratch(sizes, (up.shape[4:] + (False,), down.shape[4:] + (True,))),
        compiler_params=pltpu.CompilerParams(
            collective_id=2, has_side_effects=True, vmem_limit_bytes=VMEM_MOST
        ),
        name="sum_feed_forward",
    )(act, up, down)


def finish_kernel(
    row_ref, ada_ref, rows_ref, hot_ref, gin_ref, qkv_ref, out_ref,
    bias_ref, dada_ref, gsilu_ref, gin_full, dqkv_ref, dout_ref,
    send, recv, share_send, share_recv, row_s, share_s, *scratch,
):
    place = Place()
    count, me = place.count, place.me
    sems = Sems(send, recv)
    sums = Sums(place, sems, (qkv_ref, out_ref), (dqkv_ref, dout_ref), scratch)
    greet(place)
    rows = Gather(place, sems, row_ref, row_s, "zxyc")
    rows.own()
    rows.start(0)
    gin_done = exchange(place, sems, gin_ref, gin_full)
    for tick in range(sums.ticks):
        sums.start(tick)
        sums.finish(tick)
        if tick < 4:
            rows.wait(tick)
            if tick < 3:
                rows.start(tick + 1)
    sums.deliver()

    whole = row_s[...].reshape(count, row_ref.shape[1])
    bias_ref[...] = jnp.sum(whole, axis=0, keepdims=True)
    cols = ada_ref.shape[1]
    low = jnp.zeros((count, cols), f32)
    for y in range(place.size["y"]):
        low = jnp.where(place.at["y"] == y, whole[:, y * cols : (y + 1) * cols], low)
    low = low.astype(bf16)
    dada_ref[...] = lax.dot_general(
        rows_ref[...].astype(bf16), low, (((0,), (0,)), ((), ())), preferred_element_type=f32
    )
    grad = mm_nt(low, ada_ref[...])
    hot = hot_ref[...][:, :count]
    placed = lax.dot_general(
        hot, grad, (((0,), (0,)), ((), ())), precision=lax.Precision.HIGHEST,
        preferred_element_type=f32,
    )
    pad = share_s.shape[2] - placed.shape[1]
    placed = jnp.concatenate([placed, jnp.zeros((count, pad), f32)], axis=1)
    share_s[...] = placed.reshape(share_s.shape)

    def push(step):
        to = lax.rem(me + step, count)
        return pltpu.make_async_remote_copy(
            src_ref=share_s.at[to], dst_ref=gsilu_ref.at[me],
            send_sem=share_send.at[step], recv_sem=share_recv.at[step],
            device_id=place.numbered(to), device_id_type=MESH,
        )

    def came(step):
        source = lax.rem(me + count - step, count)
        return pltpu.make_async_remote_copy(
            src_ref=gsilu_ref.at[source], dst_ref=gsilu_ref.at[source],
            send_sem=share_send.at[step], recv_sem=share_recv.at[step],
            device_id=place.numbered(source), device_id_type=MESH,
        )

    def do_push(step, carry):
        push(step).start()
        return carry

    def do_wait(step, carry):
        came(step).wait_recv()
        push(step).wait_send()
        return carry

    lax.fori_loop(1, count, do_push, 0)
    gsilu_ref[me] = share_s[me]
    lax.fori_loop(1, count, do_wait, 0)
    sums.delivered()
    gin_done()
    sems.drain()


def finish_call(row, ada, silu_rows, hot, gin, qkv, out):
    sizes = sizes_of()
    near = sizes["c"]
    count = 8 * near * sizes["y"]
    anywhere = pl.BlockSpec(memory_space=pl.ANY)
    vmem = pl.BlockSpec(memory_space=pltpu.VMEM)
    needed = sems_needed(sizes, 5, 2 * sizes["y"] + 4 * near)
    return pl.pallas_call(
        finish_kernel,
        in_specs=[anywhere, vmem, vmem, vmem] + [anywhere] * 3,
        out_specs=[vmem] * 3 + [anywhere] * 3,
        out_shape=[
            jax.ShapeDtypeStruct(row.shape, f32),
            jax.ShapeDtypeStruct(ada.shape, f32),
            jax.ShapeDtypeStruct((count, 1, 128), f32),
            jax.ShapeDtypeStruct(gin.shape, bf16),
            final_shape(qkv, near),
            final_shape(out, near),
        ],
        scratch_shapes=[
            pltpu.SemaphoreType.DMA((needed,)),
            pltpu.SemaphoreType.DMA((needed,)),
            pltpu.SemaphoreType.DMA((count,)),
            pltpu.SemaphoreType.DMA((count,)),
            pltpu.VMEM((4, 2, near, sizes["y"], 1, row.shape[1]), f32),
            pltpu.VMEM((count, 1, 128), f32),
        ]
        + sum_scratch(sizes, (qkv.shape[4:] + (False,), out.shape[4:] + (False,))),
        compiler_params=pltpu.CompilerParams(
            collective_id=1, has_side_effects=True, vmem_limit_bytes=VMEM_MOST
        ),
        name="sum_finish",
    )(row, ada, silu_rows, hot, gin, qkv, out)


class Wire:
    def __init__(self, width):
        self.dp = lax.axis_size("dp")
        self.head = lax.axis_size("head")
        self.near = self.dp // (width // 144)
        self.width = width
        self.groups = [
            list(range(first, first + self.near)) for first in range(0, self.dp, self.near)
        ]

    def piece(self, weight):
        return lax.all_to_all(
            weight.astype(bf16), "dp", split_axis=1, concat_axis=0,
            axis_index_groups=self.groups, tiled=True,
        )

    def unpiece(self, piece):
        return lax.all_to_all(
            piece, "dp", split_axis=0, concat_axis=1, axis_index_groups=self.groups, tiled=True
        )

    def gather(self, piece):
        return lax.all_gather(piece, ("dp", "head"), axis=0)

    def scatter(self, stack):
        return lax.psum_scatter(stack, ("dp", "head"), scatter_dimension=0)

    def columns(self, stack):
        devices, rows, cols = stack.shape
        stack = stack.reshape(self.dp // self.near, self.near, self.head, rows, cols)
        if (self.near, self.head) != (2, 2):
            quarter = self.near * self.head * cols // 4
            stack = stack.transpose(0, 3, 2, 1, 4).reshape(-1, rows, 2, 2, quarter)
            stack = stack.transpose(0, 3, 2, 1, 4)
            return stack.reshape(-1, 4, rows, quarter)
        return stack.reshape(-1, 4, rows, cols)

    def uncolumns(self, stack):
        groups, _, rows, quarter = stack.shape
        cols = 4 * quarter // (self.near * self.head)
        if (self.near, self.head) != (2, 2):
            stack = stack.reshape(groups, 2, 2, rows, quarter).transpose(0, 3, 2, 1, 4)
            stack = stack.reshape(groups, rows, self.head, self.near, cols)
            stack = stack.transpose(0, 3, 2, 1, 4)
        return stack.reshape(self.dp * self.head, rows, cols)

    def rows(self, stack):
        devices, rows, cols = stack.shape
        if self.head != 2 or self.dp != 16:
            stack = stack.reshape(self.dp, self.head, rows, cols).transpose(0, 2, 1, 3)
            stack = stack.reshape(16, self.dp * rows // 16, 2, self.head * cols // 2)
            return stack.transpose(0, 2, 1, 3)
        return stack.reshape(self.dp, self.head, rows, cols)

    def unrows(self, stack):
        _, _, rows, cols = stack.shape
        if self.head != 2 or self.dp != 16:
            stack = stack.transpose(0, 2, 1, 3).reshape(
                self.dp, 16 * rows // self.dp, self.head, 2 * cols // self.head
            )
            stack = stack.transpose(0, 2, 1, 3)
        return stack.reshape(self.dp * self.head, stack.shape[-2], stack.shape[-1])


def body(
    inputs, cond, order, grid_kind, weight_ada, bias_ada, weight_qkv, bias_query, bias_value,
    weight_out, bias_out, weight_up, bias_up, weight_down, bias_down, cotangent,
):
    images, slot_local, width = inputs.shape
    head_count = lax.axis_size("head")
    dp_count = lax.axis_size("dp")
    head_at = lax.axis_index("head")
    dp_at = lax.axis_index("dp")
    assert images == head_count
    wire = Wire(width)

    def from_image(array):
        return lax.all_to_all(
            array[None], "head", split_axis=1, concat_axis=0, tiled=True
        ).astype(f32)

    rows_ada, cols_ada = weight_ada.shape
    ada_low = weight_ada.astype(bf16)
    silu_own, silu_pull = jax.vjp(lambda v: v * jax.nn.sigmoid(v), cond)
    order_mine = lax.dynamic_slice_in_dim(order, head_at, 1, 0)
    kind = lax.dynamic_slice_in_dim(grid_kind, head_at, 1, 0)
    mod, silu_grouped, hot, x, cot, qkv_full, out_full, up_full, down_full = start_call(
        silu_own, order_mine, ada_low, inputs.astype(bf16), cotangent.astype(bf16),
        wire.piece(weight_qkv), wire.piece(weight_out), wire.piece(weight_up),
        weight_down.astype(bf16),
    )
    x = x.reshape(-1, width)
    cot = cot.reshape(-1, width)
    device_stack = lambda full: full.reshape((-1,) + full.shape[4:])
    qkv_full = wire.columns(device_stack(qkv_full))
    out_full = wire.columns(device_stack(out_full))
    up_full = wire.columns(device_stack(up_full))
    down_full = wire.rows(device_stack(down_full))
    mod_flat = mod.reshape(6, width) + bias_ada.reshape(6, width)
    mod = jnp.concatenate([mod_flat, jnp.zeros((2, width), f32)], axis=0)

    bias_qkv = jnp.concatenate([bias_query, jnp.zeros_like(bias_query), bias_value])
    qkv, norm = qkv_call(x, mod, qkv_full, bias_qkv.reshape(4, 1, -1))
    mix, lse = attn_call(kind, qkv)
    attended, branch, second = out_call(mix, x, mod, out_full, bias_out)
    mlp, gsec, d_up, d_down, d_bias_up = mlp_call(
        second, cot, mod, up_full, down_full, bias_up.reshape(4, 1, -1)
    )
    act, gmid, gatt, d_out, sums = mid_back_call(
        x, branch, mlp, gsec, cot, attended, mod, out_full, bias_down
    )
    lead = (4, 2, dp_count // 8, head_count)
    stack = lambda grad: grad.reshape(lead + grad.shape[1:])
    by_image = lambda array: array.reshape(head_count, slot_local, width)
    act, d_up, d_down = sums_call(
        by_image(act), stack(wire.uncolumns(d_up)), stack(wire.unrows(d_down))
    )
    grad = attn_back_call(kind, qkv, gatt, lse)
    gin, d_qkv, d_bias_qkv, sums_in = qkv_back_call(
        grad.reshape(qkv.shape), norm, qkv_full, x, gmid, mod
    )

    bias_qkv_sum = d_bias_qkv.reshape(3, width)
    row = jnp.concatenate(
        [sums_in[0], sums_in[1], sums[0], sums[1], sums[2], sums[3],
         bias_qkv_sum[0], bias_qkv_sum[2], sums[4], sums[5], d_bias_up.reshape(-1)]
    ).reshape(1, -1)
    biases, d_ada, g_silu, gin, d_qkv, d_out = finish_call(
        row, ada_low, silu_grouped, hot, by_image(gin),
        stack(wire.uncolumns(d_qkv)), stack(wire.uncolumns(d_out)),
    )
    biases = biases[0]
    g_silu = g_silu.reshape(dp_count, head_count, 128)[:, :, :rows_ada].sum(axis=1)
    d_cond = silu_pull(g_silu.reshape(1, width))[0]
    side = lambda grad: grad.transpose(1, 0, 2).reshape(grad.shape[1], -1)
    mods = 6 * width
    return (
        act.astype(f32),
        gin.astype(f32),
        d_cond,
        d_ada,
        side(d_qkv),
        side(d_out),
        side(d_up),
        d_down,
        biases[:mods],
        biases[mods : mods + width],
        biases[mods + width : mods + 2 * width],
        biases[mods + 2 * width : mods + 3 * width],
        biases[mods + 4 * width :],
        biases[mods + 3 * width : mods + 4 * width],
    )


def solution(mesh):
    in_specs = (
        P("dp", "head", None), P(("dp", "head"), None), P("dp"), P("dp"), P("dp", "head"), P(),
        P("dp", "head"), P(), P(), P("dp", "head"), P(), P("dp", "head"), P(), P("dp", "head"),
        P(), P("dp", "head", None),
    )
    out_specs = (
        P("dp", "head", None), P("dp", "head", None), P(("dp", "head"), None), P("dp", "head"),
        P("dp", "head"), P("dp", "head"), P("dp", "head"), P("dp", "head"),
        P(), P(), P(), P(), P(), P(),
    )
    return jax.shard_map(body, mesh=mesh, in_specs=in_specs, out_specs=out_specs, check_vma=False)
```

```python
import functools
import math

import jax
import jax.numpy as jnp
from jax import lax
from jax.experimental import pallas as pl
from jax.experimental.pallas import tpu as pltpu
from jax.sharding import PartitionSpec as P

H = 16
norm_eps = 1e-06
log2_e = 1.4426950408889634
gelu_in = 0.7978845608028654
gelu_cube = 0.044715
f32 = jnp.float32
bf16 = jnp.bfloat16
VMEM_MOST = 60 * 1024 * 1024


def mm(left, right):
    return jnp.dot(left, right, preferred_element_type=f32)


def mm_nt(left, right):
    return lax.dot_general(left, right, (((1,), (1,)), ((), ())), preferred_element_type=f32)


def center_spread(values):
    center = values - jnp.mean(values, axis=-1, keepdims=True)
    spread = jnp.mean(center * center, axis=-1, keepdims=True)
    return center, lax.rsqrt(spread + norm_eps)


def norm_back(grad, unit, inv):
    return inv * (
        grad
        - jnp.mean(grad, axis=-1, keepdims=True)
        - unit * jnp.mean(grad * unit, axis=-1, keepdims=True)
    )


def whole_spec(shape):
    zeros = (0,) * len(shape)
    return pl.BlockSpec(shape, lambda *_: zeros)


def once_spec(shape):
    zeros = (0,) * len(shape)
    return pl.BlockSpec(shape, lambda *_: zeros, pipeline_mode=pl.Buffered(1))


def params(most=VMEM_MOST):
    return pltpu.CompilerParams(vmem_limit_bytes=most)


def place(quarter):
    return (quarter % 2) * 2 + quarter // 2


def masked(scores, full, kept):
    return jnp.concatenate(
        [scores[:kept], jnp.where(full, scores[kept:], -1e30)], axis=0
    )


def columns_of(w_ref):
    groups, parts, rows_each, width = w_ref.shape
    return jnp.concatenate(
        [w_ref[:, place(n)].reshape(groups * rows_each, width) for n in range(parts)], axis=1
    )


def out_kernel(
    o_ref, x_ref, cot_ref, mod_ref, w_ref, b_ref, att_ref, branch_ref, second_ref, gm_ref, w_s
):
    @pl.when(pl.program_id(0) == 0)
    def _():
        w_s[...] = columns_of(w_ref)

    attended = jnp.concatenate([o_ref[j] for j in range(o_ref.shape[0])], axis=1)
    att_ref[...] = attended
    branch = mm(attended, w_s[...]) + b_ref[...]
    branch_ref[...] = branch.astype(bf16)
    middle = x_ref[...].astype(f32) + mod_ref[2:3, :] * branch
    center, inv = center_spread(middle)
    second_ref[...] = (center * inv * (1.0 + mod_ref[4:5, :]) + mod_ref[3:4, :]).astype(bf16)
    gm_ref[...] = (cot_ref[...].astype(f32) * mod_ref[5:6, :]).astype(bf16)


def out_call(mix, x, cot, mod, weight, bias):
    slots, width = x.shape
    tm = min(256, slots)
    size = width // H
    tile = pl.BlockSpec((tm, width), lambda i: (i, 0))
    return pl.pallas_call(
        out_kernel,
        grid=(slots // tm,),
        in_specs=[
            pl.BlockSpec((H, tm, size), lambda i: (0, i, 0)),
            tile,
            tile,
            whole_spec(mod.shape),
            whole_spec(weight.shape),
            whole_spec((1, width)),
        ],
        out_specs=[tile] * 4,
        out_shape=[jax.ShapeDtypeStruct((slots, width), bf16)] * 4,
        scratch_shapes=[pltpu.VMEM((width, width), bf16)],
        compiler_params=params(),
        name="out_projection",
    )(mix, x, cot, mod, weight, bias.reshape(1, width))


def mid_back_kernel(
    x_ref, branch_ref, mlp_ref, gsec_ref, cot_ref, att_ref, mod_ref, w_ref, b_ref,
    act_ref, gmid_ref, gatt_ref, dw_ref, sums_ref, w_s, dw_s,
):
    step = pl.program_id(0)

    @pl.when(step == 0)
    def _():
        w_s[...] = columns_of(w_ref)
        sums_ref[...] = jnp.zeros_like(sums_ref)
        dw_s[...] = jnp.zeros_like(dw_s)

    gate_a = mod_ref[2:3, :]
    gate_m = mod_ref[5:6, :]
    branch = branch_ref[...].astype(f32)
    middle = x_ref[...].astype(f32) + gate_a * branch
    mlp = mlp_ref[...] + b_ref[...]
    cot = cot_ref[...].astype(f32)
    act_ref[...] = (middle + gate_m * mlp).astype(act_ref.dtype)
    center, inv = center_spread(middle)
    unit = center * inv
    grad = gsec_ref[...]
    grad_mid = cot + norm_back(grad * (1.0 + mod_ref[4:5, :]), unit, inv)
    gmid_ref[...] = grad_mid
    grad_branch = gate_a * grad_mid

    def add(row, value):
        sums_ref[row : row + 1, :] += jnp.sum(value, axis=0, keepdims=True)

    add(0, grad_mid * branch)
    add(1, grad)
    add(2, grad * unit)
    add(3, cot * mlp)
    add(4, grad_branch)
    add(5, gate_m * cot)
    grad_low = grad_branch.astype(bf16)
    grad_att = mm_nt(grad_low, w_s[...]).astype(bf16)
    size = gatt_ref.shape[2]
    for j in range(gatt_ref.shape[0]):
        gatt_ref[j] = grad_att[:, j * size : (j + 1) * size]
    dw_s[...] += mm(att_ref[...].T, grad_low)

    @pl.when(step == pl.num_programs(0) - 1)
    def _():
        groups, parts, rows_each, width = dw_ref.shape
        low = dw_s[...].astype(bf16)
        for n in range(parts):
            dw_ref[:, place(n)] = low[:, n * width : (n + 1) * width].reshape(
                groups, rows_each, width
            )


def mid_back_call(x, branch, mlp, gsec, cot, attended, mod, weight, bias_down):
    slots, width = x.shape
    tm = min(256, slots)
    size = width // H
    tile = pl.BlockSpec((tm, width), lambda i: (i, 0))
    return pl.pallas_call(
        mid_back_kernel,
        grid=(slots // tm,),
        in_specs=[tile] * 6 + [whole_spec(mod.shape), whole_spec(weight.shape), whole_spec((1, width))],
        out_specs=[
            tile,
            tile,
            pl.BlockSpec((H, tm, size), lambda i: (0, i, 0)),
            whole_spec(weight.shape),
            whole_spec((8, width)),
        ],
        out_shape=[
            jax.ShapeDtypeStruct((slots, width), bf16),
            jax.ShapeDtypeStruct((slots, width), f32),
            jax.ShapeDtypeStruct((H, slots, size), bf16),
            jax.ShapeDtypeStruct(weight.shape, bf16),
            jax.ShapeDtypeStruct((8, width), f32),
        ],
        scratch_shapes=[pltpu.VMEM((width, width), bf16), pltpu.VMEM((width, width), f32)],
        compiler_params=params(),
        name="middle_backward",
    )(x, branch, mlp, gsec, cot, attended, mod, weight, bias_down.reshape(1, width))


MESH = pl.DeviceIdType.MESH


class Place:
    def __init__(self):
        self.dp = lax.axis_size("dp")
        head = lax.axis_size("head")
        near = self.dp // 8
        at = lax.axis_index("dp")
        self.size = {"z": 4, "x": 2, "c": near, "y": head}
        self.at = {
            "z": lax.div(at, 2 * near),
            "x": lax.rem(lax.div(at, near), 2),
            "c": lax.rem(at, near),
            "y": lax.axis_index("head"),
        }
        self.count = self.dp * head
        self.me = at * head + self.at["y"]

    def device(self, axis, index):
        spot = dict(self.at)
        spot[axis] = index
        return ((spot["z"] * 2 + spot["x"]) * self.size["c"] + spot["c"], spot["y"])

    def numbered(self, index):
        head = self.size["y"]
        return (lax.div(index, head), lax.rem(index, head))

    def after(self, axis, step):
        return lax.rem(self.at[axis] + step, self.size[axis])

    def before(self, axis, step):
        return lax.rem(self.at[axis] + self.size[axis] - step, self.size[axis])


class Local:
    def __init__(self, sem, ends):
        self.sem, self.ends = sem, ends

    def made(self):
        return pltpu.make_async_copy(*self.ends(), self.sem())

    def wait(self):
        self.made().wait()


class Sems:
    def __init__(self, send, recv):
        self.send, self.recv, self.used = send, recv, 0
        self.sent = []

    def describe(self, at, src, dst, device):
        return pltpu.make_async_remote_copy(
            src_ref=src, dst_ref=dst, send_sem=self.send.at[at], recv_sem=self.recv.at[at],
            device_id=device, device_id_type=MESH,
        )

    def copy(self, ends):
        at = self.used
        self.used += 1
        self.describe(at, *ends()).start()
        self.sent.append((at, ends))
        return at

    def arrived(self, at, dst, device):
        self.describe(at, dst, dst, device).wait_recv()

    def local(self, ends):
        at = self.used
        self.used += 1
        made = Local(lambda: self.send.at[at], ends)
        made.made().start()
        return made

    def drain(self):
        for at, ends in self.sent:
            self.describe(at, *ends()).wait_send()


AXES = "zxcy"


def spans_of(rows, count):
    cuts = [16 * (rows // 16 * at // count) for at in range(count)] + [rows]
    return [(low, high - low) for low, high in zip(cuts, cuts[1:])]


def halves(rows):
    return spans_of(rows, 2)


class Gather:
    def __init__(self, place, sems, piece, full, axes, rows=None):
        self.place, self.sems, self.piece, self.full, self.axes = place, sems, piece, full, axes
        self.rows = rows
        self.slots = {}

    def part(self, got, axis=None, index=None):
        spot = dict(self.place.at)
        if axis is not None:
            spot[axis] = index
        spots = tuple(slice(None) if name in got else spot[name] for name in AXES)
        if self.rows is not None:
            spots = spots + (pl.ds(*self.rows), slice(None))
        return self.full.at[spots]

    def first(self):
        return self.piece if self.rows is None else self.piece.at[pl.ds(*self.rows)]

    def own(self):
        self.kept = self.sems.local(lambda: (self.first(), self.part("")))

    def start(self, stage):
        axis = self.axes[stage]
        got = self.axes[:stage]
        if stage == 1:
            self.kept.wait()

        def ends(step):
            return (
                self.first() if stage == 0 else self.part(got),
                self.part(got),
                self.place.device(axis, self.place.after(axis, step)),
            )

        for step in range(1, self.place.size[axis]):
            self.slots[stage, step] = self.sems.copy(functools.partial(ends, step))

    def wait(self, stage):
        axis = self.axes[stage]
        got = self.axes[:stage]
        for step in range(1, self.place.size[axis]):
            index = self.place.before(axis, step)
            self.sems.arrived(
                self.slots[stage, step], self.part(got, axis, index), self.place.device(axis, index)
            )


EVEN = ("zxyc", "zyxc")
WIDE = ("zyxc", "yzxc")


class Gathers:
    def __init__(self, place, sems, spans, orders):
        self.pairs = []
        for at in range(0, len(spans), 2):
            pair = orders[at // 2 % len(orders)]
            self.pairs.append(
                [
                    Gather(place, sems, piece, full, axes, rows)
                    for (piece, full, rows), axes in zip(spans[at : at + 2], pair)
                ]
            )
        self.ticks = len(self.pairs) + 3

    def advance(self, tick):
        if tick < len(self.pairs):
            for unit in self.pairs[tick]:
                unit.own()
                unit.start(0)
        for stage in (1, 0, 2, 3):
            if 0 <= tick - 1 - stage < len(self.pairs):
                for unit in self.pairs[tick - 1 - stage]:
                    unit.wait(stage)
                    if stage < 3:
                        unit.start(stage + 1)


def greet_all(place):
    barrier = pltpu.get_barrier_semaphore()

    def one(step, carry):
        pl.semaphore_signal(
            barrier, inc=1, device_id=place.numbered(lax.rem(place.me + step, place.count)),
            device_id_type=MESH,
        )
        return carry

    lax.fori_loop(1, place.count, one, 0)
    pl.semaphore_wait(barrier, place.count - 1)


def greet(place):
    barrier = pltpu.get_barrier_semaphore()
    for axis in AXES:
        for step in range(1, place.size[axis]):
            pl.semaphore_signal(
                barrier, inc=1, device_id=place.device(axis, place.after(axis, step)),
                device_id_type=MESH,
            )


def met(place):
    pl.semaphore_wait(pltpu.get_barrier_semaphore(), sum(n - 1 for n in place.size.values()))


def sems_needed(sizes, units, pairs):
    return units * (1 + sum(size - 1 for size in sizes.values())) + pairs


class Exchange:
    def __init__(self, place, sems, mine, whole):
        self.place, self.sems, self.mine, self.whole = place, sems, mine, whole

    def start(self):
        place = self.place
        at = place.at["y"]
        self.kept = self.sems.local(lambda: (self.mine.at[at], self.whole.at[at]))

        def ends(step):
            other = place.after("y", step)
            return self.mine.at[other], self.whole.at[at], place.device("y", other)

        self.sent = [
            (step, self.sems.copy(functools.partial(ends, step)))
            for step in range(1, place.size["y"])
        ]
        return self

    def finish(self):
        self.kept.wait()
        for step, slot in self.sent:
            index = self.place.before("y", step)
            self.sems.arrived(slot, self.whole.at[index], self.place.device("y", index))


def exchange(place, sems, mine, whole):
    return Exchange(place, sems, mine, whole).start().finish


START_ORDERS = (WIDE,)
FRONT_ORDERS = (EVEN,)
MLP_ORDERS = (EVEN,)
MLP_SUM_ORDERS = (EVEN,)
BACK_ORDERS = (EVEN,)
FINISH_ORDERS = (WIDE,)


def start_kernel(
    silu_ref, ada_ref, x_ref, qkv_ref, mod_ref, rows_ref, hot_ref, x_full, qkv_full, silu_s, share_s, terms_s, send, recv, share_send, share_recv,
):
    place = Place()
    sems = Sems(send, recv)
    count, me = place.count, place.me
    width = silu_ref.shape[1] - hot_ref.shape[1]
    rows_each = ada_ref.shape[0]
    greet_all(place)

    silu = Gather(place, sems, silu_ref, silu_s, "czxy")
    gathers = Gathers(place, sems, [(qkv_ref, qkv_full, span) for span in spans_of(qkv_ref.shape[0], 4)], START_ORDERS)
    silu.own()
    silu.start(0)
    gathers.advance(0)
    silu.wait(0)
    silu.start(1)
    silu.wait(1)
    silu.start(2)
    silu.wait(2)
    silu.start(3)
    gathers.advance(1)
    silu.wait(3)

    rows = silu_s[...].reshape(count, silu_ref.shape[1])
    hot = (
        rows[:, width:] == lax.broadcasted_iota(jnp.int32, (count, hot_ref.shape[1]), 1).astype(f32)
    ).astype(bf16)
    hot_ref[...] = hot.astype(f32)
    first = lax.axis_index("dp") * rows_each
    pick = (
        lax.broadcasted_iota(jnp.int32, (width, rows_each), 0)
        == first + lax.broadcasted_iota(jnp.int32, (width, rows_each), 1)
    ).astype(bf16)
    local = mm(rows[:, :width].astype(bf16), pick).astype(bf16)
    grouped = mm(hot[:, :count], local)
    rows_ref[...] = grouped
    share = mm(grouped.astype(bf16), ada_ref[...])
    share_s[...] = share.reshape(share_s.shape)

    def push(step):
        to = lax.rem(me + step, count)
        return pltpu.make_async_remote_copy(
            src_ref=share_s.at[to], dst_ref=terms_s.at[me],
            send_sem=share_send.at[step], recv_sem=share_recv.at[step],
            device_id=place.numbered(to), device_id_type=MESH,
        )

    def came(step):
        source = lax.rem(me + count - step, count)
        return pltpu.make_async_remote_copy(
            src_ref=terms_s.at[source], dst_ref=terms_s.at[source],
            send_sem=share_send.at[step], recv_sem=share_recv.at[step],
            device_id=place.numbered(source), device_id_type=MESH,
        )

    def do_push(step, carry):
        push(step).start()
        return carry

    lax.fori_loop(1, count, do_push, 0)
    terms_s[me] = share_s[me]

    def do_wait(step, carry):
        came(step).wait_recv()
        return carry

    def do_sent(step, carry):
        push(step).wait_send()
        return carry

    x_done = exchange(place, sems, x_ref, x_full)
    gathers.advance(2)
    lax.fori_loop(1, count, do_wait, 0)
    heads = place.size["y"]
    for y in range(heads):
        mod_ref[y] = lax.fori_loop(
            0, count // heads, lambda i, total: total + terms_s[i * heads + y],
            jnp.zeros(terms_s.shape[1:], f32),
        )
    for tick in range(3, gathers.ticks + 1):
        gathers.advance(tick)
    x_done()
    sems.drain()
    lax.fori_loop(1, count, do_sent, 0)


def start_call(silu, order_mine, ada, x, qkv):
    dp, head = lax.axis_size("dp"), lax.axis_size("head")
    count = dp * head
    lead = (4, 2, dp // 8, head)
    lanes = max(128, count)
    width = silu.shape[1]
    row = jnp.concatenate(
        [silu.astype(bf16).astype(f32), jnp.broadcast_to(order_mine.astype(f32), (1, lanes))], axis=1
    )
    sizes = {"z": 4, "x": 2, "c": dp // 8, "y": head}
    needed = sems_needed(sizes, 5, 2 * head)
    anywhere = pl.BlockSpec(memory_space=pl.ANY)
    vmem = pl.BlockSpec(memory_space=pltpu.VMEM)
    slot_shape = x.shape
    return pl.pallas_call(
        start_kernel,
        in_specs=[anywhere, vmem] + [anywhere] * 2,
        out_specs=[vmem] * 3 + [anywhere] * 2,
        out_shape=[
            jax.ShapeDtypeStruct((head, 1, ada.shape[1]), f32),
            jax.ShapeDtypeStruct((count, ada.shape[0]), f32),
            jax.ShapeDtypeStruct((count, lanes), f32),
            jax.ShapeDtypeStruct(slot_shape, bf16),
            jax.ShapeDtypeStruct(lead + qkv.shape, bf16),
        ],
        scratch_shapes=[
            pltpu.VMEM(lead + (1, width + lanes), f32),
            pltpu.VMEM((count, 1, ada.shape[1]), f32),
            pltpu.VMEM((count, 1, ada.shape[1]), f32),
            pltpu.SemaphoreType.DMA((needed,)),
            pltpu.SemaphoreType.DMA((needed,)),
            pltpu.SemaphoreType.DMA((count,)),
            pltpu.SemaphoreType.DMA((count,)),
        ],
        compiler_params=pltpu.CompilerParams(
            collective_id=0, has_side_effects=True, vmem_limit_bytes=VMEM_MOST
        ),
        name="gather_start",
    )(row, ada, x, qkv)


def front_kernel(
    tiles, ts, kind_ref, x_ref, mod_ref, w_ref, b_ref, out_p, up_p, down_p, cot_p,
    qkv_ref, norm_ref, o_ref, lse_ref, out_f, up_f, down_f, cot_f,
    qkv_s, norm_s, copied, send, recv,
):
    step = pl.program_id(0)
    groups, _, rows_each, width = w_ref.shape
    _, slots, size = qkv_s.shape
    heads = width // size
    parts = 3 * H // heads
    tm = slots // tiles
    first_head = parts * tiles
    last = first_head + H - 1

    place = Place()
    sems = Sems(send, recv)
    wanted = []
    for piece, full, count in ((up_p, up_f, 4), (down_p, down_f, 4), (out_p, out_f, 2)):
        wanted += [(piece, full, span) for span in spans_of(piece.shape[0], count)]
    gathers = Gathers(place, sems, wanted, FRONT_ORDERS)
    keep = pltpu.make_async_copy(qkv_s, qkv_ref, copied.at[0])
    keep_norm = pltpu.make_async_copy(norm_s, norm_ref, copied.at[1])
    cot_done = None
    for tick in range(gathers.ticks):
        at = min(FRONT_STEPS[tick], last)
        if tick == 0:
            @pl.when(step == 0)
            def _():
                greet(place)

            @pl.when(step == at)
            def _():
                met(place)
                gathers.advance(0)
        elif at < last:
            if tick == 1:
                cot_done = Exchange(place, sems, cot_p, cot_f)

            @pl.when(step == at)
            def _(tick=tick):
                gathers.advance(tick)
                if tick == 1:
                    cot_done.start()

    @pl.when(step < first_head)
    def _():
        rows = pl.ds(pl.multiple_of(lax.rem(step, tiles) * tm, tm), tm)
        part = lax.div(step, tiles)

        @pl.when(part == 0)
        def _():
            center, inv = center_spread(x_ref[...].astype(f32))
            norm_s[rows, :] = (
                center * inv * (1.0 + mod_ref[1:2, :]) + mod_ref[0:1, :]
            ).astype(bf16)

        weight = w_ref[...].reshape(groups * rows_each, width)
        out = (mm(norm_s[rows, :], weight) + b_ref[0]).astype(bf16)
        for j in range(heads):
            qkv_s[part * heads + j, rows, :] = out[:, j * size : (j + 1) * size]

    @pl.when(step == first_head)
    def _():
        keep.start()
        keep_norm.start()

    @pl.when(step >= first_head)
    def _():
        head = step - first_head
        kept = slots - slots // 16
        factor = log2_e * size ** (-0.5)
        full = kind_ref[0] == 0
        keys = qkv_s[H + head]
        values_t = qkv_s[2 * H + head].T
        for start in range(0, slots, ts):
            here = slice(start, start + ts)
            scores = masked(mm_nt(keys, qkv_s[head, here, :]), full, kept)
            peak = jnp.max(scores, axis=0, keepdims=True) * factor
            exponent = jnp.exp2(scores * factor - peak)
            total = jnp.sum(exponent, axis=0, keepdims=True)
            mix = mm(values_t, exponent.astype(bf16)) * (1.0 / total)
            o_ref[0, here, :] = mix.T.astype(bf16)
            lse_ref[0, :, here] = peak + jnp.log2(total)

    @pl.when(step == last)
    def _():
        for tick in range(gathers.ticks):
            if FRONT_STEPS[tick] >= last:
                gathers.advance(tick)
        gathers.advance(gathers.ticks)
        cot_done.finish()
        keep.wait()
        keep_norm.wait()
        sems.drain()


FRONT_STEPS = (1, 3, 6, 10, 14, 18, 21, 99)


def front_call(kind, x, mod, weight, bias, out, up, down, cot):
    slots, width = x.shape
    tiles = 2
    groups, parts, rows_each, part_width = weight.shape
    size = width // H
    sizes = sizes_of()
    lead = tuple(sizes[a] for a in AXES)
    needed = sems_needed(sizes, 10, 2 * sizes["y"])
    first_head = parts * tiles
    anywhere = pl.BlockSpec(memory_space=pl.ANY)

    def part(s):
        return jnp.minimum(lax.div(s, tiles), parts - 1)

    def head(s):
        return jnp.maximum(s - first_head, 0)

    return pl.pallas_call(
        functools.partial(front_kernel, tiles, min(256, slots)),
        grid=(first_head + H,),
        in_specs=[
            pl.BlockSpec(memory_space=pltpu.SMEM),
            pl.BlockSpec((slots // tiles, width), lambda s: (jnp.where(s < tiles, s, tiles - 1), 0)),
            whole_spec(mod.shape),
            pl.BlockSpec(
                (groups, 1, rows_each, part_width),
                lambda s: (0, lax.rem(part(s), 2) * 2 + lax.div(part(s), 2), 0, 0),
            ),
            pl.BlockSpec((1, 1, part_width), lambda s: (part(s), 0, 0)),
        ]
        + [anywhere] * 4,
        out_specs=[
            anywhere,
            anywhere,
            pl.BlockSpec((1, slots, size), lambda s: (head(s), 0, 0)),
            pl.BlockSpec((1, 1, slots), lambda s: (head(s), 0, 0)),
        ]
        + [anywhere] * 4,
        out_shape=[
            jax.ShapeDtypeStruct((3 * H, slots, size), bf16),
            jax.ShapeDtypeStruct((slots, width), bf16),
            jax.ShapeDtypeStruct((H, slots, size), bf16),
            jax.ShapeDtypeStruct((H, 1, slots), f32),
        ]
        + [jax.ShapeDtypeStruct(lead + piece.shape, bf16) for piece in (out, up, down)]
        + [jax.ShapeDtypeStruct(cot.shape, bf16)],
        scratch_shapes=[
            pltpu.VMEM((3 * H, slots, size), bf16),
            pltpu.VMEM((slots, width), bf16),
            pltpu.SemaphoreType.DMA((2,)),
            pltpu.SemaphoreType.DMA((needed,)),
            pltpu.SemaphoreType.DMA((needed,)),
        ],
        compiler_params=pltpu.CompilerParams(
            collective_id=3, has_side_effects=True, vmem_limit_bytes=VMEM_MOST
        ),
        name="front",
    )(kind, x, mod, weight, bias, out, up, down, cot)


class Scatter:
    def __init__(self, place, sems, grad, held, recvs, axes, rows=None):
        self.place, self.sems, self.grad, self.held, self.recvs, self.axes = (
            place, sems, grad, held, recvs, axes
        )
        self.rows = rows
        self.slots = {}

    @staticmethod
    def scratch(sizes, axes, rows, width):
        held = pltpu.VMEM(tuple(sizes[a] for a in "zxy") + (rows, width), bf16)
        recvs = []
        for at, axis in enumerate(axes):
            left = tuple(sizes[a] for a in "zxy" if a not in axes[: at + 1])
            recvs.append(pltpu.VMEM((sizes[axis] - 1,) + left + (rows, width), bf16))
        return [held] + recvs

    def wanted(self, of):
        spots = tuple(of if name == "c" else slice(None) for name in AXES)
        if self.rows is not None:
            spots = spots + (pl.ds(*self.rows), slice(None))
        return self.grad.at[spots]

    def share(self, stage, index):
        done = self.axes[1:stage]
        spots = []
        for name in "zxy":
            if name in done:
                spots.append(self.place.at[name])
            elif name == self.axes[stage]:
                spots.append(index)
            else:
                spots.append(slice(None))
        return self.held.at[tuple(spots)]

    def start(self, stage):
        axis = self.axes[stage]
        place = self.place
        if stage == 0:
            self.kept = self.sems.local(lambda: (self.wanted(place.at["c"]), self.held))

        def ends(step):
            index = place.after(axis, step)
            src = self.wanted(index) if stage == 0 else self.share(stage, index)
            return src, self.recvs[stage].at[step - 1], place.device(axis, index)

        for step in range(1, place.size[axis]):
            self.slots[stage, step] = self.sems.copy(functools.partial(ends, step))

    def arrive(self, stage):
        axis = self.axes[stage]
        place = self.place
        if stage == 0:
            self.kept.wait()
        for step in range(1, place.size[axis]):
            self.sems.arrived(
                self.slots[stage, step], self.recvs[stage].at[step - 1],
                place.device(axis, place.before(axis, step)),
            )

    def finish(self, stage):
        self.arrive(stage)
        place = self.place
        left = [a for a in "zxy" if a not in self.axes[: stage + 1]]
        recv = self.recvs[stage]

        def one(at, carry):
            spots = {}
            for a in reversed(left):
                spots[a] = lax.rem(at, place.size[a])
                at = lax.div(at, place.size[a])
            where = tuple(spots.get(a, place.at[a]) for a in "zxy")
            inner = tuple(spots[a] for a in left)
            total = self.held[where].astype(f32)
            for step in range(recv.shape[0]):
                total = total + recv[(step,) + inner].astype(f32)
            self.held[where] = total.astype(bf16)
            return carry

        lax.fori_loop(0, math.prod(place.size[a] for a in left), one, 0)

    def result(self, stage):
        self.arrive(stage)
        place = self.place
        recv = self.recvs[stage]
        total = self.held[tuple(place.at[a] for a in "zxy")].astype(f32)
        for step in range(recv.shape[0]):
            total = total + recv[step].astype(f32)
        return total


def sum_axes(orders, at):
    return orders[at // 2 % len(orders)][at % 2][::-1]


def sum_scratch(sizes, grads, orders):
    scratch, number = [], 0
    for rows, width, whole, count in grads:
        near = sizes["c"]
        scratch.append(
            pltpu.VMEM((rows, width) if whole else (near, rows // near, width), f32)
        )
        for span in spans_of(rows, count):
            scratch += Scatter.scratch(sizes, sum_axes(orders, number), span[1], width)
            number += 1
    return scratch


class Sums:
    def __init__(self, place, sems, grads, finals, scratch, orders):
        self.place, self.sems, self.finals = place, sems, finals
        scratch = list(scratch)
        self.totals, self.pairs = [], []
        at = -1
        for which, (grad, count) in enumerate(grads):
            self.totals.append(scratch.pop(0))
            for span in spans_of(grad.shape[4], count):
                at += 1
                axes = sum_axes(orders, at)
                held, recvs, scratch = scratch[0], scratch[1:5], scratch[5:]
                unit = Scatter(place, sems, grad, held, recvs, axes, span)
                if at % 2 == 0:
                    self.pairs.append([])
                self.pairs[-1].append((unit, span, which))
        self.ticks = len(self.pairs) + 3

    def advance(self, tick):
        if tick < len(self.pairs):
            for unit, *_ in self.pairs[tick]:
                unit.start(0)
        for stage in (0, 2, 1, 3):
            if 0 <= tick - 1 - stage < len(self.pairs):
                for unit, span, which in self.pairs[tick - 1 - stage]:
                    if stage == 3:
                        self.settle(which, unit, span)
                    else:
                        unit.finish(stage)
                        unit.start(stage + 1)

    def settle(self, at, unit, span):
        value = unit.result(3)
        first, size = span
        total = self.totals[at]
        if len(total.shape) == 2:
            total[first : first + size, :] = value
            return
        each = total.shape[1]
        for to in range(total.shape[0]):
            low, high = max(first, to * each), min(first + size, (to + 1) * each)
            if low < high:
                total[to, low - to * each : high - to * each, :] = value[
                    low - first : high - first, :
                ]

    def deliver(self):
        place = self.place
        mine = place.at["c"]
        self.kept, self.flights = [], []
        def ends(total, final, step):
            to = place.after("c", step)
            return total.at[to], final.at[mine], place.device("c", to)

        for total, final in zip(self.totals, self.finals):
            if len(total.shape) == 2:
                self.kept.append(self.sems.local(lambda t=total, f=final: (t, f)))
                continue
            self.kept.append(self.sems.local(lambda t=total, f=final: (t.at[mine], f.at[mine])))
            for step in range(1, place.size["c"]):
                slot = self.sems.copy(functools.partial(ends, total, final, step))
                self.flights.append((final, step, slot))

    def delivered(self):
        for made in self.kept:
            made.wait()
        for final, step, slot in self.flights:
            source = self.place.before("c", step)
            self.sems.arrived(slot, final.at[source], self.place.device("c", source))


def sizes_of():
    dp, head = lax.axis_size("dp"), lax.axis_size("head")
    return {"z": 4, "x": 2, "c": dp // 8, "y": head}


def final_shape(grad, near):
    return jax.ShapeDtypeStruct((near, grad.shape[4] // near, grad.shape[5]), f32)


def finish_kernel(
    row_ref, ada_ref, rows_ref, hot_ref, gin_ref, qkv_ref,
    bias_ref, dada_ref, gsilu_ref, gin_full, dqkv_ref,
    send, recv, share_send, share_recv, row_s, share_s, *scratch,
):
    place = Place()
    count, me = place.count, place.me
    sems = Sems(send, recv)
    sums = Sums(
        place, sems, [(qkv_ref, FINISH_SPANS)], (dqkv_ref,), scratch, FINISH_ORDERS
    )
    greet_all(place)
    rows = Gather(place, sems, row_ref, row_s, "zxyc")
    rows.own()
    rows.start(0)
    gin_done = exchange(place, sems, gin_ref, gin_full)
    sums.advance(0)
    for tick in range(1, sums.ticks + 1):
        sums.advance(tick)
        if tick < 5:
            rows.wait(tick - 1)
            if tick < 4:
                rows.start(tick)
    sums.deliver()

    whole = row_s[...].reshape(count, row_ref.shape[1])
    bias_ref[...] = jnp.sum(whole, axis=0, keepdims=True)
    cols = ada_ref.shape[1]
    low = jnp.zeros((count, cols), f32)
    for y in range(place.size["y"]):
        low = jnp.where(place.at["y"] == y, whole[:, y * cols : (y + 1) * cols], low)
    low = low.astype(bf16)
    dada_ref[...] = lax.dot_general(
        rows_ref[...].astype(bf16), low, (((0,), (0,)), ((), ())), preferred_element_type=f32
    )
    grad = mm_nt(low, ada_ref[...])
    hot = hot_ref[...][:, :count]
    placed = lax.dot_general(
        hot, grad, (((0,), (0,)), ((), ())), precision=lax.Precision.HIGHEST,
        preferred_element_type=f32,
    )
    pad = share_s.shape[2] - placed.shape[1]
    placed = jnp.concatenate([placed, jnp.zeros((count, pad), f32)], axis=1)
    share_s[...] = placed.reshape(share_s.shape)

    def push(step):
        to = lax.rem(me + step, count)
        return pltpu.make_async_remote_copy(
            src_ref=share_s.at[to], dst_ref=gsilu_ref.at[me],
            send_sem=share_send.at[step], recv_sem=share_recv.at[step],
            device_id=place.numbered(to), device_id_type=MESH,
        )

    def came(step):
        source = lax.rem(me + count - step, count)
        return pltpu.make_async_remote_copy(
            src_ref=gsilu_ref.at[source], dst_ref=gsilu_ref.at[source],
            send_sem=share_send.at[step], recv_sem=share_recv.at[step],
            device_id=place.numbered(source), device_id_type=MESH,
        )

    def do_push(step, carry):
        push(step).start()
        return carry

    def do_wait(step, carry):
        came(step).wait_recv()
        push(step).wait_send()
        return carry

    lax.fori_loop(1, count, do_push, 0)
    gsilu_ref[me] = share_s[me]
    lax.fori_loop(1, count, do_wait, 0)
    sums.delivered()
    gin_done()
    sems.drain()


FINISH_SPANS = 4


def finish_call(row, ada, silu_rows, hot, gin, qkv):
    sizes = sizes_of()
    near = sizes["c"]
    count = 8 * near * sizes["y"]
    anywhere = pl.BlockSpec(memory_space=pl.ANY)
    vmem = pl.BlockSpec(memory_space=pltpu.VMEM)
    needed = sems_needed(sizes, 2 + FINISH_SPANS, 2 * sizes["y"] + 4 * near)
    return pl.pallas_call(
        finish_kernel,
        in_specs=[anywhere, vmem, vmem, vmem] + [anywhere] * 2,
        out_specs=[vmem] * 3 + [anywhere] * 2,
        out_shape=[
            jax.ShapeDtypeStruct(row.shape, f32),
            jax.ShapeDtypeStruct(ada.shape, f32),
            jax.ShapeDtypeStruct((count, 1, 128), f32),
            jax.ShapeDtypeStruct(gin.shape, bf16),
            final_shape(qkv, near),
        ],
        scratch_shapes=[
            pltpu.SemaphoreType.DMA((needed,)),
            pltpu.SemaphoreType.DMA((needed,)),
            pltpu.SemaphoreType.DMA((count,)),
            pltpu.SemaphoreType.DMA((count,)),
            pltpu.VMEM((4, 2, near, sizes["y"], 1, row.shape[1]), f32),
            pltpu.VMEM((count, 1, 128), f32),
        ]
        + sum_scratch(
            sizes,
            [qkv.shape[4:] + (False, FINISH_SPANS)],
            FINISH_ORDERS,
        ),
        compiler_params=pltpu.CompilerParams(
            collective_id=1, has_side_effects=True, vmem_limit_bytes=VMEM_MOST
        ),
        name="sum_finish",
    )(row, ada, silu_rows, hot, gin, qkv)


BACK_SPANS = (4, 4, 2)
BACK_STEPS = (1, 2, 4, 7, 10, 13, 99, 99)


def attn_back_kernel(
    ts, kind_ref, q_ref, k_ref, v_ref, g_ref, lse_ref, act_p, up_p, down_p, out_p,
    out_ref, act_f, dup_ref, ddown_ref, dout_ref, dk_s, dv_s, send, recv, *scratch,
):
    step = pl.program_id(0)
    last = pl.num_programs(0) - 1
    place = Place()
    sems = Sems(send, recv)
    sums = Sums(
        place, sems, list(zip((up_p, down_p, out_p), BACK_SPANS)), (dup_ref, ddown_ref, dout_ref),
        scratch, BACK_ORDERS,
    )
    act_move = Exchange(place, sems, act_p, act_f)

    @pl.when(step == 0)
    def _():
        greet(place)

    for tick in range(sums.ticks):
        if BACK_STEPS[tick] < H - 1:
            @pl.when(step == BACK_STEPS[tick])
            def _(tick=tick):
                if tick == 0:
                    met(place)
                sums.advance(tick)
                if tick == 2:
                    act_move.start()

    slots, size = q_ref.shape[1:]
    kept = slots - slots // 16
    scale = size ** (-0.5)
    factor = log2_e * scale
    full = kind_ref[0] == 0
    keys = k_ref[0]
    keys_t = keys.T
    values = v_ref[0]
    for start in range(0, slots, ts):
        here = slice(start, start + ts)
        queries = q_ref[0, here, :]
        grad = g_ref[0, here, :]
        scores = masked(mm_nt(keys, queries), full, kept)
        probs = jnp.exp2(scores * factor - lse_ref[0, :, here])
        weighted = probs * mm_nt(values, grad)
        inner = jnp.sum(weighted, axis=0, keepdims=True)
        grad_scores = (weighted - probs * inner).astype(bf16)
        add_v = mm(probs.astype(bf16), grad)
        add_k = mm(grad_scores, queries)
        if start == 0:
            dv_s[...] = add_v
            dk_s[...] = add_k
        else:
            dv_s[...] += add_v
            dk_s[...] += add_k
        out_ref[0, 0, here, :] = (mm(keys_t, grad_scores) * scale).T.astype(bf16)
    out_ref[1, 0] = (dk_s[...] * scale).astype(bf16)
    out_ref[2, 0] = dv_s[...].astype(bf16)

    @pl.when(step == last)
    def _():
        for tick in range(sums.ticks):
            if BACK_STEPS[tick] >= H - 1:
                sums.advance(tick)
        sums.advance(sums.ticks)
        sums.deliver()
        sums.delivered()
        act_move.finish()
        sems.drain()


def attn_back_call(kind, qkv, grad, lse, act, up, down, out):
    _, slots, size = qkv.shape
    ts = min(256, slots)
    block = (1, slots, size)
    sizes = sizes_of()
    anywhere = pl.BlockSpec(memory_space=pl.ANY)
    needed = sems_needed(sizes, sum(BACK_SPANS), 2 * sizes["y"] + 4 * sizes["c"])
    return pl.pallas_call(
        functools.partial(attn_back_kernel, ts),
        grid=(H,),
        in_specs=[
            pl.BlockSpec(memory_space=pltpu.SMEM),
            pl.BlockSpec(block, lambda h: (h, 0, 0)),
            pl.BlockSpec(block, lambda h: (h + H, 0, 0)),
            pl.BlockSpec(block, lambda h: (h + 2 * H, 0, 0)),
            pl.BlockSpec(block, lambda h: (h, 0, 0)),
            pl.BlockSpec((1, 1, slots), lambda h: (h, 0, 0)),
        ]
        + [anywhere] * 4,
        out_specs=[pl.BlockSpec((3, 1, slots, size), lambda h: (0, h, 0, 0))] + [anywhere] * 4,
        out_shape=[
            jax.ShapeDtypeStruct((3, H, slots, size), bf16),
            jax.ShapeDtypeStruct(act.shape, bf16),
            final_shape(up, sizes["c"]),
            jax.ShapeDtypeStruct(down.shape[4:], f32),
            final_shape(out, sizes["c"]),
        ],
        scratch_shapes=[
            pltpu.VMEM((slots, size), f32),
            pltpu.VMEM((slots, size), f32),
            pltpu.SemaphoreType.DMA((needed,)),
            pltpu.SemaphoreType.DMA((needed,)),
        ]
        + sum_scratch(
            sizes,
            [
                grad.shape[4:] + (at == 1, count)
                for at, (grad, count) in enumerate(zip((up, down, out), BACK_SPANS))
            ],
            BACK_ORDERS,
        ),
        compiler_params=pltpu.CompilerParams(
            collective_id=2, has_side_effects=True, vmem_limit_bytes=VMEM_MOST
        ),
        name="attention_backward",
    )(kind, qkv, qkv, qkv, grad, lse, act, up, down, out)


MLP_SPANS = 4
MLP_GATHER = (1, 2, 3, 5, 7, 9, 11)
MLP_SUM = (12, 13, 15, 17, 19, 21, 22)


def mlp_kernel(
    tiles, second_ref, gm_ref, up0_f, down0_f, up1_p, down1_p, b_ref,
    mlp_ref, gsec_ref, bias_ref, up1_f, down1_f, dup0_ref, ddown0_ref, dup1_ref, ddown1_ref,
    sup_ref, sdown_ref,
    sec_t, act_t, gh_s, up_s, down_s, raw_up, raw_down, loaded, stored,
    send, recv, *scratch,
):
    step = pl.program_id(0)
    subs = tiles + 2
    last = 4 * subs - 1
    tile_at = lax.div(step, subs)
    sub = lax.rem(step, subs)
    slots, width = second_ref.shape
    hidden = up_s.shape[1]
    tm = slots // tiles

    place = Place()
    sems = Sems(send, recv)
    near, head_half = place.size["c"], place.size["y"] // 2

    def loads(tile):
        half = tile % 2
        up, down = ((up0_f, down0_f), (up1_f, down1_f))[tile // 2]
        return (
            pltpu.make_async_copy(
                up.at[:, :, :, pl.ds(half * head_half, head_half)], raw_up, loaded.at[0]
            ),
            pltpu.make_async_copy(down.at[pl.ds(2 * half, 2)], raw_down, loaded.at[1]),
        )

    def stores(tile):
        half = tile % 2
        up, down = ((dup0_ref, ddown0_ref), (dup1_ref, ddown1_ref))[tile // 2]
        return (
            pltpu.make_async_copy(
                raw_up, up.at[:, :, :, pl.ds(half * head_half, head_half)], stored.at[0]
            ),
            pltpu.make_async_copy(raw_down, down.at[pl.ds(2 * half, 2)], stored.at[1]),
        )

    wanted = []
    for piece, full in ((up1_p, up1_f), (down1_p, down1_f)):
        wanted += [(piece, full, span) for span in spans_of(piece.shape[0], MLP_SPANS)]
    gathers = Gathers(place, sems, wanted, MLP_ORDERS)
    sums = Sums(
        place, sems, [(dup0_ref, MLP_SPANS), (ddown0_ref, MLP_SPANS)], (sup_ref, sdown_ref), scratch,
        MLP_SUM_ORDERS,
    )

    @pl.when(step == 0)
    def _():
        greet(place)

    for tick in range(gathers.ticks):
        @pl.when(step == MLP_GATHER[tick])
        def _(tick=tick):
            if tick == 0:
                met(place)
            gathers.advance(tick)

    @pl.when(step == 2 * subs)
    def _():
        gathers.advance(gathers.ticks)

    @pl.when(step == 0)
    def _():
        sec_t[...] = second_ref[...].T
        mlp_ref[...] = jnp.zeros_like(mlp_ref)
        gsec_ref[...] = jnp.zeros_like(gsec_ref)
        for made in loads(0):
            made.start()

    for tile in range(4):
        @pl.when(step == tile * subs)
        def _(tile=tile):
            if tile > 0:
                stores(tile - 1)[1].wait()
                loads(tile)[1].start()
            if tile == 2:
                loads(tile)[0].start()
            for made in loads(tile):
                made.wait()

    @pl.when(sub == 0)
    def _():
        share = raw_up.shape[5]
        for y in range(raw_up.shape[3]):
            for c in range(near):
                off = (y * near + c) * share
                up_s[:, off : off + share] = raw_up[:, :, c, y].reshape(width, share)
        chunk, share = raw_down.shape[4:]
        for at in range(4 * near):
            for y in range(raw_down.shape[3]):
                down_s[at * chunk : (at + 1) * chunk, y * share : (y + 1) * share] = raw_down[
                    at // (2 * near), (at // near) % 2, at % near, y
                ]
        bias_ref[...] = jnp.zeros_like(bias_ref)

    for tick in range(sums.ticks):
        if MLP_SUM[tick] < last:
            @pl.when(step == MLP_SUM[tick])
            def _(tick=tick):
                sums.advance(tick)

    @pl.when(sub < tiles)
    def _():
        rows = pl.ds(pl.multiple_of(sub * tm, tm), tm)
        pre = mm(second_ref[rows, :], up_s[...]) + b_ref[0]
        square = pre * pre
        tanh = jnp.tanh(gelu_in * (pre + gelu_cube * pre * square))
        act = (0.5 * pre * (1.0 + tanh)).astype(bf16)
        slope = 0.5 * (1.0 + tanh) + 0.5 * pre * (1.0 - tanh * tanh) * (
            gelu_in * (1.0 + 3.0 * gelu_cube * square)
        )
        grad = mm_nt(gm_ref[rows, :], down_s[...]) * slope
        bias_ref[0] += jnp.sum(grad, axis=0, keepdims=True)
        grad_low = grad.astype(bf16)
        gh_s[rows, :] = grad_low
        act_t[:, rows] = act.T
        mlp_ref[rows, :] += mm(act, down_s[...])
        gsec_ref[rows, :] += mm_nt(grad_low, up_s[...])

    @pl.when(sub == tiles)
    def _():
        share = raw_up.shape[5]
        half = width // 2
        for j in range(2):
            grad = mm(sec_t[j * half : (j + 1) * half, :], gh_s[...]).astype(bf16)
            for y in range(raw_up.shape[3]):
                for c in range(near):
                    off = (y * near + c) * share
                    raw_up[2 * j : 2 * j + 2, :, c, y] = grad[:, off : off + share].reshape(
                        2, 2, half // 4, share
                    )

    @pl.when(sub == tiles + 1)
    def _():
        chunk, share = raw_down.shape[4:]
        half = hidden // 2
        for j in range(2):
            grad = mm(act_t[j * half : (j + 1) * half, :], gm_ref[...]).astype(bf16)
            for at in range(2 * near):
                for y in range(raw_down.shape[3]):
                    raw_down[j, at // near, at % near, y] = grad[
                        at * chunk : (at + 1) * chunk, y * share : (y + 1) * share
                    ]

    for tile in range(4):
        @pl.when(step == tile * subs + tiles)
        def _(tile=tile):
            stores(tile)[0].start()

        @pl.when(step == tile * subs + tiles + 1)
        def _(tile=tile):
            stores(tile)[0].wait()
            if tile in (0, 2):
                loads(tile + 1)[0].start()
            stores(tile)[1].start()

    @pl.when(step == last)
    def _():
        stores(3)[1].wait()
        for tick in range(sums.ticks):
            if MLP_SUM[tick] >= last:
                sums.advance(tick)
        sums.advance(sums.ticks)
        sums.deliver()
        sums.delivered()
        sems.drain()


def mlp_call(second, gm, up0, down0, up1, down1, bias):
    slots, width = second.shape
    tiles = 4
    subs = tiles + 2
    sizes = sizes_of()
    near, head = sizes["c"], sizes["y"]
    lead = tuple(sizes[a] for a in AXES)
    rows_up, share_up = up1.shape
    rows_down, share_down = down1.shape
    hidden = share_up * near * head // 2
    anywhere = pl.BlockSpec(memory_space=pl.ANY)
    needed = sems_needed(sizes, 4 * MLP_SPANS, 4 * near)
    bias_spec = pl.BlockSpec((1, 1, hidden), lambda s: (lax.div(s, subs), 0, 0))
    full_up = jax.ShapeDtypeStruct(lead + up1.shape, bf16)
    full_down = jax.ShapeDtypeStruct(lead + down1.shape, bf16)
    return pl.pallas_call(
        functools.partial(mlp_kernel, tiles),
        grid=(4 * subs,),
        in_specs=[once_spec((slots, width)), once_spec((slots, width))]
        + [anywhere] * 4
        + [bias_spec],
        out_specs=[once_spec((slots, width)), once_spec((slots, width)), bias_spec] + [anywhere] * 8,
        out_shape=[
            jax.ShapeDtypeStruct((slots, width), f32),
            jax.ShapeDtypeStruct((slots, width), f32),
            jax.ShapeDtypeStruct(bias.shape, f32),
            full_up, full_down, full_up, full_down, full_up, full_down,
            final_shape(full_up, near),
            jax.ShapeDtypeStruct(down1.shape, f32),
        ],
        scratch_shapes=[
            pltpu.VMEM((width, slots), bf16),
            pltpu.VMEM((hidden, slots), bf16),
            pltpu.VMEM((slots, hidden), bf16),
            pltpu.VMEM((width, hidden), bf16),
            pltpu.VMEM((hidden, width), bf16),
            pltpu.VMEM((4, 2, near, head // 2) + up1.shape, bf16),
            pltpu.VMEM((2, 2, near, head) + down1.shape, bf16),
            pltpu.SemaphoreType.DMA((2,)),
            pltpu.SemaphoreType.DMA((2,)),
            pltpu.SemaphoreType.DMA((needed,)),
            pltpu.SemaphoreType.DMA((needed,)),
        ]
        + sum_scratch(
            sizes, (up1.shape + (False, MLP_SPANS), down1.shape + (True, MLP_SPANS)), MLP_SUM_ORDERS
        ),
        compiler_params=pltpu.CompilerParams(
            collective_id=4, has_side_effects=True, vmem_limit_bytes=MLP_VMEM
        ),
        name="feed_forward_both_ways",
    )(second, gm, up0, down0, up1, down1, bias)


MLP_VMEM = 63 * 1024 * 1024


def qkv_back_kernel(
    tm, g_ref, norm_ref, w_ref, x_ref, gmid_ref, mod_ref,
    gin_ref, dw_ref, bias_ref, sums_ref, norm_t, gp_s, gn_s,
):
    part = pl.program_id(0)
    slots, width = x_ref.shape
    tiles = slots // tm
    groups, _, rows_each, part_width = w_ref.shape
    heads = g_ref.shape[0]

    @pl.when(part == 0)
    def _():
        norm_t[...] = norm_ref[...].T
        gn_s[...] = jnp.zeros_like(gn_s)

    def tile(i, total):
        rows = pl.ds(pl.multiple_of(i * tm, tm), tm)
        grad = jnp.concatenate([g_ref[j, rows, :] for j in range(heads)], axis=1)
        gp_s[rows, :] = grad
        gn_s[rows, :] += mm_nt(grad, w_ref[...].reshape(width, part_width))
        return total + jnp.sum(grad.astype(f32), axis=0, keepdims=True)

    bias_ref[0] = lax.fori_loop(0, tiles, tile, jnp.zeros((1, part_width), f32))
    per = groups // 2
    for j in range(2):
        dw_ref[per * j : per * (j + 1), 0] = (
            mm(norm_t[per * j * rows_each : per * (j + 1) * rows_each, :], gp_s[...])
            .astype(bf16)
            .reshape(per, rows_each, part_width)
        )

    @pl.when(part == pl.num_programs(0) - 1)
    def _():
        def finish(i, sums):
            rows = pl.ds(pl.multiple_of(i * tm, tm), tm)
            center, inv = center_spread(x_ref[rows, :].astype(f32))
            unit = center * inv
            grad = gn_s[rows, :]
            gin_ref[rows, :] = (
                gmid_ref[rows, :] + norm_back(grad * (1.0 + mod_ref[1:2, :]), unit, inv)
            ).astype(gin_ref.dtype)
            return (
                sums[0] + jnp.sum(grad, axis=0, keepdims=True),
                sums[1] + jnp.sum(grad * unit, axis=0, keepdims=True),
            )

        zero = jnp.zeros((1, width), f32)
        shift, scale = lax.fori_loop(0, tiles, finish, (zero, zero))
        sums_ref[...] = jnp.zeros_like(sums_ref)
        sums_ref[0:1, :] = shift
        sums_ref[1:2, :] = scale


def qkv_back_call(grad, norm, weight, x, gmid, mod):
    slots, width = x.shape
    tm = min(256, slots)
    size = width // H
    groups, parts, rows_each, part_width = weight.shape
    heads = part_width // size
    w_spec = pl.BlockSpec((groups, 1, rows_each, part_width), lambda p: (0, place(p), 0, 0))
    return pl.pallas_call(
        functools.partial(qkv_back_kernel, tm),
        grid=(parts,),
        in_specs=[
            pl.BlockSpec((heads, slots, size), lambda p: (p, 0, 0)),
            once_spec((slots, width)),
            w_spec,
            once_spec((slots, width)),
            once_spec((slots, width)),
            whole_spec(mod.shape),
        ],
        out_specs=[
            once_spec((slots, width)),
            w_spec,
            pl.BlockSpec((1, 1, part_width), lambda p: (p, 0, 0)),
            whole_spec((8, width)),
        ],
        out_shape=[
            jax.ShapeDtypeStruct((slots, width), bf16),
            jax.ShapeDtypeStruct(weight.shape, bf16),
            jax.ShapeDtypeStruct((parts, 1, part_width), f32),
            jax.ShapeDtypeStruct((8, width), f32),
        ],
        scratch_shapes=[
            pltpu.VMEM((width, slots), bf16),
            pltpu.VMEM((slots, part_width), bf16),
            pltpu.VMEM((slots, width), f32),
        ],
        compiler_params=params(),
        name="qkv_backward",
    )(grad, norm, weight, x, gmid, mod)


class Wire:
    def __init__(self, width):
        self.dp = lax.axis_size("dp")
        self.head = lax.axis_size("head")
        self.near = self.dp // (width // 144)
        self.width = width
        self.groups = [
            list(range(first, first + self.near)) for first in range(0, self.dp, self.near)
        ]

    def piece(self, weight):
        return lax.all_to_all(
            weight.astype(bf16), "dp", split_axis=1, concat_axis=0,
            axis_index_groups=self.groups, tiled=True,
        )

    def columns(self, stack):
        devices, rows, cols = stack.shape
        stack = stack.reshape(self.dp // self.near, self.near, self.head, rows, cols)
        if (self.near, self.head) != (2, 2):
            quarter = self.near * self.head * cols // 4
            stack = stack.transpose(0, 3, 2, 1, 4).reshape(-1, rows, 2, 2, quarter)
            stack = stack.transpose(0, 3, 2, 1, 4)
            return stack.reshape(-1, 4, rows, quarter)
        return stack.reshape(-1, 4, rows, cols)

    def uncolumns(self, stack):
        groups, _, rows, quarter = stack.shape
        cols = 4 * quarter // (self.near * self.head)
        if (self.near, self.head) != (2, 2):
            stack = stack.reshape(groups, 2, 2, rows, quarter).transpose(0, 3, 2, 1, 4)
            stack = stack.reshape(groups, rows, self.head, self.near, cols)
            stack = stack.transpose(0, 3, 2, 1, 4)
        return stack.reshape(self.dp * self.head, rows, cols)


def body(
    inputs, cond, order, grid_kind, weight_ada, bias_ada, weight_qkv, bias_query, bias_value,
    weight_out, bias_out, weight_up, bias_up, weight_down, bias_down, cotangent,
):
    images, slot_local, width = inputs.shape
    head_count = lax.axis_size("head")
    dp_count = lax.axis_size("dp")
    head_at = lax.axis_index("head")
    dp_at = lax.axis_index("dp")
    assert images == head_count
    wire = Wire(width)

    def from_image(array):
        return lax.all_to_all(
            array[None], "head", split_axis=1, concat_axis=0, tiled=True
        ).astype(f32)

    rows_ada, cols_ada = weight_ada.shape
    ada_low = weight_ada.astype(bf16)
    silu_own, silu_pull = jax.vjp(lambda v: v * jax.nn.sigmoid(v), cond)
    order_mine = lax.dynamic_slice_in_dim(order, head_at, 1, 0)
    kind = lax.dynamic_slice_in_dim(grid_kind, head_at, 1, 0)
    mod, silu_grouped, hot, x, qkv_full = start_call(
        silu_own, order_mine, ada_low, inputs.astype(bf16), wire.piece(weight_qkv)
    )
    x = x.reshape(-1, width)
    device_stack = lambda full: full.reshape((-1,) + full.shape[4:])
    qkv_full = wire.columns(device_stack(qkv_full))
    mod_flat = mod.reshape(6, width) + bias_ada.reshape(6, width)
    mod = jnp.concatenate([mod_flat, jnp.zeros((2, width), f32)], axis=0)

    bias_qkv = jnp.concatenate([bias_query, jnp.zeros_like(bias_query), bias_value])
    chunk = weight_down.shape[0] // 2
    up_phases = weight_up.astype(bf16).reshape(rows_ada, -1, 2, chunk)
    up0, up1 = (wire.piece(up_phases[:, :, at].reshape(rows_ada, -1)) for at in range(2))
    down0, down1 = (weight_down[at * chunk : (at + 1) * chunk].astype(bf16) for at in range(2))
    bias_phases = bias_up.reshape(-1, 2, chunk).swapaxes(0, 1).reshape(4, 1, -1)
    qkv, norm, mix, lse, out_full, up_full, down_full, cot = front_call(
        kind, x, mod, qkv_full, bias_qkv.reshape(4, 1, -1),
        wire.piece(weight_out), up0, down0, cotangent.astype(bf16),
    )
    cot = cot.reshape(-1, width)
    out_full = wire.columns(device_stack(out_full))
    attended, branch, second, gm = out_call(mix, x, cot, mod, out_full, bias_out)
    mlp, gsec, d_bias_up, _, _, _, _, d_up1, d_down1, d_up0, d_down0 = mlp_call(
        second, gm, up_full, down_full, up1, down1, bias_phases
    )
    d_bias_up = d_bias_up.reshape(2, -1, chunk).swapaxes(0, 1)
    act, gmid, gatt, d_out, sums = mid_back_call(
        x, branch, mlp, gsec, cot, attended, mod, out_full, bias_down
    )
    lead = (4, 2, dp_count // 8, head_count)
    stack = lambda grad: grad.reshape(lead + grad.shape[1:])
    by_image = lambda array: array.reshape(head_count, slot_local, width)
    grad, act, d_up1, d_down1, d_out = attn_back_call(
        kind, qkv, gatt, lse, by_image(act), d_up1, d_down1, stack(wire.uncolumns(d_out))
    )
    gin, d_qkv, d_bias_qkv, sums_in = qkv_back_call(
        grad.reshape(qkv.shape), norm, qkv_full, x, gmid, mod
    )

    bias_qkv_sum = d_bias_qkv.reshape(3, width)
    row = jnp.concatenate(
        [sums_in[0], sums_in[1], sums[0], sums[1], sums[2], sums[3],
         bias_qkv_sum[0], bias_qkv_sum[2], sums[4], sums[5], d_bias_up.reshape(-1)]
    ).reshape(1, -1)
    biases, d_ada, g_silu, gin, d_qkv = finish_call(
        row, ada_low, silu_grouped, hot, by_image(gin), stack(wire.uncolumns(d_qkv))
    )
    biases = biases[0]
    g_silu = g_silu.reshape(dp_count, head_count, 128)[:, :, :rows_ada].sum(axis=1)
    d_cond = silu_pull(g_silu.reshape(1, width))[0]
    side = lambda grad: grad.transpose(1, 0, 2).reshape(grad.shape[1], -1)
    d_up = jnp.stack(
        [side(part).reshape(rows_ada, -1, chunk) for part in (d_up0, d_up1)], axis=2
    ).reshape(rows_ada, -1)
    d_down = jnp.concatenate([d_down0, d_down1], axis=0)
    mods = 6 * width
    return (
        act.astype(f32),
        gin.astype(f32),
        d_cond,
        d_ada,
        side(d_qkv),
        side(d_out),
        d_up,
        d_down,
        biases[:mods],
        biases[mods : mods + width],
        biases[mods + width : mods + 2 * width],
        biases[mods + 2 * width : mods + 3 * width],
        biases[mods + 4 * width :],
        biases[mods + 3 * width : mods + 4 * width],
    )


def solution(mesh):
    in_specs = (
        P("dp", "head", None), P(("dp", "head"), None), P("dp"), P("dp"), P("dp", "head"), P(),
        P("dp", "head"), P(), P(), P("dp", "head"), P(), P("dp", "head"), P(), P("dp", "head"),
        P(), P("dp", "head", None),
    )
    out_specs = (
        P("dp", "head", None), P("dp", "head", None), P(("dp", "head"), None), P("dp", "head"),
        P("dp", "head"), P("dp", "head"), P("dp", "head"), P("dp", "head"),
        P(), P(), P(), P(), P(), P(),
    )
    return jax.shard_map(body, mesh=mesh, in_specs=in_specs, out_specs=out_specs, check_vma=False)
```

```python
import functools
import math

import jax
import jax.numpy as jnp
from jax import lax
from jax.experimental import pallas as pl
from jax.experimental.pallas import tpu as pltpu
from jax.sharding import PartitionSpec as P

H = 16
norm_eps = 1e-06
log2_e = 1.4426950408889634
gelu_in = 0.7978845608028654
gelu_cube = 0.044715
f32 = jnp.float32
bf16 = jnp.bfloat16
VMEM_MOST = 60 * 1024 * 1024


def mm(left, right):
    return jnp.dot(left, right, preferred_element_type=f32)


def mm_nt(left, right):
    return lax.dot_general(left, right, (((1,), (1,)), ((), ())), preferred_element_type=f32)


def center_spread(values):
    center = values - jnp.mean(values, axis=-1, keepdims=True)
    spread = jnp.mean(center * center, axis=-1, keepdims=True)
    return center, lax.rsqrt(spread + norm_eps)


def norm_back(grad, unit, inv):
    return inv * (
        grad
        - jnp.mean(grad, axis=-1, keepdims=True)
        - unit * jnp.mean(grad * unit, axis=-1, keepdims=True)
    )


def whole_spec(shape):
    zeros = (0,) * len(shape)
    return pl.BlockSpec(shape, lambda *_: zeros)


def once_spec(shape):
    zeros = (0,) * len(shape)
    return pl.BlockSpec(shape, lambda *_: zeros, pipeline_mode=pl.Buffered(1))


def params(most=VMEM_MOST):
    return pltpu.CompilerParams(vmem_limit_bytes=most)


def place(quarter):
    return (quarter % 2) * 2 + quarter // 2


def masked(scores, full, kept):
    return jnp.concatenate(
        [scores[:kept], jnp.where(full, scores[kept:], -1e30)], axis=0
    )


def columns_of(w_ref):
    groups, parts, rows_each, width = w_ref.shape
    return jnp.concatenate(
        [w_ref[:, place(n)].reshape(groups * rows_each, width) for n in range(parts)], axis=1
    )


def out_kernel(
    o_ref, x_ref, cot_ref, mod_ref, w_ref, b_ref, att_ref, branch_ref, second_ref, gm_ref, w_s
):
    @pl.when(pl.program_id(0) == 0)
    def _():
        w_s[...] = columns_of(w_ref)

    attended = jnp.concatenate([o_ref[j] for j in range(o_ref.shape[0])], axis=1)
    att_ref[...] = attended
    branch = mm(attended, w_s[...]) + b_ref[...]
    branch_ref[...] = branch.astype(bf16)
    middle = x_ref[...].astype(f32) + mod_ref[2:3, :] * branch
    center, inv = center_spread(middle)
    second_ref[...] = (center * inv * (1.0 + mod_ref[4:5, :]) + mod_ref[3:4, :]).astype(bf16)
    gm_ref[...] = (cot_ref[...].astype(f32) * mod_ref[5:6, :]).astype(bf16)


def out_call(mix, x, cot, mod, weight, bias):
    slots, width = x.shape
    tm = min(256, slots)
    size = width // H
    tile = pl.BlockSpec((tm, width), lambda i: (i, 0))
    return pl.pallas_call(
        out_kernel,
        grid=(slots // tm,),
        in_specs=[
            pl.BlockSpec((H, tm, size), lambda i: (0, i, 0)),
            tile,
            tile,
            whole_spec(mod.shape),
            whole_spec(weight.shape),
            whole_spec((1, width)),
        ],
        out_specs=[tile] * 4,
        out_shape=[jax.ShapeDtypeStruct((slots, width), bf16)] * 4,
        scratch_shapes=[pltpu.VMEM((width, width), bf16)],
        compiler_params=params(),
        name="out_projection",
    )(mix, x, cot, mod, weight, bias.reshape(1, width))


def mid_back_kernel(
    x_ref, branch_ref, mlp_ref, gsec_ref, cot_ref, att_ref, mod_ref, w_ref, b_ref,
    act_ref, gmid_ref, gatt_ref, dw_ref, sums_ref, w_s, dw_s,
):
    step = pl.program_id(0)

    @pl.when(step == 0)
    def _():
        w_s[...] = columns_of(w_ref)
        sums_ref[...] = jnp.zeros_like(sums_ref)
        dw_s[...] = jnp.zeros_like(dw_s)

    gate_a = mod_ref[2:3, :]
    gate_m = mod_ref[5:6, :]
    branch = branch_ref[...].astype(f32)
    middle = x_ref[...].astype(f32) + gate_a * branch
    mlp = mlp_ref[...] + b_ref[...]
    cot = cot_ref[...].astype(f32)
    act_ref[...] = (middle + gate_m * mlp).astype(act_ref.dtype)
    center, inv = center_spread(middle)
    unit = center * inv
    grad = gsec_ref[...]
    grad_mid = cot + norm_back(grad * (1.0 + mod_ref[4:5, :]), unit, inv)
    gmid_ref[...] = grad_mid
    grad_branch = gate_a * grad_mid

    def add(row, value):
        sums_ref[row : row + 1, :] += jnp.sum(value, axis=0, keepdims=True)

    add(0, grad_mid * branch)
    add(1, grad)
    add(2, grad * unit)
    add(3, cot * mlp)
    add(4, grad_branch)
    add(5, gate_m * cot)
    grad_low = grad_branch.astype(bf16)
    grad_att = mm_nt(grad_low, w_s[...]).astype(bf16)
    size = gatt_ref.shape[2]
    for j in range(gatt_ref.shape[0]):
        gatt_ref[j] = grad_att[:, j * size : (j + 1) * size]
    dw_s[...] += mm(att_ref[...].T, grad_low)

    @pl.when(step == pl.num_programs(0) - 1)
    def _():
        groups, parts, rows_each, width = dw_ref.shape
        low = dw_s[...].astype(bf16)
        for n in range(parts):
            dw_ref[:, place(n)] = low[:, n * width : (n + 1) * width].reshape(
                groups, rows_each, width
            )


def mid_back_call(x, branch, mlp, gsec, cot, attended, mod, weight, bias_down):
    slots, width = x.shape
    tm = min(256, slots)
    size = width // H
    tile = pl.BlockSpec((tm, width), lambda i: (i, 0))
    return pl.pallas_call(
        mid_back_kernel,
        grid=(slots // tm,),
        in_specs=[tile] * 6 + [whole_spec(mod.shape), whole_spec(weight.shape), whole_spec((1, width))],
        out_specs=[
            tile,
            tile,
            pl.BlockSpec((H, tm, size), lambda i: (0, i, 0)),
            whole_spec(weight.shape),
            whole_spec((8, width)),
        ],
        out_shape=[
            jax.ShapeDtypeStruct((slots, width), bf16),
            jax.ShapeDtypeStruct((slots, width), f32),
            jax.ShapeDtypeStruct((H, slots, size), bf16),
            jax.ShapeDtypeStruct(weight.shape, bf16),
            jax.ShapeDtypeStruct((8, width), f32),
        ],
        scratch_shapes=[pltpu.VMEM((width, width), bf16), pltpu.VMEM((width, width), f32)],
        compiler_params=params(),
        name="middle_backward",
    )(x, branch, mlp, gsec, cot, attended, mod, weight, bias_down.reshape(1, width))


MESH = pl.DeviceIdType.MESH


class Place:
    def __init__(self):
        self.dp = lax.axis_size("dp")
        head = lax.axis_size("head")
        near = self.dp // 8
        at = lax.axis_index("dp")
        self.size = {"z": 4, "x": 2, "c": near, "y": head}
        self.at = {
            "z": lax.div(at, 2 * near),
            "x": lax.rem(lax.div(at, near), 2),
            "c": lax.rem(at, near),
            "y": lax.axis_index("head"),
        }
        self.count = self.dp * head
        self.me = at * head + self.at["y"]

    def device(self, axis, index):
        spot = dict(self.at)
        spot[axis] = index
        return ((spot["z"] * 2 + spot["x"]) * self.size["c"] + spot["c"], spot["y"])

    def numbered(self, index):
        head = self.size["y"]
        return (lax.div(index, head), lax.rem(index, head))

    def after(self, axis, step):
        return lax.rem(self.at[axis] + step, self.size[axis])

    def before(self, axis, step):
        return lax.rem(self.at[axis] + self.size[axis] - step, self.size[axis])


class Local:
    def __init__(self, sem, ends):
        self.sem, self.ends = sem, ends

    def made(self):
        return pltpu.make_async_copy(*self.ends(), self.sem())

    def wait(self):
        self.made().wait()


class Sems:
    def __init__(self, send, recv):
        self.send, self.recv, self.used = send, recv, 0
        self.sent = []

    def describe(self, at, src, dst, device):
        return pltpu.make_async_remote_copy(
            src_ref=src, dst_ref=dst, send_sem=self.send.at[at], recv_sem=self.recv.at[at],
            device_id=device, device_id_type=MESH,
        )

    def copy(self, ends):
        at = self.used
        self.used += 1
        self.describe(at, *ends()).start()
        self.sent.append((at, ends))
        return at

    def arrived(self, at, dst, device):
        self.describe(at, dst, dst, device).wait_recv()

    def local(self, ends):
        at = self.used
        self.used += 1
        made = Local(lambda: self.send.at[at], ends)
        made.made().start()
        return made

    def drain(self):
        for at, ends in self.sent:
            self.describe(at, *ends()).wait_send()


AXES = "zxcy"


def spans_of(rows, count):
    cuts = [16 * (rows // 16 * at // count) for at in range(count)] + [rows]
    return [(low, high - low) for low, high in zip(cuts, cuts[1:])]


def halves(rows):
    return spans_of(rows, 2)


class Gather:
    def __init__(self, place, sems, piece, full, axes, rows=None):
        self.place, self.sems, self.piece, self.full, self.axes = place, sems, piece, full, axes
        self.rows = rows
        self.slots = {}

    def part(self, got, axis=None, index=None):
        spot = dict(self.place.at)
        if axis is not None:
            spot[axis] = index
        spots = tuple(slice(None) if name in got else spot[name] for name in AXES)
        if self.rows is not None:
            spots = spots + (pl.ds(*self.rows), slice(None))
        return self.full.at[spots]

    def first(self):
        return self.piece if self.rows is None else self.piece.at[pl.ds(*self.rows)]

    def own(self):
        self.kept = self.sems.local(lambda: (self.first(), self.part("")))

    def start(self, stage):
        axis = self.axes[stage]
        got = self.axes[:stage]
        if stage == 1:
            self.kept.wait()

        def ends(step):
            return (
                self.first() if stage == 0 else self.part(got),
                self.part(got),
                self.place.device(axis, self.place.after(axis, step)),
            )

        for step in range(1, self.place.size[axis]):
            self.slots[stage, step] = self.sems.copy(functools.partial(ends, step))

    def wait(self, stage):
        axis = self.axes[stage]
        got = self.axes[:stage]
        for step in range(1, self.place.size[axis]):
            index = self.place.before(axis, step)
            self.sems.arrived(
                self.slots[stage, step], self.part(got, axis, index), self.place.device(axis, index)
            )


EVEN = ("zxyc", "zyxc")
WIDE = ("zyxc", "yzxc")


AHEAD = 2


def fresh(pairs, tick):
    return pairs[:AHEAD] if tick == 0 else pairs[tick + AHEAD - 1 : tick + AHEAD]


class Gathers:
    def __init__(self, place, sems, spans, orders):
        self.pairs = []
        for at in range(0, len(spans), 2):
            pair = orders[at // 2 % len(orders)]
            self.pairs.append(
                [
                    Gather(place, sems, piece, full, axes, rows)
                    for (piece, full, rows), axes in zip(spans[at : at + 2], pair)
                ]
            )
        self.ticks = len(self.pairs) + 3

    def advance(self, tick):
        for pair in fresh(self.pairs, tick):
            for unit in pair:
                unit.own()
                unit.start(0)
        for stage in (1, 0, 2, 3):
            if 0 <= tick - 1 - stage < len(self.pairs):
                for unit in self.pairs[tick - 1 - stage]:
                    unit.wait(stage)
                    if stage < 3:
                        unit.start(stage + 1)


def greet_all(place):
    barrier = pltpu.get_barrier_semaphore()

    def one(step, carry):
        pl.semaphore_signal(
            barrier, inc=1, device_id=place.numbered(lax.rem(place.me + step, place.count)),
            device_id_type=MESH,
        )
        return carry

    lax.fori_loop(1, place.count, one, 0)
    pl.semaphore_wait(barrier, place.count - 1)


def greet(place):
    barrier = pltpu.get_barrier_semaphore()
    for axis in AXES:
        for step in range(1, place.size[axis]):
            pl.semaphore_signal(
                barrier, inc=1, device_id=place.device(axis, place.after(axis, step)),
                device_id_type=MESH,
            )


def met(place):
    pl.semaphore_wait(pltpu.get_barrier_semaphore(), sum(n - 1 for n in place.size.values()))


def sems_needed(sizes, units, pairs):
    return units * (1 + sum(size - 1 for size in sizes.values())) + pairs


class Exchange:
    def __init__(self, place, sems, mine, whole, chunks):
        self.place, self.sems, self.mine, self.whole = place, sems, mine, whole
        self.spans = spans_of(mine.shape[1], chunks)
        self.sent = []

    def start(self, which):
        place = self.place
        at = place.at["y"]
        rows = pl.ds(*self.spans[which])
        if which == 0:
            self.kept = self.sems.local(lambda: (self.mine.at[at], self.whole.at[at]))

        def ends(step):
            other = place.after("y", step)
            return self.mine.at[other, rows], self.whole.at[at, rows], place.device("y", other)

        for step in range(1, place.size["y"]):
            self.sent.append((step, rows, self.sems.copy(functools.partial(ends, step))))

    def finish(self):
        self.kept.wait()
        for step, rows, slot in self.sent:
            index = self.place.before("y", step)
            self.sems.arrived(slot, self.whole.at[index, rows], self.place.device("y", index))


EXCHANGE_CHUNKS = 4


START_ORDERS = (WIDE,)
FRONT_ORDERS = (EVEN,)
MLP_ORDERS = (EVEN,)
MLP_SUM_ORDERS = (EVEN,)
BACK_ORDERS = (EVEN,)
FINISH_ORDERS = (WIDE,)


def start_kernel(
    silu_ref, ada_ref, x_ref, qkv_ref, mod_ref, rows_ref, hot_ref, x_full, qkv_full, silu_s, share_s, terms_s, send, recv, share_send, share_recv,
):
    place = Place()
    sems = Sems(send, recv)
    count, me = place.count, place.me
    width = silu_ref.shape[1] - hot_ref.shape[1]
    rows_each = ada_ref.shape[0]
    greet_all(place)

    silu = Gather(place, sems, silu_ref, silu_s, "czxy")
    gathers = Gathers(place, sems, [(qkv_ref, qkv_full, span) for span in spans_of(qkv_ref.shape[0], 4)], START_ORDERS)
    silu.own()
    silu.start(0)
    gathers.advance(0)
    silu.wait(0)
    silu.start(1)
    silu.wait(1)
    silu.start(2)
    silu.wait(2)
    silu.start(3)
    gathers.advance(1)
    silu.wait(3)

    rows = silu_s[...].reshape(count, silu_ref.shape[1])
    hot = (
        rows[:, width:] == lax.broadcasted_iota(jnp.int32, (count, hot_ref.shape[1]), 1).astype(f32)
    ).astype(bf16)
    hot_ref[...] = hot.astype(f32)
    first = lax.axis_index("dp") * rows_each
    pick = (
        lax.broadcasted_iota(jnp.int32, (width, rows_each), 0)
        == first + lax.broadcasted_iota(jnp.int32, (width, rows_each), 1)
    ).astype(bf16)
    local = mm(rows[:, :width].astype(bf16), pick).astype(bf16)
    grouped = mm(hot[:, :count], local)
    rows_ref[...] = grouped
    share = mm(grouped.astype(bf16), ada_ref[...])
    share_s[...] = share.reshape(share_s.shape)

    def push(step):
        to = lax.rem(me + step, count)
        return pltpu.make_async_remote_copy(
            src_ref=share_s.at[to], dst_ref=terms_s.at[me],
            send_sem=share_send.at[step], recv_sem=share_recv.at[step],
            device_id=place.numbered(to), device_id_type=MESH,
        )

    def came(step):
        source = lax.rem(me + count - step, count)
        return pltpu.make_async_remote_copy(
            src_ref=terms_s.at[source], dst_ref=terms_s.at[source],
            send_sem=share_send.at[step], recv_sem=share_recv.at[step],
            device_id=place.numbered(source), device_id_type=MESH,
        )

    def do_push(step, carry):
        push(step).start()
        return carry

    lax.fori_loop(1, count, do_push, 0)
    terms_s[me] = share_s[me]

    def do_wait(step, carry):
        came(step).wait_recv()
        return carry

    def do_sent(step, carry):
        push(step).wait_send()
        return carry

    x_move = Exchange(place, sems, x_ref, x_full, EXCHANGE_CHUNKS)
    gathers.advance(2)
    for which in range(2):
        x_move.start(which)
    lax.fori_loop(1, count, do_wait, 0)
    heads = place.size["y"]
    for y in range(heads):
        mod_ref[y] = lax.fori_loop(
            0, count // heads, lambda i, total: total + terms_s[i * heads + y],
            jnp.zeros(terms_s.shape[1:], f32),
        )
    for tick in range(3, gathers.ticks + 1):
        gathers.advance(tick)
        if tick < EXCHANGE_CHUNKS + 1:
            x_move.start(tick - 1)
    x_move.finish()
    sems.drain()
    lax.fori_loop(1, count, do_sent, 0)


def start_call(silu, order_mine, ada, x, qkv):
    dp, head = lax.axis_size("dp"), lax.axis_size("head")
    count = dp * head
    lead = (4, 2, dp // 8, head)
    lanes = max(128, count)
    width = silu.shape[1]
    row = jnp.concatenate(
        [silu.astype(bf16).astype(f32), jnp.broadcast_to(order_mine.astype(f32), (1, lanes))], axis=1
    )
    sizes = {"z": 4, "x": 2, "c": dp // 8, "y": head}
    needed = sems_needed(sizes, 5, 1 + EXCHANGE_CHUNKS * head)
    anywhere = pl.BlockSpec(memory_space=pl.ANY)
    vmem = pl.BlockSpec(memory_space=pltpu.VMEM)
    slot_shape = x.shape
    return pl.pallas_call(
        start_kernel,
        in_specs=[anywhere, vmem] + [anywhere] * 2,
        out_specs=[vmem] * 3 + [anywhere] * 2,
        out_shape=[
            jax.ShapeDtypeStruct((head, 1, ada.shape[1]), f32),
            jax.ShapeDtypeStruct((count, ada.shape[0]), f32),
            jax.ShapeDtypeStruct((count, lanes), f32),
            jax.ShapeDtypeStruct(slot_shape, bf16),
            jax.ShapeDtypeStruct(lead + qkv.shape, bf16),
        ],
        scratch_shapes=[
            pltpu.VMEM(lead + (1, width + lanes), f32),
            pltpu.VMEM((count, 1, ada.shape[1]), f32),
            pltpu.VMEM((count, 1, ada.shape[1]), f32),
            pltpu.SemaphoreType.DMA((needed,)),
            pltpu.SemaphoreType.DMA((needed,)),
            pltpu.SemaphoreType.DMA((count,)),
            pltpu.SemaphoreType.DMA((count,)),
        ],
        compiler_params=pltpu.CompilerParams(
            collective_id=0, has_side_effects=True, vmem_limit_bytes=VMEM_MOST
        ),
        name="gather_start",
    )(row, ada, x, qkv)


def front_kernel(
    tiles, ts, kind_ref, x_ref, mod_ref, w_ref, b_ref, out_p, up_p, down_p, cot_p,
    qkv_ref, norm_ref, o_ref, lse_ref, out_f, up_f, down_f, cot_f,
    qkv_s, norm_s, copied, send, recv,
):
    step = pl.program_id(0)
    groups, _, rows_each, width = w_ref.shape
    _, slots, size = qkv_s.shape
    heads = width // size
    parts = 3 * H // heads
    tm = slots // tiles
    first_head = parts * tiles
    last = first_head + H - 1

    place = Place()
    sems = Sems(send, recv)
    wanted = []
    for piece, full, count in ((up_p, up_f, 4), (down_p, down_f, 4), (out_p, out_f, 2)):
        wanted += [(piece, full, span) for span in spans_of(piece.shape[0], count)]
    gathers = Gathers(place, sems, wanted, FRONT_ORDERS)
    keep = pltpu.make_async_copy(qkv_s, qkv_ref, copied.at[0])
    keep_norm = pltpu.make_async_copy(norm_s, norm_ref, copied.at[1])
    cot_move = Exchange(place, sems, cot_p, cot_f, EXCHANGE_CHUNKS)
    for tick in range(gathers.ticks):
        at = min(FRONT_STEPS[tick], last)
        if tick == 0:
            @pl.when(step == 0)
            def _():
                greet(place)

            @pl.when(step == at)
            def _():
                met(place)
                gathers.advance(0)
        elif at < last:
            @pl.when(step == at)
            def _(tick=tick):
                gathers.advance(tick)
                if tick in FRONT_EXCHANGE:
                    cot_move.start(FRONT_EXCHANGE.index(tick))

    @pl.when(step < first_head)
    def _():
        rows = pl.ds(pl.multiple_of(lax.rem(step, tiles) * tm, tm), tm)
        part = lax.div(step, tiles)

        @pl.when(part == 0)
        def _():
            center, inv = center_spread(x_ref[...].astype(f32))
            norm_s[rows, :] = (
                center * inv * (1.0 + mod_ref[1:2, :]) + mod_ref[0:1, :]
            ).astype(bf16)

        weight = w_ref[...].reshape(groups * rows_each, width)
        out = (mm(norm_s[rows, :], weight) + b_ref[0]).astype(bf16)
        for j in range(heads):
            qkv_s[part * heads + j, rows, :] = out[:, j * size : (j + 1) * size]

    @pl.when(step == first_head)
    def _():
        keep.start()
        keep_norm.start()

    @pl.when(step >= first_head)
    def _():
        head = step - first_head
        kept = slots - slots // 16
        factor = log2_e * size ** (-0.5)
        full = kind_ref[0] == 0
        keys = qkv_s[H + head]
        values_t = qkv_s[2 * H + head].T
        for start in range(0, slots, ts):
            here = slice(start, start + ts)
            scores = masked(mm_nt(keys, qkv_s[head, here, :]), full, kept)
            peak = jnp.max(scores, axis=0, keepdims=True) * factor
            exponent = jnp.exp2(scores * factor - peak)
            total = jnp.sum(exponent, axis=0, keepdims=True)
            mix = mm(values_t, exponent.astype(bf16)) * (1.0 / total)
            o_ref[0, here, :] = mix.T.astype(bf16)
            lse_ref[0, :, here] = peak + jnp.log2(total)

    @pl.when(step == last)
    def _():
        for tick in range(gathers.ticks):
            if FRONT_STEPS[tick] >= last:
                gathers.advance(tick)
        gathers.advance(gathers.ticks)
        cot_move.finish()
        keep.wait()
        keep_norm.wait()
        sems.drain()


FRONT_EXCHANGE = (1, 2, 4, 5)
FRONT_STEPS = (1, 3, 6, 10, 14, 18, 21, 99)


def front_call(kind, x, mod, weight, bias, out, up, down, cot):
    slots, width = x.shape
    tiles = 2
    groups, parts, rows_each, part_width = weight.shape
    size = width // H
    sizes = sizes_of()
    lead = tuple(sizes[a] for a in AXES)
    needed = sems_needed(sizes, 10, 1 + EXCHANGE_CHUNKS * sizes["y"])
    first_head = parts * tiles
    anywhere = pl.BlockSpec(memory_space=pl.ANY)

    def part(s):
        return jnp.minimum(lax.div(s, tiles), parts - 1)

    def head(s):
        return jnp.maximum(s - first_head, 0)

    return pl.pallas_call(
        functools.partial(front_kernel, tiles, min(256, slots)),
        grid=(first_head + H,),
        in_specs=[
            pl.BlockSpec(memory_space=pltpu.SMEM),
            pl.BlockSpec((slots // tiles, width), lambda s: (jnp.where(s < tiles, s, tiles - 1), 0)),
            whole_spec(mod.shape),
            pl.BlockSpec(
                (groups, 1, rows_each, part_width),
                lambda s: (0, lax.rem(part(s), 2) * 2 + lax.div(part(s), 2), 0, 0),
            ),
            pl.BlockSpec((1, 1, part_width), lambda s: (part(s), 0, 0)),
        ]
        + [anywhere] * 4,
        out_specs=[
            anywhere,
            anywhere,
            pl.BlockSpec((1, slots, size), lambda s: (head(s), 0, 0)),
            pl.BlockSpec((1, 1, slots), lambda s: (head(s), 0, 0)),
        ]
        + [anywhere] * 4,
        out_shape=[
            jax.ShapeDtypeStruct((3 * H, slots, size), bf16),
            jax.ShapeDtypeStruct((slots, width), bf16),
            jax.ShapeDtypeStruct((H, slots, size), bf16),
            jax.ShapeDtypeStruct((H, 1, slots), f32),
        ]
        + [jax.ShapeDtypeStruct(lead + piece.shape, bf16) for piece in (out, up, down)]
        + [jax.ShapeDtypeStruct(cot.shape, bf16)],
        scratch_shapes=[
            pltpu.VMEM((3 * H, slots, size), bf16),
            pltpu.VMEM((slots, width), bf16),
            pltpu.SemaphoreType.DMA((2,)),
            pltpu.SemaphoreType.DMA((needed,)),
            pltpu.SemaphoreType.DMA((needed,)),
        ],
        compiler_params=pltpu.CompilerParams(
            collective_id=3, has_side_effects=True, vmem_limit_bytes=VMEM_MOST
        ),
        name="front",
    )(kind, x, mod, weight, bias, out, up, down, cot)


class Scatter:
    def __init__(self, place, sems, grad, held, recvs, axes, rows=None):
        self.place, self.sems, self.grad, self.held, self.recvs, self.axes = (
            place, sems, grad, held, recvs, axes
        )
        self.rows = rows
        self.slots = {}

    @staticmethod
    def scratch(sizes, axes, rows, width):
        held = pltpu.VMEM(tuple(sizes[a] for a in "zxy") + (rows, width), bf16)
        recvs = []
        for at, axis in enumerate(axes):
            left = tuple(sizes[a] for a in "zxy" if a not in axes[: at + 1])
            recvs.append(pltpu.VMEM((sizes[axis] - 1,) + left + (rows, width), bf16))
        return [held] + recvs

    def wanted(self, of):
        spots = tuple(of if name == "c" else slice(None) for name in AXES)
        if self.rows is not None:
            spots = spots + (pl.ds(*self.rows), slice(None))
        return self.grad.at[spots]

    def share(self, stage, index):
        done = self.axes[1:stage]
        spots = []
        for name in "zxy":
            if name in done:
                spots.append(self.place.at[name])
            elif name == self.axes[stage]:
                spots.append(index)
            else:
                spots.append(slice(None))
        return self.held.at[tuple(spots)]

    def start(self, stage):
        axis = self.axes[stage]
        place = self.place
        if stage == 0:
            self.kept = self.sems.local(lambda: (self.wanted(place.at["c"]), self.held))

        def ends(step):
            index = place.after(axis, step)
            src = self.wanted(index) if stage == 0 else self.share(stage, index)
            return src, self.recvs[stage].at[step - 1], place.device(axis, index)

        for step in range(1, place.size[axis]):
            self.slots[stage, step] = self.sems.copy(functools.partial(ends, step))

    def arrive(self, stage):
        axis = self.axes[stage]
        place = self.place
        if stage == 0:
            self.kept.wait()
        for step in range(1, place.size[axis]):
            self.sems.arrived(
                self.slots[stage, step], self.recvs[stage].at[step - 1],
                place.device(axis, place.before(axis, step)),
            )

    def finish(self, stage):
        self.arrive(stage)
        place = self.place
        left = [a for a in "zxy" if a not in self.axes[: stage + 1]]
        recv = self.recvs[stage]

        def one(at, carry):
            spots = {}
            for a in reversed(left):
                spots[a] = lax.rem(at, place.size[a])
                at = lax.div(at, place.size[a])
            where = tuple(spots.get(a, place.at[a]) for a in "zxy")
            inner = tuple(spots[a] for a in left)
            total = self.held[where].astype(f32)
            for step in range(recv.shape[0]):
                total = total + recv[(step,) + inner].astype(f32)
            self.held[where] = total.astype(bf16)
            return carry

        lax.fori_loop(0, math.prod(place.size[a] for a in left), one, 0)

    def result(self, stage):
        self.arrive(stage)
        place = self.place
        recv = self.recvs[stage]
        total = self.held[tuple(place.at[a] for a in "zxy")].astype(f32)
        for step in range(recv.shape[0]):
            total = total + recv[step].astype(f32)
        return total


def sum_axes(orders, at):
    return orders[at // 2 % len(orders)][at % 2][::-1]


def sum_scratch(sizes, grads, orders):
    scratch, number = [], 0
    for rows, width, whole, count in grads:
        near = sizes["c"]
        scratch.append(
            pltpu.VMEM((rows, width) if whole else (near, rows // near, width), f32)
        )
        for span in spans_of(rows, count):
            scratch += Scatter.scratch(sizes, sum_axes(orders, number), span[1], width)
            number += 1
    return scratch


class Sums:
    def __init__(self, place, sems, grads, finals, scratch, orders):
        self.place, self.sems, self.finals = place, sems, finals
        scratch = list(scratch)
        self.totals, self.pairs = [], []
        at = -1
        for which, (grad, count) in enumerate(grads):
            self.totals.append(scratch.pop(0))
            for span in spans_of(grad.shape[4], count):
                at += 1
                axes = sum_axes(orders, at)
                held, recvs, scratch = scratch[0], scratch[1:5], scratch[5:]
                unit = Scatter(place, sems, grad, held, recvs, axes, span)
                if at % 2 == 0:
                    self.pairs.append([])
                self.pairs[-1].append((unit, span, which))
        self.ticks = len(self.pairs) + 3

    def advance(self, tick):
        for pair in fresh(self.pairs, tick):
            for unit, *_ in pair:
                unit.start(0)
        for stage in (0, 2, 1, 3):
            if 0 <= tick - 1 - stage < len(self.pairs):
                for unit, span, which in self.pairs[tick - 1 - stage]:
                    if stage == 3:
                        self.settle(which, unit, span)
                    else:
                        unit.finish(stage)
                        unit.start(stage + 1)

    def settle(self, at, unit, span):
        value = unit.result(3)
        first, size = span
        total = self.totals[at]
        if len(total.shape) == 2:
            total[first : first + size, :] = value
            return
        each = total.shape[1]
        for to in range(total.shape[0]):
            low, high = max(first, to * each), min(first + size, (to + 1) * each)
            if low < high:
                total[to, low - to * each : high - to * each, :] = value[
                    low - first : high - first, :
                ]

    def deliver(self):
        place = self.place
        mine = place.at["c"]
        self.kept, self.flights = [], []
        def ends(total, final, step):
            to = place.after("c", step)
            return total.at[to], final.at[mine], place.device("c", to)

        for total, final in zip(self.totals, self.finals):
            if len(total.shape) == 2:
                self.kept.append(self.sems.local(lambda t=total, f=final: (t, f)))
                continue
            self.kept.append(self.sems.local(lambda t=total, f=final: (t.at[mine], f.at[mine])))
            for step in range(1, place.size["c"]):
                slot = self.sems.copy(functools.partial(ends, total, final, step))
                self.flights.append((final, step, slot))

    def delivered(self):
        for made in self.kept:
            made.wait()
        for final, step, slot in self.flights:
            source = self.place.before("c", step)
            self.sems.arrived(slot, final.at[source], self.place.device("c", source))


def sizes_of():
    dp, head = lax.axis_size("dp"), lax.axis_size("head")
    return {"z": 4, "x": 2, "c": dp // 8, "y": head}


def final_shape(grad, near):
    return jax.ShapeDtypeStruct((near, grad.shape[4] // near, grad.shape[5]), f32)


def finish_kernel(
    row_ref, ada_ref, rows_ref, hot_ref, gin_ref, qkv_ref,
    bias_ref, dada_ref, gsilu_ref, gin_full, dqkv_ref,
    send, recv, share_send, share_recv, row_s, share_s, *scratch,
):
    place = Place()
    count, me = place.count, place.me
    sems = Sems(send, recv)
    sums = Sums(
        place, sems, [(qkv_ref, FINISH_SPANS)], (dqkv_ref,), scratch, FINISH_ORDERS
    )
    greet_all(place)
    rows = Gather(place, sems, row_ref, row_s, "zxyc")
    rows.own()
    rows.start(0)
    gin_move = Exchange(place, sems, gin_ref, gin_full, EXCHANGE_CHUNKS)
    sums.advance(0)
    gin_move.start(0)
    for tick in range(1, 5):
        sums.advance(tick)
        if tick < EXCHANGE_CHUNKS:
            gin_move.start(tick)
        rows.wait(tick - 1)
        if tick < 4:
            rows.start(tick)

    whole = row_s[...].reshape(count, row_ref.shape[1])
    bias_ref[...] = jnp.sum(whole, axis=0, keepdims=True)
    cols = ada_ref.shape[1]
    low = jnp.zeros((count, cols), f32)
    for y in range(place.size["y"]):
        low = jnp.where(place.at["y"] == y, whole[:, y * cols : (y + 1) * cols], low)
    low = low.astype(bf16)
    dada_ref[...] = lax.dot_general(
        rows_ref[...].astype(bf16), low, (((0,), (0,)), ((), ())), preferred_element_type=f32
    )
    grad = mm_nt(low, ada_ref[...])
    hot = hot_ref[...][:, :count]
    placed = lax.dot_general(
        hot, grad, (((0,), (0,)), ((), ())), precision=lax.Precision.HIGHEST,
        preferred_element_type=f32,
    )
    pad = share_s.shape[2] - placed.shape[1]
    placed = jnp.concatenate([placed, jnp.zeros((count, pad), f32)], axis=1)
    share_s[...] = placed.reshape(share_s.shape)

    def push(step):
        to = lax.rem(me + step, count)
        return pltpu.make_async_remote_copy(
            src_ref=share_s.at[to], dst_ref=gsilu_ref.at[me],
            send_sem=share_send.at[step], recv_sem=share_recv.at[step],
            device_id=place.numbered(to), device_id_type=MESH,
        )

    def came(step):
        source = lax.rem(me + count - step, count)
        return pltpu.make_async_remote_copy(
            src_ref=gsilu_ref.at[source], dst_ref=gsilu_ref.at[source],
            send_sem=share_send.at[step], recv_sem=share_recv.at[step],
            device_id=place.numbered(source), device_id_type=MESH,
        )

    def do_push(step, carry):
        push(step).start()
        return carry

    def do_wait(step, carry):
        came(step).wait_recv()
        push(step).wait_send()
        return carry

    lax.fori_loop(1, count, do_push, 0)
    gsilu_ref[me] = share_s[me]
    for tick in range(5, sums.ticks + 1):
        sums.advance(tick)
    sums.deliver()
    lax.fori_loop(1, count, do_wait, 0)
    sums.delivered()
    gin_move.finish()
    sems.drain()


FINISH_SPANS = 4


def finish_call(row, ada, silu_rows, hot, gin, qkv):
    sizes = sizes_of()
    near = sizes["c"]
    count = 8 * near * sizes["y"]
    anywhere = pl.BlockSpec(memory_space=pl.ANY)
    vmem = pl.BlockSpec(memory_space=pltpu.VMEM)
    needed = sems_needed(sizes, 2 + FINISH_SPANS, 1 + EXCHANGE_CHUNKS * sizes["y"] + 4 * near)
    return pl.pallas_call(
        finish_kernel,
        in_specs=[anywhere, vmem, vmem, vmem] + [anywhere] * 2,
        out_specs=[vmem] * 3 + [anywhere] * 2,
        out_shape=[
            jax.ShapeDtypeStruct(row.shape, f32),
            jax.ShapeDtypeStruct(ada.shape, f32),
            jax.ShapeDtypeStruct((count, 1, 128), f32),
            jax.ShapeDtypeStruct(gin.shape, bf16),
            final_shape(qkv, near),
        ],
        scratch_shapes=[
            pltpu.SemaphoreType.DMA((needed,)),
            pltpu.SemaphoreType.DMA((needed,)),
            pltpu.SemaphoreType.DMA((count,)),
            pltpu.SemaphoreType.DMA((count,)),
            pltpu.VMEM((4, 2, near, sizes["y"], 1, row.shape[1]), f32),
            pltpu.VMEM((count, 1, 128), f32),
        ]
        + sum_scratch(
            sizes,
            [qkv.shape[4:] + (False, FINISH_SPANS)],
            FINISH_ORDERS,
        ),
        compiler_params=pltpu.CompilerParams(
            collective_id=1, has_side_effects=True, vmem_limit_bytes=VMEM_MOST
        ),
        name="sum_finish",
    )(row, ada, silu_rows, hot, gin, qkv)


BACK_SPANS = (4, 4)
BACK_STEPS = (1, 2, 4, 7, 10, 13, 99)


def attn_back_kernel(
    ts, kind_ref, q_ref, k_ref, v_ref, g_ref, lse_ref, up_p, down_p,
    out_ref, dup_ref, ddown_ref, dk_s, dv_s, send, recv, *scratch,
):
    step = pl.program_id(0)
    last = pl.num_programs(0) - 1
    place = Place()
    sems = Sems(send, recv)
    sums = Sums(
        place, sems, list(zip((up_p, down_p), BACK_SPANS)), (dup_ref, ddown_ref), scratch,
        BACK_ORDERS,
    )

    @pl.when(step == 0)
    def _():
        greet(place)

    for tick in range(sums.ticks):
        if BACK_STEPS[tick] < H - 1:
            @pl.when(step == BACK_STEPS[tick])
            def _(tick=tick):
                if tick == 0:
                    met(place)
                sums.advance(tick)

    slots, size = q_ref.shape[1:]
    kept = slots - slots // 16
    scale = size ** (-0.5)
    factor = log2_e * scale
    full = kind_ref[0] == 0
    keys = k_ref[0]
    keys_t = keys.T
    values = v_ref[0]
    for start in range(0, slots, ts):
        here = slice(start, start + ts)
        queries = q_ref[0, here, :]
        grad = g_ref[0, here, :]
        scores = masked(mm_nt(keys, queries), full, kept)
        probs = jnp.exp2(scores * factor - lse_ref[0, :, here])
        weighted = probs * mm_nt(values, grad)
        inner = jnp.sum(weighted, axis=0, keepdims=True)
        grad_scores = (weighted - probs * inner).astype(bf16)
        add_v = mm(probs.astype(bf16), grad)
        add_k = mm(grad_scores, queries)
        if start == 0:
            dv_s[...] = add_v
            dk_s[...] = add_k
        else:
            dv_s[...] += add_v
            dk_s[...] += add_k
        out_ref[0, 0, here, :] = (mm(keys_t, grad_scores) * scale).T.astype(bf16)
    out_ref[1, 0] = (dk_s[...] * scale).astype(bf16)
    out_ref[2, 0] = dv_s[...].astype(bf16)

    @pl.when(step == last)
    def _():
        for tick in range(sums.ticks):
            if BACK_STEPS[tick] >= H - 1:
                sums.advance(tick)
        sums.advance(sums.ticks)
        sums.deliver()
        sums.delivered()
        sems.drain()


def attn_back_call(kind, qkv, grad, lse, up, down):
    _, slots, size = qkv.shape
    ts = min(256, slots)
    block = (1, slots, size)
    sizes = sizes_of()
    anywhere = pl.BlockSpec(memory_space=pl.ANY)
    needed = sems_needed(sizes, sum(BACK_SPANS), 2 * sizes["y"] + 4 * sizes["c"])
    return pl.pallas_call(
        functools.partial(attn_back_kernel, ts),
        grid=(H,),
        in_specs=[
            pl.BlockSpec(memory_space=pltpu.SMEM),
            pl.BlockSpec(block, lambda h: (h, 0, 0)),
            pl.BlockSpec(block, lambda h: (h + H, 0, 0)),
            pl.BlockSpec(block, lambda h: (h + 2 * H, 0, 0)),
            pl.BlockSpec(block, lambda h: (h, 0, 0)),
            pl.BlockSpec((1, 1, slots), lambda h: (h, 0, 0)),
        ]
        + [anywhere] * 2,
        out_specs=[pl.BlockSpec((3, 1, slots, size), lambda h: (0, h, 0, 0))] + [anywhere] * 2,
        out_shape=[
            jax.ShapeDtypeStruct((3, H, slots, size), bf16),
            final_shape(up, sizes["c"]),
            jax.ShapeDtypeStruct(down.shape[4:], f32),
        ],
        scratch_shapes=[
            pltpu.VMEM((slots, size), f32),
            pltpu.VMEM((slots, size), f32),
            pltpu.SemaphoreType.DMA((needed,)),
            pltpu.SemaphoreType.DMA((needed,)),
        ]
        + sum_scratch(
            sizes,
            [
                grad.shape[4:] + (at == 1, count)
                for at, (grad, count) in enumerate(zip((up, down), BACK_SPANS))
            ],
            BACK_ORDERS,
        ),
        compiler_params=pltpu.CompilerParams(
            collective_id=2, has_side_effects=True, vmem_limit_bytes=VMEM_MOST
        ),
        name="attention_backward",
    )(kind, qkv, qkv, qkv, grad, lse, up, down)


MLP_SPANS = 4
MLP_GATHER = (1, 2, 3, 5, 7, 9, 11)
MLP_SUM = (12, 13, 15, 17, 19, 21, 22)


def mlp_kernel(
    tiles, second_ref, gm_ref, up0_f, down0_f, up1_p, down1_p, b_ref,
    mlp_ref, gsec_ref, bias_ref, up1_f, down1_f, dup0_ref, ddown0_ref, dup1_ref, ddown1_ref,
    sup_ref, sdown_ref,
    sec_t, act_t, gh_s, up_s, down_s, raw_up, raw_down, loaded, stored,
    send, recv, *scratch,
):
    step = pl.program_id(0)
    subs = tiles + 2
    last = 4 * subs - 1
    tile_at = lax.div(step, subs)
    sub = lax.rem(step, subs)
    slots, width = second_ref.shape
    hidden = up_s.shape[1]
    tm = slots // tiles

    place = Place()
    sems = Sems(send, recv)
    near, head_half = place.size["c"], place.size["y"] // 2

    def loads(tile):
        half = tile % 2
        up, down = ((up0_f, down0_f), (up1_f, down1_f))[tile // 2]
        return (
            pltpu.make_async_copy(
                up.at[:, :, :, pl.ds(half * head_half, head_half)], raw_up, loaded.at[0]
            ),
            pltpu.make_async_copy(down.at[pl.ds(2 * half, 2)], raw_down, loaded.at[1]),
        )

    def stores(tile):
        half = tile % 2
        up, down = ((dup0_ref, ddown0_ref), (dup1_ref, ddown1_ref))[tile // 2]
        return (
            pltpu.make_async_copy(
                raw_up, up.at[:, :, :, pl.ds(half * head_half, head_half)], stored.at[0]
            ),
            pltpu.make_async_copy(raw_down, down.at[pl.ds(2 * half, 2)], stored.at[1]),
        )

    wanted = []
    for piece, full in ((up1_p, up1_f), (down1_p, down1_f)):
        wanted += [(piece, full, span) for span in spans_of(piece.shape[0], MLP_SPANS)]
    gathers = Gathers(place, sems, wanted, MLP_ORDERS)
    sums = Sums(
        place, sems, [(dup0_ref, MLP_SPANS), (ddown0_ref, MLP_SPANS)], (sup_ref, sdown_ref), scratch,
        MLP_SUM_ORDERS,
    )

    @pl.when(step == 0)
    def _():
        greet(place)

    for tick in range(gathers.ticks):
        @pl.when(step == MLP_GATHER[tick])
        def _(tick=tick):
            if tick == 0:
                met(place)
            gathers.advance(tick)

    @pl.when(step == 2 * subs)
    def _():
        gathers.advance(gathers.ticks)

    @pl.when(step == 0)
    def _():
        sec_t[...] = second_ref[...].T
        mlp_ref[...] = jnp.zeros_like(mlp_ref)
        gsec_ref[...] = jnp.zeros_like(gsec_ref)
        for made in loads(0):
            made.start()

    for tile in range(4):
        @pl.when(step == tile * subs)
        def _(tile=tile):
            if tile > 0:
                stores(tile - 1)[1].wait()
                loads(tile)[1].start()
            if tile == 2:
                loads(tile)[0].start()
            for made in loads(tile):
                made.wait()

    @pl.when(sub == 0)
    def _():
        share = raw_up.shape[5]
        for y in range(raw_up.shape[3]):
            for c in range(near):
                off = (y * near + c) * share
                up_s[:, off : off + share] = raw_up[:, :, c, y].reshape(width, share)
        chunk, share = raw_down.shape[4:]
        for at in range(4 * near):
            for y in range(raw_down.shape[3]):
                down_s[at * chunk : (at + 1) * chunk, y * share : (y + 1) * share] = raw_down[
                    at // (2 * near), (at // near) % 2, at % near, y
                ]
        bias_ref[...] = jnp.zeros_like(bias_ref)

    for tick in range(sums.ticks):
        if MLP_SUM[tick] < last:
            @pl.when(step == MLP_SUM[tick])
            def _(tick=tick):
                sums.advance(tick)

    @pl.when(sub < tiles)
    def _():
        rows = pl.ds(pl.multiple_of(sub * tm, tm), tm)
        pre = mm(second_ref[rows, :], up_s[...]) + b_ref[0]
        square = pre * pre
        tanh = jnp.tanh(gelu_in * (pre + gelu_cube * pre * square))
        act = (0.5 * pre * (1.0 + tanh)).astype(bf16)
        slope = 0.5 * (1.0 + tanh) + 0.5 * pre * (1.0 - tanh * tanh) * (
            gelu_in * (1.0 + 3.0 * gelu_cube * square)
        )
        grad = mm_nt(gm_ref[rows, :], down_s[...]) * slope
        bias_ref[0] += jnp.sum(grad, axis=0, keepdims=True)
        grad_low = grad.astype(bf16)
        gh_s[rows, :] = grad_low
        act_t[:, rows] = act.T
        mlp_ref[rows, :] += mm(act, down_s[...])
        gsec_ref[rows, :] += mm_nt(grad_low, up_s[...])

    @pl.when(sub == tiles)
    def _():
        share = raw_up.shape[5]
        half = width // 2
        for j in range(2):
            grad = mm(sec_t[j * half : (j + 1) * half, :], gh_s[...]).astype(bf16)
            for y in range(raw_up.shape[3]):
                for c in range(near):
                    off = (y * near + c) * share
                    raw_up[2 * j : 2 * j + 2, :, c, y] = grad[:, off : off + share].reshape(
                        2, 2, half // 4, share
                    )

    @pl.when(sub == tiles + 1)
    def _():
        chunk, share = raw_down.shape[4:]
        half = hidden // 2
        for j in range(2):
            grad = mm(act_t[j * half : (j + 1) * half, :], gm_ref[...]).astype(bf16)
            for at in range(2 * near):
                for y in range(raw_down.shape[3]):
                    raw_down[j, at // near, at % near, y] = grad[
                        at * chunk : (at + 1) * chunk, y * share : (y + 1) * share
                    ]

    for tile in range(4):
        @pl.when(step == tile * subs + tiles)
        def _(tile=tile):
            stores(tile)[0].start()

        @pl.when(step == tile * subs + tiles + 1)
        def _(tile=tile):
            stores(tile)[0].wait()
            if tile in (0, 2):
                loads(tile + 1)[0].start()
            stores(tile)[1].start()

    @pl.when(step == last)
    def _():
        stores(3)[1].wait()
        for tick in range(sums.ticks):
            if MLP_SUM[tick] >= last:
                sums.advance(tick)
        sums.advance(sums.ticks)
        sums.deliver()
        sums.delivered()
        sems.drain()


def mlp_call(second, gm, up0, down0, up1, down1, bias):
    slots, width = second.shape
    tiles = 4
    subs = tiles + 2
    sizes = sizes_of()
    near, head = sizes["c"], sizes["y"]
    lead = tuple(sizes[a] for a in AXES)
    rows_up, share_up = up1.shape
    rows_down, share_down = down1.shape
    hidden = share_up * near * head // 2
    anywhere = pl.BlockSpec(memory_space=pl.ANY)
    needed = sems_needed(sizes, 4 * MLP_SPANS, 4 * near)
    bias_spec = pl.BlockSpec((1, 1, hidden), lambda s: (lax.div(s, subs), 0, 0))
    full_up = jax.ShapeDtypeStruct(lead + up1.shape, bf16)
    full_down = jax.ShapeDtypeStruct(lead + down1.shape, bf16)
    return pl.pallas_call(
        functools.partial(mlp_kernel, tiles),
        grid=(4 * subs,),
        in_specs=[once_spec((slots, width)), once_spec((slots, width))]
        + [anywhere] * 4
        + [bias_spec],
        out_specs=[once_spec((slots, width)), once_spec((slots, width)), bias_spec] + [anywhere] * 8,
        out_shape=[
            jax.ShapeDtypeStruct((slots, width), f32),
            jax.ShapeDtypeStruct((slots, width), f32),
            jax.ShapeDtypeStruct(bias.shape, f32),
            full_up, full_down, full_up, full_down, full_up, full_down,
            final_shape(full_up, near),
            jax.ShapeDtypeStruct(down1.shape, f32),
        ],
        scratch_shapes=[
            pltpu.VMEM((width, slots), bf16),
            pltpu.VMEM((hidden, slots), bf16),
            pltpu.VMEM((slots, hidden), bf16),
            pltpu.VMEM((width, hidden), bf16),
            pltpu.VMEM((hidden, width), bf16),
            pltpu.VMEM((4, 2, near, head // 2) + up1.shape, bf16),
            pltpu.VMEM((2, 2, near, head) + down1.shape, bf16),
            pltpu.SemaphoreType.DMA((2,)),
            pltpu.SemaphoreType.DMA((2,)),
            pltpu.SemaphoreType.DMA((needed,)),
            pltpu.SemaphoreType.DMA((needed,)),
        ]
        + sum_scratch(
            sizes, (up1.shape + (False, MLP_SPANS), down1.shape + (True, MLP_SPANS)), MLP_SUM_ORDERS
        ),
        compiler_params=pltpu.CompilerParams(
            collective_id=4, has_side_effects=True, vmem_limit_bytes=MLP_VMEM
        ),
        name="feed_forward_both_ways",
    )(second, gm, up0, down0, up1, down1, bias)


MLP_VMEM = 63 * 1024 * 1024


QKV_SPANS = 2
QKV_ORDERS = (EVEN,)


def qkv_back_kernel(
    tm, g_ref, norm_ref, w_ref, x_ref, gmid_ref, mod_ref, act_p, out_p,
    gin_ref, dw_ref, bias_ref, sums_ref, act_f, dout_ref, norm_t, gp_s, gn_s, send, recv, *scratch,
):
    part = pl.program_id(0)
    slots, width = x_ref.shape
    tiles = slots // tm
    groups, _, rows_each, part_width = w_ref.shape
    heads = g_ref.shape[0]
    last = pl.num_programs(0) - 1

    place = Place()
    sems = Sems(send, recv)
    sums = Sums(place, sems, [(out_p, QKV_SPANS)], (dout_ref,), scratch, QKV_ORDERS)
    act_move = Exchange(place, sems, act_p, act_f, EXCHANGE_CHUNKS)
    for tick in range(4):
        @pl.when(part == tick)
        def _(tick=tick):
            if tick == 0:
                greet(place)
                met(place)
            sums.advance(tick)
            act_move.start(tick)

    @pl.when(part == 0)
    def _():
        norm_t[...] = norm_ref[...].T
        gn_s[...] = jnp.zeros_like(gn_s)

    def tile(i, total):
        rows = pl.ds(pl.multiple_of(i * tm, tm), tm)
        grad = jnp.concatenate([g_ref[j, rows, :] for j in range(heads)], axis=1)
        gp_s[rows, :] = grad
        gn_s[rows, :] += mm_nt(grad, w_ref[...].reshape(width, part_width))
        return total + jnp.sum(grad.astype(f32), axis=0, keepdims=True)

    bias_ref[0] = lax.fori_loop(0, tiles, tile, jnp.zeros((1, part_width), f32))
    per = groups // 2
    for j in range(2):
        dw_ref[per * j : per * (j + 1), 0] = (
            mm(norm_t[per * j * rows_each : per * (j + 1) * rows_each, :], gp_s[...])
            .astype(bf16)
            .reshape(per, rows_each, part_width)
        )

    @pl.when(part == pl.num_programs(0) - 1)
    def _():
        def finish(i, sums):
            rows = pl.ds(pl.multiple_of(i * tm, tm), tm)
            center, inv = center_spread(x_ref[rows, :].astype(f32))
            unit = center * inv
            grad = gn_s[rows, :]
            gin_ref[rows, :] = (
                gmid_ref[rows, :] + norm_back(grad * (1.0 + mod_ref[1:2, :]), unit, inv)
            ).astype(gin_ref.dtype)
            return (
                sums[0] + jnp.sum(grad, axis=0, keepdims=True),
                sums[1] + jnp.sum(grad * unit, axis=0, keepdims=True),
            )

        zero = jnp.zeros((1, width), f32)
        shift, scale = lax.fori_loop(0, tiles, finish, (zero, zero))
        sums_ref[...] = jnp.zeros_like(sums_ref)
        sums_ref[0:1, :] = shift
        sums_ref[1:2, :] = scale

    @pl.when(part == last)
    def _():
        sums.advance(4)
        sums.deliver()
        sums.delivered()
        act_move.finish()
        sems.drain()


def qkv_back_call(grad, norm, weight, x, gmid, mod, act, out):
    slots, width = x.shape
    tm = min(256, slots)
    size = width // H
    groups, parts, rows_each, part_width = weight.shape
    heads = part_width // size
    sizes = sizes_of()
    anywhere = pl.BlockSpec(memory_space=pl.ANY)
    needed = sems_needed(sizes, QKV_SPANS, 1 + EXCHANGE_CHUNKS * sizes["y"] + 4 * sizes["c"])
    w_spec = pl.BlockSpec((groups, 1, rows_each, part_width), lambda p: (0, place(p), 0, 0))
    return pl.pallas_call(
        functools.partial(qkv_back_kernel, tm),
        grid=(parts,),
        in_specs=[
            pl.BlockSpec((heads, slots, size), lambda p: (p, 0, 0)),
            once_spec((slots, width)),
            w_spec,
            once_spec((slots, width)),
            once_spec((slots, width)),
            whole_spec(mod.shape),
            anywhere,
            anywhere,
        ],
        out_specs=[
            once_spec((slots, width)),
            w_spec,
            pl.BlockSpec((1, 1, part_width), lambda p: (p, 0, 0)),
            whole_spec((8, width)),
            anywhere,
            anywhere,
        ],
        out_shape=[
            jax.ShapeDtypeStruct((slots, width), bf16),
            jax.ShapeDtypeStruct(weight.shape, bf16),
            jax.ShapeDtypeStruct((parts, 1, part_width), f32),
            jax.ShapeDtypeStruct((8, width), f32),
            jax.ShapeDtypeStruct(act.shape, bf16),
            final_shape(out, sizes["c"]),
        ],
        scratch_shapes=[
            pltpu.VMEM((width, slots), bf16),
            pltpu.VMEM((slots, part_width), bf16),
            pltpu.VMEM((slots, width), f32),
            pltpu.SemaphoreType.DMA((needed,)),
            pltpu.SemaphoreType.DMA((needed,)),
        ]
        + sum_scratch(sizes, [out.shape[4:] + (False, QKV_SPANS)], QKV_ORDERS),
        compiler_params=pltpu.CompilerParams(
            collective_id=5, has_side_effects=True, vmem_limit_bytes=VMEM_MOST
        ),
        name="qkv_backward",
    )(grad, norm, weight, x, gmid, mod, act, out)


class Wire:
    def __init__(self, width):
        self.dp = lax.axis_size("dp")
        self.head = lax.axis_size("head")
        self.near = self.dp // (width // 144)
        self.width = width
        self.groups = [
            list(range(first, first + self.near)) for first in range(0, self.dp, self.near)
        ]

    def pieces(self, weights):
        rows = weights[0].shape[0]
        stack = jnp.concatenate(
            [weight.astype(bf16).reshape(rows, self.near, -1) for weight in weights], axis=2
        )
        stack = lax.all_to_all(
            stack, "dp", split_axis=1, concat_axis=0, axis_index_groups=self.groups, tiled=True
        )
        stack = stack.reshape(rows * self.near, -1)
        ends = [0]
        for weight in weights:
            ends.append(ends[-1] + weight.shape[1] // self.near)
        return [stack[:, low:high] for low, high in zip(ends, ends[1:])]

    def columns(self, stack):
        devices, rows, cols = stack.shape
        stack = stack.reshape(self.dp // self.near, self.near, self.head, rows, cols)
        if (self.near, self.head) != (2, 2):
            quarter = self.near * self.head * cols // 4
            stack = stack.transpose(0, 3, 2, 1, 4).reshape(-1, rows, 2, 2, quarter)
            stack = stack.transpose(0, 3, 2, 1, 4)
            return stack.reshape(-1, 4, rows, quarter)
        return stack.reshape(-1, 4, rows, cols)

    def uncolumns(self, stack):
        groups, _, rows, quarter = stack.shape
        cols = 4 * quarter // (self.near * self.head)
        if (self.near, self.head) != (2, 2):
            stack = stack.reshape(groups, 2, 2, rows, quarter).transpose(0, 3, 2, 1, 4)
            stack = stack.reshape(groups, rows, self.head, self.near, cols)
            stack = stack.transpose(0, 3, 2, 1, 4)
        return stack.reshape(self.dp * self.head, rows, cols)


def body(
    inputs, cond, order, grid_kind, weight_ada, bias_ada, weight_qkv, bias_query, bias_value,
    weight_out, bias_out, weight_up, bias_up, weight_down, bias_down, cotangent,
):
    images, slot_local, width = inputs.shape
    head_count = lax.axis_size("head")
    dp_count = lax.axis_size("dp")
    head_at = lax.axis_index("head")
    dp_at = lax.axis_index("dp")
    assert images == head_count
    wire = Wire(width)

    def from_image(array):
        return lax.all_to_all(
            array[None], "head", split_axis=1, concat_axis=0, tiled=True
        ).astype(f32)

    rows_ada, cols_ada = weight_ada.shape
    ada_low = weight_ada.astype(bf16)
    silu_own, silu_pull = jax.vjp(lambda v: v * jax.nn.sigmoid(v), cond)
    chunk = weight_down.shape[0] // 2
    up_phases = weight_up.reshape(rows_ada, -1, 2, chunk)
    up0_p, up1_p, qkv_p, out_p = wire.pieces(
        [up_phases[:, :, at].reshape(rows_ada, -1) for at in range(2)] + [weight_qkv, weight_out]
    )
    order_mine = lax.dynamic_slice_in_dim(order, head_at, 1, 0)
    kind = lax.dynamic_slice_in_dim(grid_kind, head_at, 1, 0)
    mod, silu_grouped, hot, x, qkv_full = start_call(
        silu_own, order_mine, ada_low, inputs.astype(bf16), qkv_p
    )
    x = x.reshape(-1, width)
    device_stack = lambda full: full.reshape((-1,) + full.shape[4:])
    qkv_full = wire.columns(device_stack(qkv_full))
    mod_flat = mod.reshape(6, width) + bias_ada.reshape(6, width)
    mod = jnp.concatenate([mod_flat, jnp.zeros((2, width), f32)], axis=0)

    bias_qkv = jnp.concatenate([bias_query, jnp.zeros_like(bias_query), bias_value])
    down0, down1 = (weight_down[at * chunk : (at + 1) * chunk].astype(bf16) for at in range(2))
    bias_phases = bias_up.reshape(-1, 2, chunk).swapaxes(0, 1).reshape(4, 1, -1)
    qkv, norm, mix, lse, out_full, up_full, down_full, cot = front_call(
        kind, x, mod, qkv_full, bias_qkv.reshape(4, 1, -1),
        out_p, up0_p, down0, cotangent.astype(bf16),
    )
    cot = cot.reshape(-1, width)
    out_full = wire.columns(device_stack(out_full))
    attended, branch, second, gm = out_call(mix, x, cot, mod, out_full, bias_out)
    mlp, gsec, d_bias_up, _, _, _, _, d_up1, d_down1, d_up0, d_down0 = mlp_call(
        second, gm, up_full, down_full, up1_p, down1, bias_phases
    )
    d_bias_up = d_bias_up.reshape(2, -1, chunk).swapaxes(0, 1)
    act, gmid, gatt, d_out, sums = mid_back_call(
        x, branch, mlp, gsec, cot, attended, mod, out_full, bias_down
    )
    lead = (4, 2, dp_count // 8, head_count)
    stack = lambda grad: grad.reshape(lead + grad.shape[1:])
    by_image = lambda array: array.reshape(head_count, slot_local, width)
    grad, d_up1, d_down1 = attn_back_call(kind, qkv, gatt, lse, d_up1, d_down1)
    gin, d_qkv, d_bias_qkv, sums_in, act, d_out = qkv_back_call(
        grad.reshape(qkv.shape), norm, qkv_full, x, gmid, mod, by_image(act),
        stack(wire.uncolumns(d_out)),
    )

    bias_qkv_sum = d_bias_qkv.reshape(3, width)
    row = jnp.concatenate(
        [sums_in[0], sums_in[1], sums[0], sums[1], sums[2], sums[3],
         bias_qkv_sum[0], bias_qkv_sum[2], sums[4], sums[5], d_bias_up.reshape(-1)]
    ).reshape(1, -1)
    biases, d_ada, g_silu, gin, d_qkv = finish_call(
        row, ada_low, silu_grouped, hot, by_image(gin), stack(wire.uncolumns(d_qkv))
    )
    biases = biases[0]
    g_silu = g_silu.reshape(dp_count, head_count, 128)[:, :, :rows_ada].sum(axis=1)
    d_cond = silu_pull(g_silu.reshape(1, width))[0]
    side = lambda grad: grad.transpose(1, 0, 2).reshape(grad.shape[1], -1)
    d_up = jnp.stack(
        [side(part).reshape(rows_ada, -1, chunk) for part in (d_up0, d_up1)], axis=2
    ).reshape(rows_ada, -1)
    d_down = jnp.concatenate([d_down0, d_down1], axis=0)
    mods = 6 * width
    return (
        act.astype(f32),
        gin.astype(f32),
        d_cond,
        d_ada,
        side(d_qkv),
        side(d_out),
        d_up,
        d_down,
        biases[:mods],
        biases[mods : mods + width],
        biases[mods + width : mods + 2 * width],
        biases[mods + 2 * width : mods + 3 * width],
        biases[mods + 4 * width :],
        biases[mods + 3 * width : mods + 4 * width],
    )


def solution(mesh):
    in_specs = (
        P("dp", "head", None), P(("dp", "head"), None), P("dp"), P("dp"), P("dp", "head"), P(),
        P("dp", "head"), P(), P(), P("dp", "head"), P(), P("dp", "head"), P(), P("dp", "head"),
        P(), P("dp", "head", None),
    )
    out_specs = (
        P("dp", "head", None), P("dp", "head", None), P(("dp", "head"), None), P("dp", "head"),
        P("dp", "head"), P("dp", "head"), P("dp", "head"), P("dp", "head"),
        P(), P(), P(), P(), P(), P(),
    )
    return jax.shard_map(body, mesh=mesh, in_specs=in_specs, out_specs=out_specs, check_vma=False)
```

```python
import functools
import math

import jax
import jax.numpy as jnp
from jax import lax
from jax.experimental import pallas as pl
from jax.experimental.pallas import tpu as pltpu
from jax.sharding import PartitionSpec as P

H = 16
norm_eps = 1e-06
log2_e = 1.4426950408889634
gelu_in = 0.7978845608028654
gelu_cube = 0.044715
f32 = jnp.float32
bf16 = jnp.bfloat16
VMEM_MOST = 60 * 1024 * 1024


def mm(left, right):
    return jnp.dot(left, right, preferred_element_type=f32)


def mm_nt(left, right):
    return lax.dot_general(left, right, (((1,), (1,)), ((), ())), preferred_element_type=f32)


def center_spread(values):
    center = values - jnp.mean(values, axis=-1, keepdims=True)
    spread = jnp.mean(center * center, axis=-1, keepdims=True)
    return center, lax.rsqrt(spread + norm_eps)


def norm_back(grad, unit, inv):
    return inv * (
        grad
        - jnp.mean(grad, axis=-1, keepdims=True)
        - unit * jnp.mean(grad * unit, axis=-1, keepdims=True)
    )


def whole_spec(shape):
    zeros = (0,) * len(shape)
    return pl.BlockSpec(shape, lambda *_: zeros)


def once_spec(shape):
    zeros = (0,) * len(shape)
    return pl.BlockSpec(shape, lambda *_: zeros, pipeline_mode=pl.Buffered(1))


def params(most=VMEM_MOST):
    return pltpu.CompilerParams(vmem_limit_bytes=most)


def place(quarter):
    return (quarter % 2) * 2 + quarter // 2


def masked(scores, full, kept):
    return jnp.concatenate(
        [scores[:kept], jnp.where(full, scores[kept:], -1e30)], axis=0
    )


def columns_of(w_ref):
    groups, parts, rows_each, width = w_ref.shape
    return jnp.concatenate(
        [w_ref[:, place(n)].reshape(groups * rows_each, width) for n in range(parts)], axis=1
    )


def out_kernel(
    o_ref, x_ref, cot_ref, mod_ref, w_ref, b_ref, att_ref, branch_ref, second_ref, gm_ref, w_s
):
    @pl.when(pl.program_id(0) == 0)
    def _():
        w_s[...] = columns_of(w_ref)

    attended = jnp.concatenate([o_ref[j] for j in range(o_ref.shape[0])], axis=1)
    att_ref[...] = attended
    branch = mm(attended, w_s[...]) + b_ref[...]
    branch_ref[...] = branch.astype(bf16)
    middle = x_ref[...].astype(f32) + mod_ref[2:3, :] * branch
    center, inv = center_spread(middle)
    second_ref[...] = (center * inv * (1.0 + mod_ref[4:5, :]) + mod_ref[3:4, :]).astype(bf16)
    gm_ref[...] = (cot_ref[...].astype(f32) * mod_ref[5:6, :]).astype(bf16)


def out_call(mix, x, cot, mod, weight, bias):
    slots, width = x.shape
    tm = min(256, slots)
    size = width // H
    tile = pl.BlockSpec((tm, width), lambda i: (i, 0))
    return pl.pallas_call(
        out_kernel,
        grid=(slots // tm,),
        in_specs=[
            pl.BlockSpec((H, tm, size), lambda i: (0, i, 0)),
            tile,
            tile,
            whole_spec(mod.shape),
            whole_spec(weight.shape),
            whole_spec((1, width)),
        ],
        out_specs=[tile] * 4,
        out_shape=[jax.ShapeDtypeStruct((slots, width), bf16)] * 4,
        scratch_shapes=[pltpu.VMEM((width, width), bf16)],
        compiler_params=params(),
        name="out_projection",
    )(mix, x, cot, mod, weight, bias.reshape(1, width))


def mid_back_kernel(
    x_ref, branch_ref, mlp_ref, gsec_ref, cot_ref, att_ref, mod_ref, w_ref, b_ref,
    act_ref, gmid_ref, gatt_ref, dw_ref, sums_ref, w_s, dw_s,
):
    step = pl.program_id(0)

    @pl.when(step == 0)
    def _():
        w_s[...] = columns_of(w_ref)
        sums_ref[...] = jnp.zeros_like(sums_ref)
        dw_s[...] = jnp.zeros_like(dw_s)

    gate_a = mod_ref[2:3, :]
    gate_m = mod_ref[5:6, :]
    branch = branch_ref[...].astype(f32)
    middle = x_ref[...].astype(f32) + gate_a * branch
    mlp = mlp_ref[...] + b_ref[...]
    cot = cot_ref[...].astype(f32)
    act_ref[...] = (middle + gate_m * mlp).astype(act_ref.dtype)
    center, inv = center_spread(middle)
    unit = center * inv
    grad = gsec_ref[...]
    grad_mid = cot + norm_back(grad * (1.0 + mod_ref[4:5, :]), unit, inv)
    gmid_ref[...] = grad_mid
    grad_branch = gate_a * grad_mid

    def add(row, value):
        sums_ref[row : row + 1, :] += jnp.sum(value, axis=0, keepdims=True)

    add(0, grad_mid * branch)
    add(1, grad)
    add(2, grad * unit)
    add(3, cot * mlp)
    add(4, grad_branch)
    add(5, gate_m * cot)
    grad_low = grad_branch.astype(bf16)
    grad_att = mm_nt(grad_low, w_s[...]).astype(bf16)
    size = gatt_ref.shape[2]
    for j in range(gatt_ref.shape[0]):
        gatt_ref[j] = grad_att[:, j * size : (j + 1) * size]
    dw_s[...] += mm(att_ref[...].T, grad_low)

    @pl.when(step == pl.num_programs(0) - 1)
    def _():
        groups, parts, rows_each, width = dw_ref.shape
        low = dw_s[...].astype(bf16)
        for n in range(parts):
            dw_ref[:, place(n)] = low[:, n * width : (n + 1) * width].reshape(
                groups, rows_each, width
            )


def mid_back_call(x, branch, mlp, gsec, cot, attended, mod, weight, bias_down):
    slots, width = x.shape
    tm = min(256, slots)
    size = width // H
    tile = pl.BlockSpec((tm, width), lambda i: (i, 0))
    return pl.pallas_call(
        mid_back_kernel,
        grid=(slots // tm,),
        in_specs=[tile] * 6 + [whole_spec(mod.shape), whole_spec(weight.shape), whole_spec((1, width))],
        out_specs=[
            tile,
            tile,
            pl.BlockSpec((H, tm, size), lambda i: (0, i, 0)),
            whole_spec(weight.shape),
            whole_spec((8, width)),
        ],
        out_shape=[
            jax.ShapeDtypeStruct((slots, width), bf16),
            jax.ShapeDtypeStruct((slots, width), f32),
            jax.ShapeDtypeStruct((H, slots, size), bf16),
            jax.ShapeDtypeStruct(weight.shape, bf16),
            jax.ShapeDtypeStruct((8, width), f32),
        ],
        scratch_shapes=[pltpu.VMEM((width, width), bf16), pltpu.VMEM((width, width), f32)],
        compiler_params=params(),
        name="middle_backward",
    )(x, branch, mlp, gsec, cot, attended, mod, weight, bias_down.reshape(1, width))


MESH = pl.DeviceIdType.MESH


class Place:
    def __init__(self):
        self.dp = lax.axis_size("dp")
        head = lax.axis_size("head")
        near = self.dp // 8
        at = lax.axis_index("dp")
        self.size = {"z": 4, "x": 2, "c": near, "y": head}
        self.at = {
            "z": lax.div(at, 2 * near),
            "x": lax.rem(lax.div(at, near), 2),
            "c": lax.rem(at, near),
            "y": lax.axis_index("head"),
        }
        self.count = self.dp * head
        self.me = at * head + self.at["y"]

    def device(self, axis, index):
        spot = dict(self.at)
        spot[axis] = index
        return ((spot["z"] * 2 + spot["x"]) * self.size["c"] + spot["c"], spot["y"])

    def numbered(self, index):
        head = self.size["y"]
        return (lax.div(index, head), lax.rem(index, head))

    def after(self, axis, step):
        return lax.rem(self.at[axis] + step, self.size[axis])

    def before(self, axis, step):
        return lax.rem(self.at[axis] + self.size[axis] - step, self.size[axis])


class Local:
    def __init__(self, sem, ends):
        self.sem, self.ends = sem, ends

    def made(self):
        return pltpu.make_async_copy(*self.ends(), self.sem())

    def wait(self):
        self.made().wait()


class Sems:
    def __init__(self, send, recv):
        self.send, self.recv, self.used = send, recv, 0
        self.sent = []

    def describe(self, at, src, dst, device):
        return pltpu.make_async_remote_copy(
            src_ref=src, dst_ref=dst, send_sem=self.send.at[at], recv_sem=self.recv.at[at],
            device_id=device, device_id_type=MESH,
        )

    def copy(self, ends):
        at = self.used
        self.used += 1
        self.describe(at, *ends()).start()
        self.sent.append((at, ends))
        return at

    def arrived(self, at, dst, device):
        self.describe(at, dst, dst, device).wait_recv()

    def local(self, ends):
        at = self.used
        self.used += 1
        made = Local(lambda: self.send.at[at], ends)
        made.made().start()
        return made

    def drain(self):
        for at, ends in self.sent:
            self.describe(at, *ends()).wait_send()


AXES = "zxcy"


def spans_of(rows, count):
    cuts = [16 * (rows // 16 * at // count) for at in range(count)] + [rows]
    return [(low, high - low) for low, high in zip(cuts, cuts[1:])]


def halves(rows):
    return spans_of(rows, 2)


class Gather:
    def __init__(self, place, sems, piece, full, axes, rows=None):
        self.place, self.sems, self.piece, self.full, self.axes = place, sems, piece, full, axes
        self.rows = rows
        self.slots = {}

    def part(self, got, axis=None, index=None):
        spot = dict(self.place.at)
        if axis is not None:
            spot[axis] = index
        spots = tuple(slice(None) if name in got else spot[name] for name in AXES)
        if self.rows is not None:
            spots = spots + (pl.ds(*self.rows), slice(None))
        return self.full.at[spots]

    def first(self):
        return self.piece if self.rows is None else self.piece.at[pl.ds(*self.rows)]

    def own(self):
        self.kept = self.sems.local(lambda: (self.first(), self.part("")))

    def start(self, stage):
        axis = self.axes[stage]
        got = self.axes[:stage]
        if stage == 1:
            self.kept.wait()

        def ends(step):
            return (
                self.first() if stage == 0 else self.part(got),
                self.part(got),
                self.place.device(axis, self.place.after(axis, step)),
            )

        for step in range(1, self.place.size[axis]):
            self.slots[stage, step] = self.sems.copy(functools.partial(ends, step))

    def wait(self, stage):
        axis = self.axes[stage]
        got = self.axes[:stage]
        for step in range(1, self.place.size[axis]):
            index = self.place.before(axis, step)
            self.sems.arrived(
                self.slots[stage, step], self.part(got, axis, index), self.place.device(axis, index)
            )


EVEN = ("zxyc", "zyxc")
WIDE = ("zyxc", "yzxc")


AHEAD = 2


def fresh(pairs, tick):
    return pairs[:AHEAD] if tick == 0 else pairs[tick + AHEAD - 1 : tick + AHEAD]


class Gathers:
    def __init__(self, place, sems, spans, orders):
        self.pairs = []
        for at in range(0, len(spans), 2):
            pair = orders[at // 2 % len(orders)]
            self.pairs.append(
                [
                    Gather(place, sems, piece, full, axes, rows)
                    for (piece, full, rows), axes in zip(spans[at : at + 2], pair)
                ]
            )
        self.ticks = len(self.pairs) + 3

    def advance(self, tick):
        for pair in fresh(self.pairs, tick):
            for unit in pair:
                unit.own()
                unit.start(0)
        for stage in (1, 0, 2, 3):
            if 0 <= tick - 1 - stage < len(self.pairs):
                for unit in self.pairs[tick - 1 - stage]:
                    unit.wait(stage)
                    if stage < 3:
                        unit.start(stage + 1)


def greet_all(place):
    barrier = pltpu.get_barrier_semaphore()

    def one(step, carry):
        pl.semaphore_signal(
            barrier, inc=1, device_id=place.numbered(lax.rem(place.me + step, place.count)),
            device_id_type=MESH,
        )
        return carry

    lax.fori_loop(1, place.count, one, 0)
    pl.semaphore_wait(barrier, place.count - 1)


def greet(place):
    barrier = pltpu.get_barrier_semaphore()
    for axis in AXES:
        for step in range(1, place.size[axis]):
            pl.semaphore_signal(
                barrier, inc=1, device_id=place.device(axis, place.after(axis, step)),
                device_id_type=MESH,
            )


def met(place):
    pl.semaphore_wait(pltpu.get_barrier_semaphore(), sum(n - 1 for n in place.size.values()))


def sems_needed(sizes, units, pairs):
    return units * (1 + sum(size - 1 for size in sizes.values())) + pairs


class Exchange:
    def __init__(self, place, sems, mine, whole, chunks):
        self.place, self.sems, self.mine, self.whole = place, sems, mine, whole
        self.spans = spans_of(mine.shape[1], chunks)
        self.sent = []

    def start(self, which):
        place = self.place
        at = place.at["y"]
        rows = pl.ds(*self.spans[which])
        if which == 0:
            self.kept = self.sems.local(lambda: (self.mine.at[at], self.whole.at[at]))

        def ends(step):
            other = place.after("y", step)
            return self.mine.at[other, rows], self.whole.at[at, rows], place.device("y", other)

        for step in range(1, place.size["y"]):
            self.sent.append((step, rows, self.sems.copy(functools.partial(ends, step))))

    def finish(self):
        self.kept.wait()
        for step, rows, slot in self.sent:
            index = self.place.before("y", step)
            self.sems.arrived(slot, self.whole.at[index, rows], self.place.device("y", index))


EXCHANGE_CHUNKS = 4


START_ORDERS = (WIDE,)
FRONT_ORDERS = (EVEN,)
MLP_ORDERS = (EVEN,)
MLP_SUM_ORDERS = (EVEN,)
BACK_ORDERS = (EVEN,)
FINISH_ORDERS = (WIDE,)


def start_kernel(
    silu_ref, ada_ref, x_ref, qkv_ref, mod_ref, rows_ref, hot_ref, x_full, qkv_full, silu_s, share_s, terms_s, send, recv, share_send, share_recv,
):
    place = Place()
    sems = Sems(send, recv)
    count, me = place.count, place.me
    width = silu_ref.shape[1] - hot_ref.shape[1]
    rows_each = ada_ref.shape[0]
    greet_all(place)

    silu = Gather(place, sems, silu_ref, silu_s, "czxy")
    gathers = Gathers(place, sems, [(qkv_ref, qkv_full, span) for span in spans_of(qkv_ref.shape[0], 4)], START_ORDERS)
    silu.own()
    silu.start(0)
    gathers.advance(0)
    silu.wait(0)
    silu.start(1)
    silu.wait(1)
    silu.start(2)
    silu.wait(2)
    silu.start(3)
    x_move = Exchange(place, sems, x_ref, x_full, EXCHANGE_CHUNKS)
    gathers.advance(1)
    x_move.start(0)
    silu.wait(3)

    rows = silu_s[...].reshape(count, silu_ref.shape[1])
    hot = (
        rows[:, width:] == lax.broadcasted_iota(jnp.int32, (count, hot_ref.shape[1]), 1).astype(f32)
    ).astype(bf16)
    hot_ref[...] = hot.astype(f32)
    first = lax.axis_index("dp") * rows_each
    pick = (
        lax.broadcasted_iota(jnp.int32, (width, rows_each), 0)
        == first + lax.broadcasted_iota(jnp.int32, (width, rows_each), 1)
    ).astype(bf16)
    local = mm(rows[:, :width].astype(bf16), pick).astype(bf16)
    grouped = mm(hot[:, :count], local)
    rows_ref[...] = grouped
    share = mm(grouped.astype(bf16), ada_ref[...])
    share_s[...] = share.reshape(share_s.shape)

    def push(step):
        to = lax.rem(me + step, count)
        return pltpu.make_async_remote_copy(
            src_ref=share_s.at[to], dst_ref=terms_s.at[me],
            send_sem=share_send.at[step], recv_sem=share_recv.at[step],
            device_id=place.numbered(to), device_id_type=MESH,
        )

    def came(step):
        source = lax.rem(me + count - step, count)
        return pltpu.make_async_remote_copy(
            src_ref=terms_s.at[source], dst_ref=terms_s.at[source],
            send_sem=share_send.at[step], recv_sem=share_recv.at[step],
            device_id=place.numbered(source), device_id_type=MESH,
        )

    def do_push(step, carry):
        push(step).start()
        return carry

    lax.fori_loop(1, count, do_push, 0)
    terms_s[me] = share_s[me]

    def do_wait(step, carry):
        came(step).wait_recv()
        return carry

    def do_sent(step, carry):
        push(step).wait_send()
        return carry

    gathers.advance(2)
    x_move.start(1)
    lax.fori_loop(1, count, do_wait, 0)
    heads = place.size["y"]
    for y in range(heads):
        mod_ref[y] = lax.fori_loop(
            0, count // heads, lambda i, total: total + terms_s[i * heads + y],
            jnp.zeros(terms_s.shape[1:], f32),
        )
    for tick in range(3, gathers.ticks + 1):
        gathers.advance(tick)
        if tick < EXCHANGE_CHUNKS + 1:
            x_move.start(tick - 1)
    x_move.finish()
    sems.drain()
    lax.fori_loop(1, count, do_sent, 0)


def start_call(silu, order_mine, ada, x, qkv):
    dp, head = lax.axis_size("dp"), lax.axis_size("head")
    count = dp * head
    lead = (4, 2, dp // 8, head)
    lanes = max(128, count)
    width = silu.shape[1]
    row = jnp.concatenate(
        [silu.astype(bf16).astype(f32), jnp.broadcast_to(order_mine.astype(f32), (1, lanes))], axis=1
    )
    sizes = {"z": 4, "x": 2, "c": dp // 8, "y": head}
    needed = sems_needed(sizes, 5, 1 + EXCHANGE_CHUNKS * head)
    anywhere = pl.BlockSpec(memory_space=pl.ANY)
    vmem = pl.BlockSpec(memory_space=pltpu.VMEM)
    slot_shape = x.shape
    return pl.pallas_call(
        start_kernel,
        in_specs=[anywhere, vmem] + [anywhere] * 2,
        out_specs=[vmem] * 3 + [anywhere] * 2,
        out_shape=[
            jax.ShapeDtypeStruct((head, 1, ada.shape[1]), f32),
            jax.ShapeDtypeStruct((count, ada.shape[0]), f32),
            jax.ShapeDtypeStruct((count, lanes), f32),
            jax.ShapeDtypeStruct(slot_shape, bf16),
            jax.ShapeDtypeStruct(lead + qkv.shape, bf16),
        ],
        scratch_shapes=[
            pltpu.VMEM(lead + (1, width + lanes), f32),
            pltpu.VMEM((count, 1, ada.shape[1]), f32),
            pltpu.VMEM((count, 1, ada.shape[1]), f32),
            pltpu.SemaphoreType.DMA((needed,)),
            pltpu.SemaphoreType.DMA((needed,)),
            pltpu.SemaphoreType.DMA((count,)),
            pltpu.SemaphoreType.DMA((count,)),
        ],
        compiler_params=pltpu.CompilerParams(
            collective_id=0, has_side_effects=True, vmem_limit_bytes=VMEM_MOST
        ),
        name="gather_start",
    )(row, ada, x, qkv)


def front_kernel(
    tiles, ts, kind_ref, x_ref, mod_ref, w_ref, b_ref, out_p, up_p, down_p, cot_p,
    qkv_ref, norm_ref, o_ref, lse_ref, out_f, up_f, down_f, cot_f,
    qkv_s, norm_s, copied, send, recv,
):
    step = pl.program_id(0)
    groups, _, rows_each, width = w_ref.shape
    _, slots, size = qkv_s.shape
    heads = width // size
    parts = 3 * H // heads
    tm = slots // tiles
    first_head = parts * tiles
    last = first_head + H - 1

    place = Place()
    sems = Sems(send, recv)
    wanted = []
    for piece, full, count in ((up_p, up_f, 4), (down_p, down_f, 4), (out_p, out_f, 2)):
        wanted += [(piece, full, span) for span in spans_of(piece.shape[0], count)]
    gathers = Gathers(place, sems, wanted, FRONT_ORDERS)
    keep = pltpu.make_async_copy(qkv_s, qkv_ref, copied.at[0])
    keep_norm = pltpu.make_async_copy(norm_s, norm_ref, copied.at[1])
    cot_move = Exchange(place, sems, cot_p, cot_f, EXCHANGE_CHUNKS)
    for tick in range(gathers.ticks):
        at = min(FRONT_STEPS[tick], last)
        if tick == 0:
            @pl.when(step == 0)
            def _():
                greet(place)

            @pl.when(step == at)
            def _():
                met(place)
                gathers.advance(0)
        elif at < last:
            @pl.when(step == at)
            def _(tick=tick):
                gathers.advance(tick)
                if tick in FRONT_EXCHANGE:
                    cot_move.start(FRONT_EXCHANGE.index(tick))

    @pl.when(step < first_head)
    def _():
        rows = pl.ds(pl.multiple_of(lax.rem(step, tiles) * tm, tm), tm)
        part = lax.div(step, tiles)

        @pl.when(part == 0)
        def _():
            center, inv = center_spread(x_ref[...].astype(f32))
            norm_s[rows, :] = (
                center * inv * (1.0 + mod_ref[1:2, :]) + mod_ref[0:1, :]
            ).astype(bf16)

        weight = w_ref[...].reshape(groups * rows_each, width)
        out = (mm(norm_s[rows, :], weight) + b_ref[0]).astype(bf16)
        for j in range(heads):
            qkv_s[part * heads + j, rows, :] = out[:, j * size : (j + 1) * size]

    @pl.when(step == first_head)
    def _():
        keep.start()
        keep_norm.start()

    @pl.when(step >= first_head)
    def _():
        head = step - first_head
        kept = slots - slots // 16
        factor = log2_e * size ** (-0.5)
        full = kind_ref[0] == 0
        keys = qkv_s[H + head]
        values_t = qkv_s[2 * H + head].T
        for start in range(0, slots, ts):
            here = slice(start, start + ts)
            scores = masked(mm_nt(keys, qkv_s[head, here, :]), full, kept)
            peak = jnp.max(scores, axis=0, keepdims=True) * factor
            exponent = jnp.exp2(scores * factor - peak)
            total = jnp.sum(exponent, axis=0, keepdims=True)
            mix = mm(values_t, exponent.astype(bf16)) * (1.0 / total)
            o_ref[0, here, :] = mix.T.astype(bf16)
            lse_ref[0, :, here] = peak + jnp.log2(total)

    @pl.when(step == last)
    def _():
        for tick in range(gathers.ticks):
            if FRONT_STEPS[tick] >= last:
                gathers.advance(tick)
        gathers.advance(gathers.ticks)
        cot_move.finish()
        keep.wait()
        keep_norm.wait()
        sems.drain()


FRONT_EXCHANGE = (1, 2, 4, 5)
FRONT_STEPS = (1, 3, 6, 10, 14, 18, 21, 99)


def front_call(kind, x, mod, weight, bias, out, up, down, cot):
    slots, width = x.shape
    tiles = 2
    groups, parts, rows_each, part_width = weight.shape
    size = width // H
    sizes = sizes_of()
    lead = tuple(sizes[a] for a in AXES)
    needed = sems_needed(sizes, 10, 1 + EXCHANGE_CHUNKS * sizes["y"])
    first_head = parts * tiles
    anywhere = pl.BlockSpec(memory_space=pl.ANY)

    def part(s):
        return jnp.minimum(lax.div(s, tiles), parts - 1)

    def head(s):
        return jnp.maximum(s - first_head, 0)

    return pl.pallas_call(
        functools.partial(front_kernel, tiles, min(256, slots)),
        grid=(first_head + H,),
        in_specs=[
            pl.BlockSpec(memory_space=pltpu.SMEM),
            pl.BlockSpec((slots // tiles, width), lambda s: (jnp.where(s < tiles, s, tiles - 1), 0)),
            whole_spec(mod.shape),
            pl.BlockSpec(
                (groups, 1, rows_each, part_width),
                lambda s: (0, lax.rem(part(s), 2) * 2 + lax.div(part(s), 2), 0, 0),
            ),
            pl.BlockSpec((1, 1, part_width), lambda s: (part(s), 0, 0)),
        ]
        + [anywhere] * 4,
        out_specs=[
            anywhere,
            anywhere,
            pl.BlockSpec((1, slots, size), lambda s: (head(s), 0, 0)),
            pl.BlockSpec((1, 1, slots), lambda s: (head(s), 0, 0)),
        ]
        + [anywhere] * 4,
        out_shape=[
            jax.ShapeDtypeStruct((3 * H, slots, size), bf16),
            jax.ShapeDtypeStruct((slots, width), bf16),
            jax.ShapeDtypeStruct((H, slots, size), bf16),
            jax.ShapeDtypeStruct((H, 1, slots), f32),
        ]
        + [jax.ShapeDtypeStruct(lead + piece.shape, bf16) for piece in (out, up, down)]
        + [jax.ShapeDtypeStruct(cot.shape, bf16)],
        scratch_shapes=[
            pltpu.VMEM((3 * H, slots, size), bf16),
            pltpu.VMEM((slots, width), bf16),
            pltpu.SemaphoreType.DMA((2,)),
            pltpu.SemaphoreType.DMA((needed,)),
            pltpu.SemaphoreType.DMA((needed,)),
        ],
        compiler_params=pltpu.CompilerParams(
            collective_id=3, has_side_effects=True, vmem_limit_bytes=VMEM_MOST
        ),
        name="front",
    )(kind, x, mod, weight, bias, out, up, down, cot)


class Scatter:
    def __init__(self, place, sems, grad, held, recvs, axes, rows=None):
        self.place, self.sems, self.grad, self.held, self.recvs, self.axes = (
            place, sems, grad, held, recvs, axes
        )
        self.rows = rows
        self.slots = {}

    @staticmethod
    def scratch(sizes, axes, rows, width):
        held = pltpu.VMEM(tuple(sizes[a] for a in "zxy") + (rows, width), bf16)
        recvs = []
        for at, axis in enumerate(axes):
            left = tuple(sizes[a] for a in "zxy" if a not in axes[: at + 1])
            recvs.append(pltpu.VMEM((sizes[axis] - 1,) + left + (rows, width), bf16))
        return [held] + recvs

    def wanted(self, of):
        spots = tuple(of if name == "c" else slice(None) for name in AXES)
        if self.rows is not None:
            spots = spots + (pl.ds(*self.rows), slice(None))
        return self.grad.at[spots]

    def share(self, stage, index):
        done = self.axes[1:stage]
        spots = []
        for name in "zxy":
            if name in done:
                spots.append(self.place.at[name])
            elif name == self.axes[stage]:
                spots.append(index)
            else:
                spots.append(slice(None))
        return self.held.at[tuple(spots)]

    def start(self, stage):
        axis = self.axes[stage]
        place = self.place
        if stage == 0:
            self.kept = self.sems.local(lambda: (self.wanted(place.at["c"]), self.held))

        def ends(step):
            index = place.after(axis, step)
            src = self.wanted(index) if stage == 0 else self.share(stage, index)
            return src, self.recvs[stage].at[step - 1], place.device(axis, index)

        for step in range(1, place.size[axis]):
            self.slots[stage, step] = self.sems.copy(functools.partial(ends, step))

    def arrive(self, stage):
        axis = self.axes[stage]
        place = self.place
        if stage == 0:
            self.kept.wait()
        for step in range(1, place.size[axis]):
            self.sems.arrived(
                self.slots[stage, step], self.recvs[stage].at[step - 1],
                place.device(axis, place.before(axis, step)),
            )

    def finish(self, stage):
        self.arrive(stage)
        place = self.place
        left = [a for a in "zxy" if a not in self.axes[: stage + 1]]
        recv = self.recvs[stage]

        def one(at, carry):
            spots = {}
            for a in reversed(left):
                spots[a] = lax.rem(at, place.size[a])
                at = lax.div(at, place.size[a])
            where = tuple(spots.get(a, place.at[a]) for a in "zxy")
            inner = tuple(spots[a] for a in left)
            total = self.held[where].astype(f32)
            for step in range(recv.shape[0]):
                total = total + recv[(step,) + inner].astype(f32)
            self.held[where] = total.astype(bf16)
            return carry

        lax.fori_loop(0, math.prod(place.size[a] for a in left), one, 0)

    def result(self, stage):
        self.arrive(stage)
        place = self.place
        recv = self.recvs[stage]
        total = self.held[tuple(place.at[a] for a in "zxy")].astype(f32)
        for step in range(recv.shape[0]):
            total = total + recv[step].astype(f32)
        return total


def sum_axes(orders, at):
    return orders[at // 2 % len(orders)][at % 2][::-1]


def sum_scratch(sizes, grads, orders):
    scratch, number = [], 0
    for rows, width, whole, count in grads:
        near = sizes["c"]
        scratch.append(
            pltpu.VMEM((rows, width) if whole else (near, rows // near, width), f32)
        )
        for span in spans_of(rows, count):
            scratch += Scatter.scratch(sizes, sum_axes(orders, number), span[1], width)
            number += 1
    return scratch


class Sums:
    def __init__(self, place, sems, grads, finals, scratch, orders):
        self.place, self.sems, self.finals = place, sems, finals
        scratch = list(scratch)
        self.totals, self.pairs = [], []
        at = -1
        for which, (grad, count) in enumerate(grads):
            self.totals.append(scratch.pop(0))
            for span in spans_of(grad.shape[4], count):
                at += 1
                axes = sum_axes(orders, at)
                held, recvs, scratch = scratch[0], scratch[1:5], scratch[5:]
                unit = Scatter(place, sems, grad, held, recvs, axes, span)
                if at % 2 == 0:
                    self.pairs.append([])
                self.pairs[-1].append((unit, span, which))
        self.ticks = len(self.pairs) + 3

    def advance(self, tick):
        for pair in fresh(self.pairs, tick):
            for unit, *_ in pair:
                unit.start(0)
        for stage in (0, 2, 1, 3):
            if 0 <= tick - 1 - stage < len(self.pairs):
                for unit, span, which in self.pairs[tick - 1 - stage]:
                    if stage == 3:
                        self.settle(which, unit, span)
                    else:
                        unit.finish(stage)
                        unit.start(stage + 1)

    def settle(self, at, unit, span):
        value = unit.result(3)
        first, size = span
        total = self.totals[at]
        if len(total.shape) == 2:
            total[first : first + size, :] = value
            return
        each = total.shape[1]
        for to in range(total.shape[0]):
            low, high = max(first, to * each), min(first + size, (to + 1) * each)
            if low < high:
                total[to, low - to * each : high - to * each, :] = value[
                    low - first : high - first, :
                ]

    def deliver(self):
        place = self.place
        mine = place.at["c"]
        self.kept, self.flights = [], []
        def ends(total, final, step):
            to = place.after("c", step)
            return total.at[to], final.at[mine], place.device("c", to)

        for total, final in zip(self.totals, self.finals):
            if len(total.shape) == 2:
                self.kept.append(self.sems.local(lambda t=total, f=final: (t, f)))
                continue
            self.kept.append(self.sems.local(lambda t=total, f=final: (t.at[mine], f.at[mine])))
            for step in range(1, place.size["c"]):
                slot = self.sems.copy(functools.partial(ends, total, final, step))
                self.flights.append((final, step, slot))

    def delivered(self):
        for made in self.kept:
            made.wait()
        for final, step, slot in self.flights:
            source = self.place.before("c", step)
            self.sems.arrived(slot, final.at[source], self.place.device("c", source))


def sizes_of():
    dp, head = lax.axis_size("dp"), lax.axis_size("head")
    return {"z": 4, "x": 2, "c": dp // 8, "y": head}


def final_shape(grad, near):
    return jax.ShapeDtypeStruct((near, grad.shape[4] // near, grad.shape[5]), f32)


def finish_kernel(
    row_ref, ada_ref, rows_ref, hot_ref, gin_ref, qkv_ref,
    bias_ref, dada_ref, gsilu_ref, gin_full, dqkv_ref,
    send, recv, share_send, share_recv, row_s, share_s, *scratch,
):
    place = Place()
    count, me = place.count, place.me
    sems = Sems(send, recv)
    sums = Sums(
        place, sems, [(qkv_ref, FINISH_SPANS)], (dqkv_ref,), scratch, FINISH_ORDERS
    )
    greet_all(place)
    rows = Gather(place, sems, row_ref, row_s, "zxyc")
    rows.own()
    rows.start(0)
    gin_move = Exchange(place, sems, gin_ref, gin_full, EXCHANGE_CHUNKS)
    sums.advance(0)
    gin_move.start(0)
    for tick in range(1, 5):
        sums.advance(tick)
        if tick < EXCHANGE_CHUNKS:
            gin_move.start(tick)
        rows.wait(tick - 1)
        if tick < 4:
            rows.start(tick)

    whole = row_s[...].reshape(count, row_ref.shape[1])
    bias_ref[...] = jnp.sum(whole, axis=0, keepdims=True)
    cols = ada_ref.shape[1]
    low = jnp.zeros((count, cols), f32)
    for y in range(place.size["y"]):
        low = jnp.where(place.at["y"] == y, whole[:, y * cols : (y + 1) * cols], low)
    low = low.astype(bf16)
    dada_ref[...] = lax.dot_general(
        rows_ref[...].astype(bf16), low, (((0,), (0,)), ((), ())), preferred_element_type=f32
    )
    grad = mm_nt(low, ada_ref[...])
    hot = hot_ref[...][:, :count]
    placed = lax.dot_general(
        hot, grad, (((0,), (0,)), ((), ())), precision=lax.Precision.HIGHEST,
        preferred_element_type=f32,
    )
    pad = share_s.shape[2] - placed.shape[1]
    placed = jnp.concatenate([placed, jnp.zeros((count, pad), f32)], axis=1)
    share_s[...] = placed.reshape(share_s.shape)

    def push(step):
        to = lax.rem(me + step, count)
        return pltpu.make_async_remote_copy(
            src_ref=share_s.at[to], dst_ref=gsilu_ref.at[me],
            send_sem=share_send.at[step], recv_sem=share_recv.at[step],
            device_id=place.numbered(to), device_id_type=MESH,
        )

    def came(step):
        source = lax.rem(me + count - step, count)
        return pltpu.make_async_remote_copy(
            src_ref=gsilu_ref.at[source], dst_ref=gsilu_ref.at[source],
            send_sem=share_send.at[step], recv_sem=share_recv.at[step],
            device_id=place.numbered(source), device_id_type=MESH,
        )

    def do_push(step, carry):
        push(step).start()
        return carry

    def do_wait(step, carry):
        came(step).wait_recv()
        push(step).wait_send()
        return carry

    lax.fori_loop(1, count, do_push, 0)
    gsilu_ref[me] = share_s[me]
    for tick in range(5, sums.ticks + 1):
        sums.advance(tick)
    sums.deliver()
    lax.fori_loop(1, count, do_wait, 0)
    sums.delivered()
    gin_move.finish()
    sems.drain()


FINISH_SPANS = 4


def finish_call(row, ada, silu_rows, hot, gin, qkv):
    sizes = sizes_of()
    near = sizes["c"]
    count = 8 * near * sizes["y"]
    anywhere = pl.BlockSpec(memory_space=pl.ANY)
    vmem = pl.BlockSpec(memory_space=pltpu.VMEM)
    needed = sems_needed(sizes, 2 + FINISH_SPANS, 1 + EXCHANGE_CHUNKS * sizes["y"] + 4 * near)
    return pl.pallas_call(
        finish_kernel,
        in_specs=[anywhere, vmem, vmem, vmem] + [anywhere] * 2,
        out_specs=[vmem] * 3 + [anywhere] * 2,
        out_shape=[
            jax.ShapeDtypeStruct(row.shape, f32),
            jax.ShapeDtypeStruct(ada.shape, f32),
            jax.ShapeDtypeStruct((count, 1, 128), f32),
            jax.ShapeDtypeStruct(gin.shape, bf16),
            final_shape(qkv, near),
        ],
        scratch_shapes=[
            pltpu.SemaphoreType.DMA((needed,)),
            pltpu.SemaphoreType.DMA((needed,)),
            pltpu.SemaphoreType.DMA((count,)),
            pltpu.SemaphoreType.DMA((count,)),
            pltpu.VMEM((4, 2, near, sizes["y"], 1, row.shape[1]), f32),
            pltpu.VMEM((count, 1, 128), f32),
        ]
        + sum_scratch(
            sizes,
            [qkv.shape[4:] + (False, FINISH_SPANS)],
            FINISH_ORDERS,
        ),
        compiler_params=pltpu.CompilerParams(
            collective_id=1, has_side_effects=True, vmem_limit_bytes=VMEM_MOST
        ),
        name="sum_finish",
    )(row, ada, silu_rows, hot, gin, qkv)


BACK_SPANS = (4, 4)
BACK_STEPS = (1, 2, 4, 6, 9, 11, 13)


def attn_back_kernel(
    ts, kind_ref, q_ref, k_ref, v_ref, g_ref, lse_ref, up_p, down_p,
    out_ref, dup_ref, ddown_ref, dk_s, dv_s, send, recv, *scratch,
):
    step = pl.program_id(0)
    last = pl.num_programs(0) - 1
    place = Place()
    sems = Sems(send, recv)
    sums = Sums(
        place, sems, list(zip((up_p, down_p), BACK_SPANS)), (dup_ref, ddown_ref), scratch,
        BACK_ORDERS,
    )

    @pl.when(step == 0)
    def _():
        greet(place)

    for tick in range(sums.ticks):
        if BACK_STEPS[tick] < H - 1:
            @pl.when(step == BACK_STEPS[tick])
            def _(tick=tick):
                if tick == 0:
                    met(place)
                sums.advance(tick)

    slots, size = q_ref.shape[1:]
    kept = slots - slots // 16
    scale = size ** (-0.5)
    factor = log2_e * scale
    full = kind_ref[0] == 0
    keys = k_ref[0]
    keys_t = keys.T
    values = v_ref[0]
    for start in range(0, slots, ts):
        here = slice(start, start + ts)
        queries = q_ref[0, here, :]
        grad = g_ref[0, here, :]
        scores = masked(mm_nt(keys, queries), full, kept)
        probs = jnp.exp2(scores * factor - lse_ref[0, :, here])
        weighted = probs * mm_nt(values, grad)
        inner = jnp.sum(weighted, axis=0, keepdims=True)
        grad_scores = (weighted - probs * inner).astype(bf16)
        add_v = mm(probs.astype(bf16), grad)
        add_k = mm(grad_scores, queries)
        if start == 0:
            dv_s[...] = add_v
            dk_s[...] = add_k
        else:
            dv_s[...] += add_v
            dk_s[...] += add_k
        out_ref[0, 0, here, :] = (mm(keys_t, grad_scores) * scale).T.astype(bf16)
    out_ref[1, 0] = (dk_s[...] * scale).astype(bf16)
    out_ref[2, 0] = dv_s[...].astype(bf16)

    @pl.when(step == last)
    def _():
        for tick in range(sums.ticks):
            if BACK_STEPS[tick] >= H - 1:
                sums.advance(tick)
        sums.advance(sums.ticks)
        sums.deliver()
        sums.delivered()
        sems.drain()


def attn_back_call(kind, qkv, grad, lse, up, down):
    _, slots, size = qkv.shape
    ts = min(256, slots)
    block = (1, slots, size)
    sizes = sizes_of()
    anywhere = pl.BlockSpec(memory_space=pl.ANY)
    needed = sems_needed(sizes, sum(BACK_SPANS), 2 * sizes["y"] + 4 * sizes["c"])
    return pl.pallas_call(
        functools.partial(attn_back_kernel, ts),
        grid=(H,),
        in_specs=[
            pl.BlockSpec(memory_space=pltpu.SMEM),
            pl.BlockSpec(block, lambda h: (h, 0, 0)),
            pl.BlockSpec(block, lambda h: (h + H, 0, 0)),
            pl.BlockSpec(block, lambda h: (h + 2 * H, 0, 0)),
            pl.BlockSpec(block, lambda h: (h, 0, 0)),
            pl.BlockSpec((1, 1, slots), lambda h: (h, 0, 0)),
        ]
        + [anywhere] * 2,
        out_specs=[pl.BlockSpec((3, 1, slots, size), lambda h: (0, h, 0, 0))] + [anywhere] * 2,
        out_shape=[
            jax.ShapeDtypeStruct((3, H, slots, size), bf16),
            final_shape(up, sizes["c"]),
            jax.ShapeDtypeStruct(down.shape[4:], f32),
        ],
        scratch_shapes=[
            pltpu.VMEM((slots, size), f32),
            pltpu.VMEM((slots, size), f32),
            pltpu.SemaphoreType.DMA((needed,)),
            pltpu.SemaphoreType.DMA((needed,)),
        ]
        + sum_scratch(
            sizes,
            [
                grad.shape[4:] + (at == 1, count)
                for at, (grad, count) in enumerate(zip((up, down), BACK_SPANS))
            ],
            BACK_ORDERS,
        ),
        compiler_params=pltpu.CompilerParams(
            collective_id=2, has_side_effects=True, vmem_limit_bytes=VMEM_MOST
        ),
        name="attention_backward",
    )(kind, qkv, qkv, qkv, grad, lse, up, down)


MLP_SPANS = 4
MLP_GATHER = (1, 2, 3, 4, 6, 8, 10)
MLP_SUM = (12, 13, 14, 16, 18, 20, 22)


def mlp_kernel(
    tiles, second_ref, gm_ref, up0_f, down0_f, up1_p, down1_p, b_ref,
    mlp_ref, gsec_ref, bias_ref, up1_f, down1_f, dup0_ref, ddown0_ref, dup1_ref, ddown1_ref,
    sup_ref, sdown_ref,
    sec_t, act_t, gh_s, up_s, down_s, raw_up, raw_down, loaded, stored,
    send, recv, *scratch,
):
    step = pl.program_id(0)
    subs = tiles + 2
    last = 4 * subs - 1
    tile_at = lax.div(step, subs)
    sub = lax.rem(step, subs)
    slots, width = second_ref.shape
    hidden = up_s.shape[1]
    tm = slots // tiles

    place = Place()
    sems = Sems(send, recv)
    near, head_half = place.size["c"], place.size["y"] // 2

    def loads(tile):
        half = tile % 2
        up, down = ((up0_f, down0_f), (up1_f, down1_f))[tile // 2]
        return (
            pltpu.make_async_copy(
                up.at[:, :, :, pl.ds(half * head_half, head_half)], raw_up, loaded.at[0]
            ),
            pltpu.make_async_copy(down.at[pl.ds(2 * half, 2)], raw_down, loaded.at[1]),
        )

    def stores(tile):
        half = tile % 2
        up, down = ((dup0_ref, ddown0_ref), (dup1_ref, ddown1_ref))[tile // 2]
        return (
            pltpu.make_async_copy(
                raw_up, up.at[:, :, :, pl.ds(half * head_half, head_half)], stored.at[0]
            ),
            pltpu.make_async_copy(raw_down, down.at[pl.ds(2 * half, 2)], stored.at[1]),
        )

    wanted = []
    for piece, full in ((up1_p, up1_f), (down1_p, down1_f)):
        wanted += [(piece, full, span) for span in spans_of(piece.shape[0], MLP_SPANS)]
    gathers = Gathers(place, sems, wanted, MLP_ORDERS)
    sums = Sums(
        place, sems, [(dup0_ref, MLP_SPANS), (ddown0_ref, MLP_SPANS)], (sup_ref, sdown_ref), scratch,
        MLP_SUM_ORDERS,
    )

    @pl.when(step == 0)
    def _():
        greet(place)

    for tick in range(gathers.ticks):
        @pl.when(step == MLP_GATHER[tick])
        def _(tick=tick):
            if tick == 0:
                met(place)
            gathers.advance(tick)

    @pl.when(step == 2 * subs)
    def _():
        gathers.advance(gathers.ticks)

    @pl.when(step == 0)
    def _():
        sec_t[...] = second_ref[...].T
        mlp_ref[...] = jnp.zeros_like(mlp_ref)
        gsec_ref[...] = jnp.zeros_like(gsec_ref)
        for made in loads(0):
            made.start()

    for tile in range(4):
        @pl.when(step == tile * subs)
        def _(tile=tile):
            if tile > 0:
                stores(tile - 1)[1].wait()
                loads(tile)[1].start()
            if tile == 2:
                loads(tile)[0].start()
            for made in loads(tile):
                made.wait()

    @pl.when(sub == 0)
    def _():
        share = raw_up.shape[5]
        for y in range(raw_up.shape[3]):
            for c in range(near):
                off = (y * near + c) * share
                up_s[:, off : off + share] = raw_up[:, :, c, y].reshape(width, share)
        chunk, share = raw_down.shape[4:]
        for at in range(4 * near):
            for y in range(raw_down.shape[3]):
                down_s[at * chunk : (at + 1) * chunk, y * share : (y + 1) * share] = raw_down[
                    at // (2 * near), (at // near) % 2, at % near, y
                ]
        bias_ref[...] = jnp.zeros_like(bias_ref)

    for tick in range(sums.ticks):
        if MLP_SUM[tick] < last:
            @pl.when(step == MLP_SUM[tick])
            def _(tick=tick):
                sums.advance(tick)

    @pl.when(sub < tiles)
    def _():
        rows = pl.ds(pl.multiple_of(sub * tm, tm), tm)
        pre = mm(second_ref[rows, :], up_s[...]) + b_ref[0]
        square = pre * pre
        tanh = jnp.tanh(gelu_in * (pre + gelu_cube * pre * square))
        act = (0.5 * pre * (1.0 + tanh)).astype(bf16)
        slope = 0.5 * (1.0 + tanh) + 0.5 * pre * (1.0 - tanh * tanh) * (
            gelu_in * (1.0 + 3.0 * gelu_cube * square)
        )
        grad = mm_nt(gm_ref[rows, :], down_s[...]) * slope
        bias_ref[0] += jnp.sum(grad, axis=0, keepdims=True)
        grad_low = grad.astype(bf16)
        gh_s[rows, :] = grad_low
        act_t[:, rows] = act.T
        mlp_ref[rows, :] += mm(act, down_s[...])
        gsec_ref[rows, :] += mm_nt(grad_low, up_s[...])

    @pl.when(sub == tiles)
    def _():
        share = raw_up.shape[5]
        half = width // 2
        for j in range(2):
            grad = mm(sec_t[j * half : (j + 1) * half, :], gh_s[...]).astype(bf16)
            for y in range(raw_up.shape[3]):
                for c in range(near):
                    off = (y * near + c) * share
                    raw_up[2 * j : 2 * j + 2, :, c, y] = grad[:, off : off + share].reshape(
                        2, 2, half // 4, share
                    )

    @pl.when(sub == tiles + 1)
    def _():
        chunk, share = raw_down.shape[4:]
        half = hidden // 2
        for j in range(2):
            grad = mm(act_t[j * half : (j + 1) * half, :], gm_ref[...]).astype(bf16)
            for at in range(2 * near):
                for y in range(raw_down.shape[3]):
                    raw_down[j, at // near, at % near, y] = grad[
                        at * chunk : (at + 1) * chunk, y * share : (y + 1) * share
                    ]

    for tile in range(4):
        @pl.when(step == tile * subs + tiles)
        def _(tile=tile):
            stores(tile)[0].start()

        @pl.when(step == tile * subs + tiles + 1)
        def _(tile=tile):
            stores(tile)[0].wait()
            if tile in (0, 2):
                loads(tile + 1)[0].start()
            stores(tile)[1].start()

    @pl.when(step == last)
    def _():
        stores(3)[1].wait()
        for tick in range(sums.ticks):
            if MLP_SUM[tick] >= last:
                sums.advance(tick)
        sums.advance(sums.ticks)
        sums.deliver()
        sums.delivered()
        sems.drain()


def mlp_call(second, gm, up0, down0, up1, down1, bias):
    slots, width = second.shape
    tiles = 4
    subs = tiles + 2
    sizes = sizes_of()
    near, head = sizes["c"], sizes["y"]
    lead = tuple(sizes[a] for a in AXES)
    rows_up, share_up = up1.shape
    rows_down, share_down = down1.shape
    hidden = share_up * near * head // 2
    anywhere = pl.BlockSpec(memory_space=pl.ANY)
    needed = sems_needed(sizes, 4 * MLP_SPANS, 4 * near)
    bias_spec = pl.BlockSpec((1, 1, hidden), lambda s: (lax.div(s, subs), 0, 0))
    full_up = jax.ShapeDtypeStruct(lead + up1.shape, bf16)
    full_down = jax.ShapeDtypeStruct(lead + down1.shape, bf16)
    return pl.pallas_call(
        functools.partial(mlp_kernel, tiles),
        grid=(4 * subs,),
        in_specs=[once_spec((slots, width)), once_spec((slots, width))]
        + [anywhere] * 4
        + [bias_spec],
        out_specs=[once_spec((slots, width)), once_spec((slots, width)), bias_spec] + [anywhere] * 8,
        out_shape=[
            jax.ShapeDtypeStruct((slots, width), f32),
            jax.ShapeDtypeStruct((slots, width), f32),
            jax.ShapeDtypeStruct(bias.shape, f32),
            full_up, full_down, full_up, full_down, full_up, full_down,
            final_shape(full_up, near),
            jax.ShapeDtypeStruct(down1.shape, f32),
        ],
        scratch_shapes=[
            pltpu.VMEM((width, slots), bf16),
            pltpu.VMEM((hidden, slots), bf16),
            pltpu.VMEM((slots, hidden), bf16),
            pltpu.VMEM((width, hidden), bf16),
            pltpu.VMEM((hidden, width), bf16),
            pltpu.VMEM((4, 2, near, head // 2) + up1.shape, bf16),
            pltpu.VMEM((2, 2, near, head) + down1.shape, bf16),
            pltpu.SemaphoreType.DMA((2,)),
            pltpu.SemaphoreType.DMA((2,)),
            pltpu.SemaphoreType.DMA((needed,)),
            pltpu.SemaphoreType.DMA((needed,)),
        ]
        + sum_scratch(
            sizes, (up1.shape + (False, MLP_SPANS), down1.shape + (True, MLP_SPANS)), MLP_SUM_ORDERS
        ),
        compiler_params=pltpu.CompilerParams(
            collective_id=4, has_side_effects=True, vmem_limit_bytes=MLP_VMEM
        ),
        name="feed_forward_both_ways",
    )(second, gm, up0, down0, up1, down1, bias)


MLP_VMEM = 63 * 1024 * 1024


QKV_SPANS = 2
QKV_ORDERS = (EVEN,)


def qkv_back_kernel(
    tm, g_ref, norm_ref, w_ref, x_ref, gmid_ref, mod_ref, act_p, out_p,
    gin_ref, dw_ref, bias_ref, sums_ref, act_f, dout_ref, norm_t, gp_s, gn_s, send, recv, *scratch,
):
    part = pl.program_id(0)
    slots, width = x_ref.shape
    tiles = slots // tm
    groups, _, rows_each, part_width = w_ref.shape
    heads = g_ref.shape[0]
    last = pl.num_programs(0) - 1

    place = Place()
    sems = Sems(send, recv)
    sums = Sums(place, sems, [(out_p, QKV_SPANS)], (dout_ref,), scratch, QKV_ORDERS)
    act_move = Exchange(place, sems, act_p, act_f, EXCHANGE_CHUNKS)
    for tick in range(4):
        @pl.when(part == tick)
        def _(tick=tick):
            if tick == 0:
                greet(place)
                met(place)
            sums.advance(tick)
            act_move.start(tick)

    @pl.when(part == 0)
    def _():
        norm_t[...] = norm_ref[...].T
        gn_s[...] = jnp.zeros_like(gn_s)

    def tile(i, total):
        rows = pl.ds(pl.multiple_of(i * tm, tm), tm)
        grad = jnp.concatenate([g_ref[j, rows, :] for j in range(heads)], axis=1)
        gp_s[rows, :] = grad
        gn_s[rows, :] += mm_nt(grad, w_ref[...].reshape(width, part_width))
        return total + jnp.sum(grad.astype(f32), axis=0, keepdims=True)

    bias_ref[0] = lax.fori_loop(0, tiles, tile, jnp.zeros((1, part_width), f32))
    per = groups // 2
    for j in range(2):
        dw_ref[per * j : per * (j + 1), 0] = (
            mm(norm_t[per * j * rows_each : per * (j + 1) * rows_each, :], gp_s[...])
            .astype(bf16)
            .reshape(per, rows_each, part_width)
        )

    @pl.when(part == pl.num_programs(0) - 1)
    def _():
        def finish(i, sums):
            rows = pl.ds(pl.multiple_of(i * tm, tm), tm)
            center, inv = center_spread(x_ref[rows, :].astype(f32))
            unit = center * inv
            grad = gn_s[rows, :]
            gin_ref[rows, :] = (
                gmid_ref[rows, :] + norm_back(grad * (1.0 + mod_ref[1:2, :]), unit, inv)
            ).astype(gin_ref.dtype)
            return (
                sums[0] + jnp.sum(grad, axis=0, keepdims=True),
                sums[1] + jnp.sum(grad * unit, axis=0, keepdims=True),
            )

        zero = jnp.zeros((1, width), f32)
        shift, scale = lax.fori_loop(0, tiles, finish, (zero, zero))
        sums_ref[...] = jnp.zeros_like(sums_ref)
        sums_ref[0:1, :] = shift
        sums_ref[1:2, :] = scale

    @pl.when(part == last)
    def _():
        sums.advance(4)
        sums.deliver()
        sums.delivered()
        act_move.finish()
        sems.drain()


def qkv_back_call(grad, norm, weight, x, gmid, mod, act, out):
    slots, width = x.shape
    tm = min(256, slots)
    size = width // H
    groups, parts, rows_each, part_width = weight.shape
    heads = part_width // size
    sizes = sizes_of()
    anywhere = pl.BlockSpec(memory_space=pl.ANY)
    needed = sems_needed(sizes, QKV_SPANS, 1 + EXCHANGE_CHUNKS * sizes["y"] + 4 * sizes["c"])
    w_spec = pl.BlockSpec((groups, 1, rows_each, part_width), lambda p: (0, place(p), 0, 0))
    return pl.pallas_call(
        functools.partial(qkv_back_kernel, tm),
        grid=(parts,),
        in_specs=[
            pl.BlockSpec((heads, slots, size), lambda p: (p, 0, 0)),
            once_spec((slots, width)),
            w_spec,
            once_spec((slots, width)),
            once_spec((slots, width)),
            whole_spec(mod.shape),
            anywhere,
            anywhere,
        ],
        out_specs=[
            once_spec((slots, width)),
            w_spec,
            pl.BlockSpec((1, 1, part_width), lambda p: (p, 0, 0)),
            whole_spec((8, width)),
            anywhere,
            anywhere,
        ],
        out_shape=[
            jax.ShapeDtypeStruct((slots, width), bf16),
            jax.ShapeDtypeStruct(weight.shape, bf16),
            jax.ShapeDtypeStruct((parts, 1, part_width), f32),
            jax.ShapeDtypeStruct((8, width), f32),
            jax.ShapeDtypeStruct(act.shape, bf16),
            final_shape(out, sizes["c"]),
        ],
        scratch_shapes=[
            pltpu.VMEM((width, slots), bf16),
            pltpu.VMEM((slots, part_width), bf16),
            pltpu.VMEM((slots, width), f32),
            pltpu.SemaphoreType.DMA((needed,)),
            pltpu.SemaphoreType.DMA((needed,)),
        ]
        + sum_scratch(sizes, [out.shape[4:] + (False, QKV_SPANS)], QKV_ORDERS),
        compiler_params=pltpu.CompilerParams(
            collective_id=5, has_side_effects=True, vmem_limit_bytes=VMEM_MOST
        ),
        name="qkv_backward",
    )(grad, norm, weight, x, gmid, mod, act, out)


class Wire:
    def __init__(self, width):
        self.dp = lax.axis_size("dp")
        self.head = lax.axis_size("head")
        self.near = self.dp // (width // 144)
        self.width = width
        self.groups = [
            list(range(first, first + self.near)) for first in range(0, self.dp, self.near)
        ]

    def pieces(self, weights):
        rows = weights[0].shape[0]
        stack = jnp.concatenate(
            [weight.astype(bf16).reshape(rows, self.near, -1) for weight in weights], axis=2
        )
        stack = lax.all_to_all(
            stack, "dp", split_axis=1, concat_axis=0, axis_index_groups=self.groups, tiled=True
        )
        stack = stack.reshape(rows * self.near, -1)
        ends = [0]
        for weight in weights:
            ends.append(ends[-1] + weight.shape[1] // self.near)
        return [stack[:, low:high] for low, high in zip(ends, ends[1:])]

    def columns(self, stack):
        devices, rows, cols = stack.shape
        stack = stack.reshape(self.dp // self.near, self.near, self.head, rows, cols)
        if (self.near, self.head) != (2, 2):
            quarter = self.near * self.head * cols // 4
            stack = stack.transpose(0, 3, 2, 1, 4).reshape(-1, rows, 2, 2, quarter)
            stack = stack.transpose(0, 3, 2, 1, 4)
            return stack.reshape(-1, 4, rows, quarter)
        return stack.reshape(-1, 4, rows, cols)

    def uncolumns(self, stack):
        groups, _, rows, quarter = stack.shape
        cols = 4 * quarter // (self.near * self.head)
        if (self.near, self.head) != (2, 2):
            stack = stack.reshape(groups, 2, 2, rows, quarter).transpose(0, 3, 2, 1, 4)
            stack = stack.reshape(groups, rows, self.head, self.near, cols)
            stack = stack.transpose(0, 3, 2, 1, 4)
        return stack.reshape(self.dp * self.head, rows, cols)


def body(
    inputs, cond, order, grid_kind, weight_ada, bias_ada, weight_qkv, bias_query, bias_value,
    weight_out, bias_out, weight_up, bias_up, weight_down, bias_down, cotangent,
):
    images, slot_local, width = inputs.shape
    head_count = lax.axis_size("head")
    dp_count = lax.axis_size("dp")
    head_at = lax.axis_index("head")
    dp_at = lax.axis_index("dp")
    assert images == head_count
    wire = Wire(width)

    def from_image(array):
        return lax.all_to_all(
            array[None], "head", split_axis=1, concat_axis=0, tiled=True
        ).astype(f32)

    rows_ada, cols_ada = weight_ada.shape
    ada_low = weight_ada.astype(bf16)
    silu_own, silu_pull = jax.vjp(lambda v: v * jax.nn.sigmoid(v), cond)
    chunk = weight_down.shape[0] // 2
    up_phases = weight_up.reshape(rows_ada, -1, 2, chunk)
    up0_p, up1_p, qkv_p, out_p = wire.pieces(
        [up_phases[:, :, at].reshape(rows_ada, -1) for at in range(2)] + [weight_qkv, weight_out]
    )
    order_mine = lax.dynamic_slice_in_dim(order, head_at, 1, 0)
    kind = lax.dynamic_slice_in_dim(grid_kind, head_at, 1, 0)
    mod, silu_grouped, hot, x, qkv_full = start_call(
        silu_own, order_mine, ada_low, inputs.astype(bf16), qkv_p
    )
    x = x.reshape(-1, width)
    device_stack = lambda full: full.reshape((-1,) + full.shape[4:])
    qkv_full = wire.columns(device_stack(qkv_full))
    mod_flat = mod.reshape(6, width) + bias_ada.reshape(6, width)
    mod = jnp.concatenate([mod_flat, jnp.zeros((2, width), f32)], axis=0)

    bias_qkv = jnp.concatenate([bias_query, jnp.zeros_like(bias_query), bias_value])
    down0, down1 = (weight_down[at * chunk : (at + 1) * chunk].astype(bf16) for at in range(2))
    bias_phases = bias_up.reshape(-1, 2, chunk).swapaxes(0, 1).reshape(4, 1, -1)
    qkv, norm, mix, lse, out_full, up_full, down_full, cot = front_call(
        kind, x, mod, qkv_full, bias_qkv.reshape(4, 1, -1),
        out_p, up0_p, down0, cotangent.astype(bf16),
    )
    cot = cot.reshape(-1, width)
    out_full = wire.columns(device_stack(out_full))
    attended, branch, second, gm = out_call(mix, x, cot, mod, out_full, bias_out)
    mlp, gsec, d_bias_up, _, _, _, _, d_up1, d_down1, d_up0, d_down0 = mlp_call(
        second, gm, up_full, down_full, up1_p, down1, bias_phases
    )
    d_bias_up = d_bias_up.reshape(2, -1, chunk).swapaxes(0, 1)
    act, gmid, gatt, d_out, sums = mid_back_call(
        x, branch, mlp, gsec, cot, attended, mod, out_full, bias_down
    )
    lead = (4, 2, dp_count // 8, head_count)
    stack = lambda grad: grad.reshape(lead + grad.shape[1:])
    by_image = lambda array: array.reshape(head_count, slot_local, width)
    grad, d_up1, d_down1 = attn_back_call(kind, qkv, gatt, lse, d_up1, d_down1)
    gin, d_qkv, d_bias_qkv, sums_in, act, d_out = qkv_back_call(
        grad.reshape(qkv.shape), norm, qkv_full, x, gmid, mod, by_image(act),
        stack(wire.uncolumns(d_out)),
    )

    bias_qkv_sum = d_bias_qkv.reshape(3, width)
    row = jnp.concatenate(
        [sums_in[0], sums_in[1], sums[0], sums[1], sums[2], sums[3],
         bias_qkv_sum[0], bias_qkv_sum[2], sums[4], sums[5], d_bias_up.reshape(-1)]
    ).reshape(1, -1)
    biases, d_ada, g_silu, gin, d_qkv = finish_call(
        row, ada_low, silu_grouped, hot, by_image(gin), stack(wire.uncolumns(d_qkv))
    )
    biases = biases[0]
    g_silu = g_silu.reshape(dp_count, head_count, 128)[:, :, :rows_ada].sum(axis=1)
    d_cond = silu_pull(g_silu.reshape(1, width))[0]
    side = lambda grad: grad.transpose(1, 0, 2).reshape(grad.shape[1], -1)
    d_up = jnp.stack(
        [side(part).reshape(rows_ada, -1, chunk) for part in (d_up0, d_up1)], axis=2
    ).reshape(rows_ada, -1)
    d_down = jnp.concatenate([d_down0, d_down1], axis=0)
    mods = 6 * width
    return (
        act.astype(f32),
        gin.astype(f32),
        d_cond,
        d_ada,
        side(d_qkv),
        side(d_out),
        d_up,
        d_down,
        biases[:mods],
        biases[mods : mods + width],
        biases[mods + width : mods + 2 * width],
        biases[mods + 2 * width : mods + 3 * width],
        biases[mods + 4 * width :],
        biases[mods + 3 * width : mods + 4 * width],
    )


def solution(mesh):
    in_specs = (
        P("dp", "head", None), P(("dp", "head"), None), P("dp"), P("dp"), P("dp", "head"), P(),
        P("dp", "head"), P(), P(), P("dp", "head"), P(), P("dp", "head"), P(), P("dp", "head"),
        P(), P("dp", "head", None),
    )
    out_specs = (
        P("dp", "head", None), P("dp", "head", None), P(("dp", "head"), None), P("dp", "head"),
        P("dp", "head"), P("dp", "head"), P("dp", "head"), P("dp", "head"),
        P(), P(), P(), P(), P(), P(),
    )
    return jax.shard_map(body, mesh=mesh, in_specs=in_specs, out_specs=out_specs, check_vma=False)
```
